128 devices in a mesh: blk: 16 (over z_hi, x, core), head: 8 (over z_lo, y).
Axes of the slice: x: 4, y: 4, z: 4 (z_hi: 2, z_lo: 2; z = z_hi * 2 + z_lo), core: 2. Of those that a mesh axis runs over, the one named last changes fastest.
Arguments:
- tokens: bfloat16 [2, 8, 1024, 2048], P(None, 'head', 'blk'), may hold values from -6 to 6
- segment_ids: int32 [2, 8, 1024], replicated, may hold values from 0 to 1023, as said below
- ln1_gain: float32 [2048], replicated, may hold values from 0.5 to 1.5
- ln1_bias: float32 [2048], replicated, may hold values from -1 to 1
- w_query: bfloat16 [2048, 2048], P('blk', 'head'), may hold values from -0.125 to 0.125
- b_query: float32 [2048], replicated, may hold values from -1.5 to 1.5
- w_kv: bfloat16 [2048, 256], P('blk', 'head'), may hold values from -0.125 to 0.125
- b_value: float32 [128], replicated, may hold values from -2.5 to 2.5
- w_out: bfloat16 [2048, 2048], P('head', 'blk'), may hold values from -0.375 to 0.375
- b_out: float32 [2048], replicated, may hold values from -1.5 to 1.5
- ln2_gain: float32 [2048], replicated, may hold values from 0.5 to 1.5
- ln2_bias: float32 [2048], replicated, may hold values from -1 to 1
- w_fc: bfloat16 [2048, 8192], P('blk', 'head'), may hold values from -0.125 to 0.125
- b_fc: float32 [8192], replicated, may hold values from -1.5 to 1.5
- w_fc2: bfloat16 [8192, 2048], P('head', 'blk'), may hold values from -0.0625 to 0.0625
- b_fc2: float32 [2048], replicated, may hold values from -1.5 to 1.5
- cotangent: bfloat16 [2, 8, 1024, 2048], P(None, 'head', 'blk'), may hold values from -6 to 6
Outputs:
- output: bfloat16 [2, 8, 1024, 2048], P(None, 'head', 'blk')
- input_grad: float32 [2, 8, 1024, 2048], P(None, 'head', 'blk')
- ln1_gain_grad: float32 [2048], replicated
- ln1_bias_grad: float32 [2048], replicated
- w_query_grad: float32 [2048, 2048], P('blk', 'head')
- b_query_grad: float32 [2048], replicated
- w_kv_grad: float32 [2048, 256], P('blk', 'head')
- b_value_grad: float32 [128], replicated
- w_out_grad: float32 [2048, 2048], P('head', 'blk')
- b_out_grad: float32 [2048], replicated
- ln2_gain_grad: float32 [2048], replicated
- ln2_bias_grad: float32 [2048], replicated
- w_fc_grad: float32 [2048, 8192], P('blk', 'head')
- b_fc_grad: float32 [8192], replicated
- w_fc2_grad: float32 [8192, 2048], P('head', 'blk')
- b_fc2_grad: float32 [2048], replicated
The draws below stay inside these ranges and needn't reach their ends.
Inputs may be any that keep to these rules, and one draw needn't show every extreme that they name: `segment_ids`: each position's id is the first position of its document within the sequence, so ids never fall along a sequence and position 0 has id 0; in every micro-batch some sequence is one single document, and some other sequence ends with a document of one position.
All inputs are finite; a program needn't handle non-finite values.
Results may differ from the reference program's by a relative error of at most 0.023.
Values may be sent and summed in bfloat16 or wider, within the bound.
No kernel may reach another device: no remote copies, remote signals or barrier semaphores. Data moves between devices by JAX's collectives and lax.ppermute only.
A program may use at most 192 MiB of HBM per device.

```python
import math
import jax
import jax.numpy as jnp
from jax import lax

D = 2048
HEADS = 16
HEAD_DIM = 128
FF = 8192
LENGTH = 1024
MICRO = 2
SEQS = 8


def draw_segment_ids(key, part):
    key = jax.random.fold_in(key, 7)
    rate_key, mark_key, whole_key = jax.random.split(key, 3)
    span_table = jnp.array([8, 32, 128, 512], jnp.int32)
    rate_picks = jax.random.randint(rate_key, (MICRO, SEQS, 1), 0, 4)
    chosen_span = jnp.sum(jnp.where(rate_picks == jnp.arange(4), span_table, 0), axis=-1, keepdims=True)
    start_marks = jax.random.randint(mark_key, (MICRO, SEQS, LENGTH), 0, chosen_span) == 0
    whole_seq = jax.random.randint(whole_key, (MICRO, 1, 1), 0, SEQS)
    seq_index = jnp.arange(SEQS)[None, :, None]
    single_doc = seq_index == whole_seq
    short_end = seq_index == (whole_seq + 1) % SEQS
    position = jnp.arange(LENGTH)[None, None, :]
    first_pos = position == 0
    last_pos = position == LENGTH - 1
    starts = start_marks & jnp.logical_not(single_doc) | first_pos | last_pos & short_end
    marked = jnp.where(starts, position, 0).astype(jnp.int32)
    return lax.cummax(marked, axis=2)


def block_levels(own_key, shape, cuts, smallest, top_value):
    def one(dim, blocks):
        draws = jax.random.uniform(jax.random.fold_in(jax.random.fold_in(own_key, 6), dim), (blocks,), jnp.float32, smallest / len(cuts), top_value / len(cuts))
        return jnp.repeat(jnp.exp(draws), shape[dim] // blocks).reshape((-1,) + (1,) * (len(shape) - dim - 1))

    loudness = one(*cuts[0])
    for cut in cuts[1:]:
        loudness = loudness * one(*cut)
    return loudness


def normal_values(own_key, shape, scale, limit, cuts=(), kind=jnp.bfloat16):
    values = jax.random.normal(own_key, shape, jnp.float32) * scale
    if len(cuts) > 0:
        values = block_levels(own_key, shape, cuts, -0.22, 0.18) * values
    return jnp.clip(values, min=-limit, max=limit).astype(kind)


def setup_inputs(seed: int = 0) -> dict:
    keys = jax.random.split(jax.random.key(seed), 18)
    tokens = normal_values(keys[0], (MICRO, SEQS, LENGTH, D), 1.0, 6.0, ((1, 8), (2, 16)))
    segment_ids = draw_segment_ids(jax.random.fold_in(keys[17], 71), 0)
    ln1_gain = jnp.clip(1.0 + 0.1 * jax.random.normal(keys[2], (D,), jnp.float32), 0.5, 1.5)
    ln1_bias = normal_values(keys[3], (D,), 0.2, 1.0, (), jnp.float32)
    w_query = normal_values(keys[4], (D, D), D ** -0.5, 0.125, ((0, 16), (1, 8)))
    b_query = normal_values(keys[5], (D,), 0.3, 1.5, (), jnp.float32)
    w_kv = normal_values(keys[6], (D, 2 * HEAD_DIM), D ** -0.5, 0.125, ((0, 16), (1, 8)))
    b_value = normal_values(keys[7], (HEAD_DIM,), 0.5, 2.5, (), jnp.float32)
    w_out = normal_values(keys[8], (D, D), (D // 8) ** -0.5, 0.375, ((0, 8), (1, 16)))
    b_out = normal_values(keys[9], (D,), 0.3, 1.5, (), jnp.float32)
    ln2_gain = jnp.clip(1.0 + 0.1 * jax.random.normal(keys[10], (D,), jnp.float32), 0.5, 1.5)
    ln2_bias = normal_values(keys[11], (D,), 0.2, 1.0, (), jnp.float32)
    w_fc = normal_values(keys[12], (D, FF), D ** -0.5, 0.125, ((0, 16), (1, 8)))
    b_fc = normal_values(keys[13], (FF,), 0.3, 1.5, (), jnp.float32)
    w_fc2 = normal_values(keys[14], (FF, D), FF ** -0.5, 0.0625, ((0, 8), (1, 16)))
    b_fc2 = normal_values(keys[15], (D,), 0.3, 1.5, (), jnp.float32)
    cotangent = normal_values(keys[16], (MICRO, SEQS, LENGTH, D), 1.0, 6.0, ((1, 8), (2, 16)))
    return dict(tokens=tokens, segment_ids=segment_ids, ln1_gain=ln1_gain, ln1_bias=ln1_bias, w_query=w_query, b_query=b_query, w_kv=w_kv, b_value=b_value, w_out=w_out, b_out=b_out, ln2_gain=ln2_gain, ln2_bias=ln2_bias, w_fc=w_fc, b_fc=b_fc, w_fc2=w_fc2, b_fc2=b_fc2, cotangent=cotangent)


@jax.custom_vjp
def low(v):
    return lax.optimization_barrier(v.astype(jnp.bfloat16)).astype(jnp.float32)

@jax.custom_vjp
def low_back(v):
    return v

def low_keep(v):
    return (low(v), None)

def low_pass(kept, grad):
    return (grad,)

def back_keep(v):
    return (v, None)

def back_low(kept, grad):
    return (low(grad),)
low.defvjp(low_keep, low_pass)
low_back.defvjp(back_keep, back_low)
EPS = 1e-05
NEG = -1e+30
HIGH = lax.Precision.HIGHEST

def matmul(left, right):
    return jnp.matmul(left, right, precision=HIGH)

def layer_norm(values, gain, shift):
    center = lax.optimization_barrier(jnp.mean(values, axis=-1, keepdims=True))
    centered = values - center
    inv_std = lax.rsqrt(lax.optimization_barrier(jnp.mean(centered * centered, axis=-1, keepdims=True)) + EPS)
    return centered * inv_std * gain + shift

def layer(params, inputs, segments):
    ln1_gain, ln1_bias, w_query, b_query, w_kv, b_value, w_out, b_out, ln2_gain, ln2_bias, w_fc, b_fc, w_fc2, b_fc2 = params
    seq_count = inputs.shape[0]
    normed_in = low(layer_norm(inputs, ln1_gain, ln1_bias))
    queries = low(low_back(matmul(normed_in, w_query) + b_query)).reshape(seq_count, LENGTH, HEADS, HEAD_DIM)
    kv_bias = jnp.concatenate([jnp.zeros((HEAD_DIM,), jnp.float32), b_value])
    key_value = low(low_back(matmul(normed_in, w_kv) + kv_bias))
    key_part = key_value[..., :HEAD_DIM]
    value_part = key_value[..., HEAD_DIM:]
    raw_scores = jnp.einsum('slhe,ske->shlk', queries, key_part, precision=HIGH)
    scores = low_back(raw_scores * HEAD_DIM ** (-0.5))
    positions = jnp.arange(LENGTH)
    allowed = (positions[None, None, :] <= positions[None, :, None]) & (segments[:, None, :] == segments[:, :, None])
    allowed = allowed[:, None]
    masked = jnp.where(allowed, scores, NEG)
    row_top = lax.optimization_barrier(jnp.max(masked, axis=-1, keepdims=True))
    expo_terms = jnp.where(allowed, jnp.exp(masked - row_top), 0.0)
    attention_probs = low(expo_terms / lax.optimization_barrier(jnp.sum(expo_terms, axis=-1, keepdims=True)))
    attended = jnp.einsum('shlk,ske->slhe', attention_probs, value_part, precision=HIGH)
    attention_reduced = low(low_back(attended)).reshape(seq_count, LENGTH, D)
    residual = inputs + low_back(matmul(attention_reduced, w_out)) + b_out
    hidden_in = low(layer_norm(residual, ln2_gain, ln2_bias))
    pre_act = low_back(matmul(hidden_in, w_fc) + b_fc)
    activation = low(jax.nn.gelu(pre_act, approximate=True))
    return residual + low_back(matmul(activation, w_fc2)) + b_fc2

def reference(tokens, segment_ids, ln1_gain, ln1_bias, w_query, b_query, w_kv, b_value, w_out, b_out, ln2_gain, ln2_bias, w_fc, b_fc, w_fc2, b_fc2, cotangent):
    params = (ln1_gain, ln1_bias, w_query.astype(jnp.float32), b_query, w_kv.astype(jnp.float32), b_value, w_out.astype(jnp.float32), b_out, ln2_gain, ln2_bias, w_fc.astype(jnp.float32), b_fc, w_fc2.astype(jnp.float32), b_fc2)
    total_seqs = MICRO * SEQS
    bundle = math.gcd(total_seqs, max(1, 4096 // LENGTH))
    inputs = tokens.astype(jnp.float32).reshape(total_seqs // bundle, bundle, LENGTH, D)
    segments = segment_ids.reshape(total_seqs // bundle, bundle, LENGTH)
    stepper = jax.checkpoint(layer)

    def forward(params, inputs):

        def scan_step(carry, item):
            return (carry, stepper(params, item[0], item[1]))
        _, outputs = lax.scan(scan_step, jnp.zeros((), jnp.float32), (inputs, segments))
        return outputs
    outputs, pull = jax.vjp(forward, params, inputs)
    grads, input_grad = pull(cotangent.astype(jnp.float32).reshape(outputs.shape))
    shape = (MICRO, SEQS, LENGTH, D)
    return (outputs.reshape(shape).astype(jnp.bfloat16), input_grad.reshape(shape), grads[0], grads[1], grads[2], grads[3], grads[4], grads[5], grads[6], grads[7], grads[8], grads[9], grads[10], grads[11], grads[12], grads[13])
```

```python
import functools

import jax
import jax.numpy as jnp
from jax import lax
from jax.experimental import pallas as pl
from jax.experimental.pallas import tpu as pltpu
from jax.sharding import Mesh
from jax.sharding import PartitionSpec as P

EPS = 1e-05
NEG = -1e30
F32 = jnp.float32
LOW = jnp.bfloat16
BLK = ("zh", "x", "c")
HEAD = ("zl", "y")
TEAM = ("c", "y")
PLANE = ("zh", "x", "zl")
LINE = ("zh", "x")
ALL = ("zh", "x", "c", "zl", "y")
Q_BLOCK = 256


def normalize(values, gain, shift):
    center = jnp.mean(values, axis=-1, keepdims=True)
    centered = values - center
    inv_std = lax.rsqrt(jnp.mean(centered * centered, axis=-1, keepdims=True) + EPS)
    normed = centered * inv_std
    return (normed * gain + shift, normed, inv_std)


def norm_back(grad, normed, inv_std, gain):
    scaled = grad * gain
    first_mean = jnp.mean(scaled, axis=-1, keepdims=True)
    second_mean = jnp.mean(scaled * normed, axis=-1, keepdims=True)
    return inv_std * (scaled - first_mean - normed * second_mean)


def gelu_tanh(values):
    return jax.nn.gelu(values, approximate=True)


def dot(left, right, left_dim, right_dim):
    return lax.dot_general(
        left, right, (((left_dim,), (right_dim,)), ((), ())), preferred_element_type=F32
    )


def block_probs(seg_ref, q_ref, keys, row, head, head_dim, scale):
    end = row + Q_BLOCK
    queries = q_ref[row:end, head * head_dim : (head + 1) * head_dim]
    scores = dot(queries, keys, 1, 1) * scale
    key_pos = lax.broadcasted_iota(jnp.int32, scores.shape, 1)
    query_pos = lax.broadcasted_iota(jnp.int32, scores.shape, 0) + row
    allowed = (key_pos <= query_pos) & (key_pos >= seg_ref[row:end, :])
    masked = jnp.where(allowed, scores, NEG)
    terms = jnp.exp(masked - jnp.max(masked, axis=1, keepdims=True))
    return queries, terms * (1.0 / jnp.sum(terms, axis=1, keepdims=True))


def attend_kernel(heads, head_dim, scale, seg_ref, qkv_ref, out_ref):
    wide = heads * head_dim
    for row in range(0, qkv_ref.shape[0], Q_BLOCK):
        end = row + Q_BLOCK
        keys = qkv_ref[:end, wide : wide + head_dim]
        values = qkv_ref[:end, wide + head_dim :]
        for head in range(heads):
            _, probs = block_probs(seg_ref, qkv_ref, keys, row, head, head_dim, scale)
            out_ref[row:end, head * head_dim : (head + 1) * head_dim] = dot(
                probs.astype(LOW), values, 1, 0
            ).astype(LOW)


def attend_back_kernel(heads, head_dim, scale, seg_ref, qkv_ref, grad_ref, out_ref, dkv_ref):
    wide = heads * head_dim
    dkv_ref[...] = jnp.zeros_like(dkv_ref)
    for row in range(0, qkv_ref.shape[0], Q_BLOCK):
        end = row + Q_BLOCK
        keys = qkv_ref[:end, wide : wide + head_dim]
        values = qkv_ref[:end, wide + head_dim :]
        for head in range(heads):
            cols = slice(head * head_dim, (head + 1) * head_dim)
            queries, probs = block_probs(seg_ref, qkv_ref, keys, row, head, head_dim, scale)
            grad = grad_ref[row:end, cols]
            d_probs = dot(grad, values, 1, 1)
            delta = jnp.sum(probs * d_probs, axis=1, keepdims=True)
            d_scores = (probs * (d_probs - delta)).astype(LOW)
            out_ref[row:end, cols] = (dot(d_scores, keys, 1, 0) * scale).astype(LOW)
            dkv_ref[:end, :head_dim] += dot(d_scores, queries, 0, 0)
            dkv_ref[:end, head_dim:] += dot(probs.astype(LOW), grad, 0, 0)
    out_ref[:, wide : wide + head_dim] = (dkv_ref[:, :head_dim] * scale).astype(LOW)
    out_ref[:, wide + head_dim :] = dkv_ref[:, head_dim:].astype(LOW)


def attend(segments, qkv, heads, head_dim):
    length = qkv.shape[0]
    return pl.pallas_call(
        functools.partial(attend_kernel, heads, head_dim, head_dim**-0.5),
        out_shape=jax.ShapeDtypeStruct((length, heads * head_dim), LOW),
        compiler_params=pltpu.CompilerParams(vmem_limit_bytes=40 * 2**20),
        cost_estimate=pl.CostEstimate(
            flops=2 * heads * length * length * head_dim,
            bytes_accessed=4 * qkv.size,
            transcendentals=heads * length * length // 2,
        ),
        name="attend",
    )(segments, qkv)


def attend_back(segments, qkv, grad, heads, head_dim):
    length = qkv.shape[0]
    return pl.pallas_call(
        functools.partial(attend_back_kernel, heads, head_dim, head_dim**-0.5),
        out_shape=jax.ShapeDtypeStruct(qkv.shape, LOW),
        scratch_shapes=[pltpu.VMEM((length, 2 * head_dim), F32)],
        compiler_params=pltpu.CompilerParams(vmem_limit_bytes=40 * 2**20),
        cost_estimate=pl.CostEstimate(
            flops=5 * heads * length * length * head_dim,
            bytes_accessed=8 * qkv.size,
            transcendentals=heads * length * length // 2,
        ),
        name="attend_back",
    )(segments, qkv, grad)


def team_gather(values):
    return lax.all_gather(values, TEAM, axis=0, tiled=True)


def team_scatter(partial):
    cores, ys = lax.axis_size("c"), lax.axis_size("y")
    rows = partial.shape[0] // (cores * ys)
    low = partial.astype(LOW).reshape(cores, ys, rows, partial.shape[1])
    core = lax.axis_index("c")
    kept = lax.dynamic_index_in_dim(low, core, 0, keepdims=False)
    sent = lax.dynamic_index_in_dim(low, 1 - core, 0, keepdims=False)
    got = lax.ppermute(sent, "c", [(0, 1), (1, 0)])
    both = (kept.astype(F32) + got.astype(F32)).astype(LOW)
    pieces = lax.all_to_all(both, "y", 0, 0, tiled=True)
    return jnp.sum(pieces.astype(F32), axis=0)


def swap(values):
    return lax.ppermute(values, ("c", "zl"), [(0, 0), (1, 2), (2, 1), (3, 3)])


def plane_gather(block):
    count = lax.axis_size(PLANE)
    spread = jnp.broadcast_to(block[None], (count,) + block.shape)
    whole = lax.all_to_all(spread, PLANE, 0, 0, tiled=True)
    return whole.reshape(count * block.shape[0], block.shape[1])


def plane_scatter(partial):
    count = lax.axis_size(PLANE)
    blocks = partial.astype(LOW).reshape(count, partial.shape[0] // count, partial.shape[1])
    return jnp.sum(lax.all_to_all(blocks, PLANE, 0, 0, tiled=True).astype(F32), axis=0)


def sum_vectors(flat):
    count = lax.axis_size(ALL)
    chunk = -(-flat.shape[0] // (count * 128)) * 128
    padded = jnp.pad(flat, (0, count * chunk - flat.shape[0])).reshape(count, chunk // 128, 128)
    mine = jnp.sum(lax.all_to_all(padded, ALL, 0, 0, tiled=True), axis=0)
    spread = jnp.broadcast_to(mine[None], padded.shape)
    return lax.all_to_all(spread, ALL, 0, 0, tiled=True).reshape(-1)[: flat.shape[0]]


def body(
    tokens,
    segment_ids,
    ln1_gain,
    ln1_bias,
    w_query,
    b_query,
    w_kv,
    b_value,
    w_out,
    b_out,
    ln2_gain,
    ln2_bias,
    w_fc,
    b_fc,
    w_fc2,
    b_fc2,
    cotangent,
):
    micro, _, rows, width = tokens.shape
    head_dim = b_value.shape[0]
    q_cols = w_query.shape[1]
    kv_cols = w_kv.shape[1]
    heads = q_cols // head_dim
    hidden = w_fc.shape[1]
    cores, ys = lax.axis_size("c"), lax.axis_size("y")
    lines = lax.axis_size(LINE)
    team_rank = lax.axis_index(TEAM)
    own = micro * rows

    def to_lines(values):
        cut = values.reshape(cores, ys, micro, rows, values.shape[-1])
        cut = jnp.transpose(cut, (2, 1, 0, 3, 4)).reshape(lines, cores * rows, values.shape[-1])
        moved = lax.all_to_all(cut, LINE, 0, 0, tiled=True)
        return moved.reshape(lines * cores * rows, values.shape[-1])

    def from_lines(values):
        cut = values.reshape(lines, cores * rows, values.shape[-1])
        moved = lax.all_to_all(cut, LINE, 0, 0, tiled=True)
        moved = moved.reshape(micro, ys, cores, rows, values.shape[-1])
        return jnp.transpose(moved, (2, 1, 0, 3, 4)).reshape(-1, values.shape[-1])

    early = swap(jnp.concatenate([w_query, w_kv], axis=1))
    kv_block = lax.all_gather(early[:, q_cols:], TEAM, axis=1, tiled=True)
    w_qkv = plane_gather(jnp.concatenate([early[:, :q_cols], kv_block], axis=1))
    late = swap(jnp.concatenate([w_out.T, w_fc, w_fc2.T], axis=1))
    w_out_t = plane_gather(late[:, :q_cols])
    w_up = plane_gather(late[:, q_cols : q_cols + hidden])
    w_down_t = plane_gather(late[:, q_cols + hidden :])

    x_own = tokens.reshape(own, width).astype(F32)
    first_norm, first_normed, first_inv = normalize(x_own, ln1_gain, ln1_bias)
    normed_in = team_gather(first_norm.astype(LOW))
    bias_qkv = jnp.concatenate(
        [
            lax.dynamic_slice_in_dim(b_query, team_rank * q_cols, q_cols),
            jnp.zeros((head_dim,), F32),
            b_value,
        ]
    )
    qkv = to_lines((dot(normed_in, w_qkv, 1, 0) + bias_qkv).astype(LOW))

    seq_rank = lax.axis_index("zl") * ys + lax.axis_index("x")
    segments = lax.dynamic_slice(
        segment_ids,
        (lax.axis_index("zh"), seq_rank, 0),
        (1, 1, segment_ids.shape[2]),
    ).reshape(-1, 1)
    attention = from_lines(attend(segments, qkv, heads, head_dim))

    projected = team_scatter(dot(attention, w_out_t, 1, 1))
    residual = x_own + projected + b_out
    second_norm, second_normed, second_inv = normalize(residual, ln2_gain, ln2_bias)
    hidden_in = team_gather(second_norm.astype(LOW))

    cot_own = cotangent.reshape(own, width)
    cot = team_gather(cot_own)
    pre_act = dot(hidden_in, w_up, 1, 0) + lax.dynamic_slice_in_dim(
        b_fc, team_rank * hidden, hidden
    )
    act, gelu_pull = jax.vjp(gelu_tanh, pre_act)
    act = act.astype(LOW)
    d_pre = gelu_pull(dot(cot, w_down_t, 1, 0))[0].astype(LOW)
    d_hidden = team_scatter(dot(d_pre, w_up, 1, 1))
    output = residual + team_scatter(dot(act, w_down_t, 1, 1)) + b_fc2
    output = output.astype(LOW).reshape(tokens.shape)
    g_down = plane_scatter(dot(cot, act, 0, 0))
    g_up = plane_scatter(dot(hidden_in, d_pre, 0, 0))

    cot_float = cot_own.astype(F32)
    d_res = cot_float + norm_back(d_hidden, second_normed, second_inv, ln2_gain)
    d_res_low = team_gather(d_res.astype(LOW))
    d_att = to_lines(dot(d_res_low, w_out_t, 1, 0).astype(LOW))
    g_out = plane_scatter(dot(d_res_low, attention, 0, 0))

    d_qkv = from_lines(attend_back(segments, qkv, d_att, heads, head_dim))
    d_in = team_scatter(dot(d_qkv, w_qkv, 1, 1))
    input_grad = d_res + norm_back(d_in, first_normed, first_inv, ln1_gain)
    g_qkv_part = dot(normed_in, d_qkv, 0, 0)
    g_qkv = plane_scatter(g_qkv_part)
    kv_pieces = lax.all_to_all(
        g_qkv[:, q_cols:].astype(LOW).reshape(-1, cores * ys, kv_cols),
        TEAM,
        1,
        1,
        tiled=True,
    )
    g_kv = jnp.sum(kv_pieces.astype(F32), axis=1)

    d_qkv_sums = jnp.sum(d_qkv.astype(F32), axis=0)
    w_qkv_float = w_qkv.astype(F32)
    ln1_bias_part = jnp.sum(w_qkv_float * d_qkv_sums, axis=1)
    ln1_gain_part = (jnp.sum(w_qkv_float * g_qkv_part, axis=1) - ln1_bias * ln1_bias_part) / ln1_gain
    placed_query = lax.dynamic_update_slice_in_dim(
        jnp.zeros(b_query.shape, F32), d_qkv_sums[:q_cols], team_rank * q_cols, 0
    )
    placed_fc = lax.dynamic_update_slice_in_dim(
        jnp.zeros(b_fc.shape, F32),
        jnp.sum(d_pre.astype(F32), axis=0),
        team_rank * hidden,
        0,
    )
    parts = [
        ln1_gain_part,
        ln1_bias_part,
        placed_query,
        d_qkv_sums[q_cols + head_dim :],
        jnp.sum(d_res, axis=0),
        jnp.sum(d_hidden * second_normed, axis=0),
        jnp.sum(d_hidden, axis=0),
        placed_fc,
        jnp.sum(cot_float, axis=0),
    ]
    summed = sum_vectors(jnp.concatenate(parts))
    vectors = []
    start = 0
    for part in parts:
        vectors.append(summed[start : start + part.shape[0]])
        start += part.shape[0]

    grads = swap(jnp.concatenate([g_qkv[:, :q_cols], g_kv, g_out, g_up, g_down], axis=1).astype(LOW))
    grads = grads.astype(F32)
    cuts = [0, q_cols, kv_cols, q_cols, hidden, hidden]
    edges = [sum(cuts[: i + 1]) for i in range(len(cuts))]
    d_wq, d_wkv, d_out, d_up, d_down = (
        grads[:, edges[i] : edges[i + 1]] for i in range(len(cuts) - 1)
    )
    return (
        output,
        input_grad.reshape(tokens.shape),
        vectors[0],
        vectors[1],
        d_wq,
        vectors[2],
        d_wkv,
        vectors[3],
        d_out.T,
        vectors[4],
        vectors[5],
        vectors[6],
        d_up,
        vectors[7],
        d_down.T,
        vectors[8],
    )


def solution(mesh):
    fine = Mesh(mesh.devices.reshape(2, 4, 2, 2, 4), ALL)
    activations = P(None, HEAD, BLK, None)
    rows_first, cols_first = P(BLK, HEAD), P(HEAD, BLK)
    return jax.shard_map(
        body,
        mesh=fine,
        in_specs=(
            activations,
            P(),
            P(),
            P(),
            rows_first,
            P(),
            rows_first,
            P(),
            cols_first,
            P(),
            P(),
            P(),
            rows_first,
            P(),
            cols_first,
            P(),
            activations,
        ),
        out_specs=(
            activations,
            activations,
            P(),
            P(),
            rows_first,
            P(),
            rows_first,
            P(),
            cols_first,
            P(),
            P(),
            P(),
            rows_first,
            P(),
            cols_first,
            P(),
        ),
        check_vma=False,
    )
```

```python
import functools

import jax
import jax.numpy as jnp
from jax import lax
from jax.experimental import pallas as pl
from jax.experimental.pallas import tpu as pltpu
from jax.sharding import Mesh
from jax.sharding import PartitionSpec as P

EPS = 1e-05
NEG = -1e30
F32 = jnp.float32
LOW = jnp.bfloat16
BLK = ("zh", "x", "c")
HEAD = ("zl", "y")
PLANE = ("zh", "x", "zl")
SHARERS = ("zl", "zh", "x", "c")
Z = ("zh", "zl")
ALL = ("zh", "x", "c", "zl", "y")
Q_BLOCK = 256
TEAM = 4
PAIRS = 2


def dot(left, right, left_dim, right_dim):
    return lax.dot_general(
        left, right, (((left_dim,), (right_dim,)), ((), ())), preferred_element_type=F32
    )


def center(values):
    centered = values - jnp.mean(values, axis=-1, keepdims=True)
    inv_std = lax.rsqrt(jnp.mean(centered * centered, axis=-1, keepdims=True) + EPS)
    return centered * inv_std, inv_std


def norm_back(grad, normed, inv_std, gain):
    scaled = grad * gain
    first_mean = jnp.mean(scaled, axis=-1, keepdims=True)
    second_mean = jnp.mean(scaled * normed, axis=-1, keepdims=True)
    return inv_std * (scaled - first_mean - normed * second_mean)


def join_pieces(pieces, whole):
    row = 0
    for piece in pieces:
        whole[row : row + piece.shape[0], :] = piece[...]
        row += piece.shape[0]


def write_parts(block, parts, cols):
    row = 0
    for part in parts:
        part[:, cols] = block[row : row + part.shape[0], :]
        row += part.shape[0]


def summed_parts(own, last_up, last_down, up, down):
    half = own.shape[0] // 2
    top = own[:half, :].astype(F32) + last_up[...].astype(F32) + down[half:, :].astype(F32)
    low = own[half:, :].astype(F32) + last_down[...].astype(F32) + up[:half, :].astype(F32)
    return jnp.concatenate([top, low], axis=0)


def slots(rows):
    for member in range(TEAM):
        for micro in range(2):
            yield (member * 2 + micro) * rows, (micro * TEAM + member) * PAIRS


def norm_kernel(x_ref, gain_ref, shift_ref, out_ref):
    normed, _ = center(x_ref[...].astype(F32))
    out_ref[...] = (normed * gain_ref[...] + shift_ref[...]).astype(LOW)


def weights_kernel(core_ref, mine_ref, other_ref, *outs):
    first = core_ref[0] == 0
    rows = mine_ref.shape[2]
    for pair in range(PAIRS):
        mine, other = mine_ref[0, pair], other_ref[0, pair]
        outs[pair][:rows, :] = jnp.where(first, mine, other)
        outs[pair][rows:, :] = jnp.where(first, other, mine)


def qkv_kernel(own, after, top, low, before, w0, w1, b0, b1, whole, out):
    join_pieces((own, after, top, low, before), whole)
    x = whole[...]
    rows, size = out.shape[1], b0.shape[1]
    first = (dot(x, w0[...], 1, 0) + b0[...]).astype(LOW)
    second = (dot(x, w1[...], 1, 0) + b1[...]).astype(LOW)
    q_cols = out.shape[2] - 2 * (size - out.shape[2] // 2)
    for row, slot in slots(rows):
        cut = slice(row, row + rows)
        shared = jnp.concatenate([first[cut, q_cols:], second[cut, q_cols:]], axis=1)
        out[slot, :, :q_cols] = first[cut, :q_cols]
        out[slot, :, q_cols:] = shared
        out[slot + 1, :, :q_cols] = second[cut, :q_cols]
        out[slot + 1, :, q_cols:] = shared


def block_probs(seg_ref, q_ref, keys, row, head, head_dim, scale):
    end = row + Q_BLOCK
    queries = q_ref[row:end, head * head_dim : (head + 1) * head_dim]
    scores = dot(queries, keys, 1, 1) * scale
    key_pos = lax.broadcasted_iota(jnp.int32, scores.shape, 1)
    query_pos = lax.broadcasted_iota(jnp.int32, scores.shape, 0) + row
    allowed = (key_pos <= query_pos) & (key_pos >= seg_ref[row:end, :])
    masked = jnp.where(allowed, scores, NEG)
    terms = jnp.exp(masked - jnp.max(masked, axis=1, keepdims=True))
    return queries, terms * (1.0 / jnp.sum(terms, axis=1, keepdims=True))


def attend_kernel(heads, head_dim, seg_ref, qkv_ref, out_ref):
    wide = heads * head_dim
    scale = head_dim**-0.5
    for row in range(0, qkv_ref.shape[0], Q_BLOCK):
        end = row + Q_BLOCK
        keys = qkv_ref[:end, wide : wide + head_dim]
        values = qkv_ref[:end, wide + head_dim :]
        for head in range(heads):
            _, probs = block_probs(seg_ref, qkv_ref, keys, row, head, head_dim, scale)
            out_ref[row:end, head * head_dim : (head + 1) * head_dim] = dot(
                probs.astype(LOW), values, 1, 0
            ).astype(LOW)


def attend_back_kernel(heads, head_dim, seg_ref, qkv_ref, grad_ref, out_ref, dkv_ref):
    wide = heads * head_dim
    scale = head_dim**-0.5
    dkv_ref[...] = jnp.zeros_like(dkv_ref)
    for row in range(0, qkv_ref.shape[0], Q_BLOCK):
        end = row + Q_BLOCK
        keys = qkv_ref[:end, wide : wide + head_dim]
        values = qkv_ref[:end, wide + head_dim :]
        for head in range(heads):
            cols = slice(head * head_dim, (head + 1) * head_dim)
            queries, probs = block_probs(seg_ref, qkv_ref, keys, row, head, head_dim, scale)
            grad = grad_ref[row:end, cols]
            d_probs = dot(grad, values, 1, 1)
            delta = jnp.sum(probs * d_probs, axis=1, keepdims=True)
            d_scores = (probs * (d_probs - delta)).astype(LOW)
            out_ref[row:end, cols] = (dot(d_scores, keys, 1, 0) * scale).astype(LOW)
            dkv_ref[:end, :head_dim] += dot(d_scores, queries, 0, 0)
            dkv_ref[:end, head_dim:] += dot(probs.astype(LOW), grad, 0, 0)
    out_ref[:, wide : wide + head_dim] = (dkv_ref[:, :head_dim] * scale).astype(LOW)
    out_ref[:, wide + head_dim :] = dkv_ref[:, head_dim:].astype(LOW)


def project_kernel(att, w0, w1, whole, *parts):
    rows, wide = att.shape[1], att.shape[2]
    for row, slot in slots(rows):
        for pair in range(PAIRS):
            whole[row : row + rows, pair * wide : (pair + 1) * wide] = att[slot + pair]
    for start in range(0, w0.shape[0], 512):
        cols = slice(start, start + 512)
        block = dot(whole[:, :wide], w0[cols, :], 1, 1) + dot(whole[:, wide:], w1[cols, :], 1, 1)
        write_parts(block.astype(LOW), parts, cols)


def residual_kernel(own, last_up, last_down, up, down, x, bias, gain, shift, residual, out):
    total = summed_parts(own, last_up, last_down, up, down)
    total = x[...].astype(F32) + total + bias[...]
    residual[...] = total
    normed, _ = center(total)
    out[...] = (normed * gain[...] + shift[...]).astype(LOW)


def hidden_kernel(own, after, top, low, before, cot, up, down, bias, whole, act, d_pre, sums):
    @pl.when(pl.program_id(0) == 0)
    def _():
        join_pieces((own, after, top, low, before), whole)

    u = dot(whole[...], up[...], 1, 0) + bias[...]
    slope = 2.0 ** 0.5 * jnp.pi ** -0.5
    square = u * u
    bent = jnp.tanh(slope * (u + 0.044715 * (square * u)))
    half = 0.5 * (1.0 + bent)
    act[...] = (u * half).astype(LOW)
    gate = half + 0.5 * u * (1.0 - bent * bent) * (slope * (1.0 + 3.0 * 0.044715 * square))
    grad = (dot(cot[...], down[...], 1, 0) * gate).astype(LOW)
    d_pre[...] = grad
    sums[...] = jnp.sum(grad.astype(F32), axis=0, keepdims=True)


def wide_kernel(x, w, *parts):
    wide = w.shape[2]
    block = dot(x[:, :wide], w[0], 1, 1) + dot(x[:, wide:], w[1], 1, 1)
    write_parts(block.astype(LOW), parts, slice(None))


def wide_grad_kernel(hid, cot, d_pre, act, out):
    wide = d_pre.shape[1]
    out[:, :wide] = dot(hid[...], d_pre[...], 0, 0).astype(LOW)
    out[:, wide:] = dot(cot[...], act[...], 0, 0).astype(LOW)


def residual_back_kernel(
    own, last_up, last_down, up, down, cot, residual, gain, d_res, d_low, sums
):
    d_hidden = summed_parts(own, last_up, last_down, up, down)
    normed, inv_std = center(residual[...])
    cot_float = cot[...].astype(F32)
    total = cot_float + norm_back(d_hidden, normed, inv_std, gain[...])
    d_res[...] = total
    d_low[...] = total.astype(LOW)
    rows = (total, d_hidden * normed, d_hidden, cot_float)
    for i, values in enumerate(rows):
        sums[i : i + 1, :] = jnp.sum(values, axis=0, keepdims=True)


def d_att_kernel(own, after, top, low, before, w0, w1, whole, out):
    join_pieces((own, after, top, low, before), whole)
    rows = out.shape[1]
    for pair, weight in enumerate((w0, w1)):
        grads = dot(whole[...], weight[...], 1, 0).astype(LOW)
        for row, slot in slots(rows):
            out[slot + pair] = grads[row : row + rows, :]


def d_in_kernel(grads, w0, w1, normed, whole, sums, totals, *parts):
    rows, wide = grads.shape[1], w0.shape[1]
    q_cols = grads.shape[2] // 2
    key_cols = wide - q_cols
    for row, slot in slots(rows):
        cut = slice(row, row + rows)
        for pair in range(PAIRS):
            start = pair * wide
            from_col = q_cols + pair * key_cols
            shared = grads[slot, :, from_col : from_col + key_cols].astype(F32) + grads[
                slot + 1, :, from_col : from_col + key_cols
            ].astype(F32)
            whole[cut, start : start + q_cols] = grads[slot + pair, :, :q_cols]
            whole[cut, start + q_cols : start + wide] = shared.astype(LOW)
    totals[...] = jnp.sum(whole[...].astype(F32), axis=0, keepdims=True)
    for start in range(0, w0.shape[0], 512):
        cols = slice(start, start + 512)
        block = dot(whole[:, :wide], w0[cols, :], 1, 1) + dot(whole[:, wide:], w1[cols, :], 1, 1)
        write_parts(block.astype(LOW), parts, cols)
        sums[0:1, cols] = jnp.sum(block * normed[:, cols].astype(F32), axis=0, keepdims=True)
        sums[1:2, cols] = jnp.sum(block, axis=0, keepdims=True)


def grad_rows_kernel(core_ref, left, right, *refs):
    *extra, out = refs
    wide = out.shape[-1]
    for pair in range(PAIRS):
        block = dot(left[...], right[:, pair * wide : (pair + 1) * wide], 0, 0)
        if extra:
            block = block + extra[0][0, pair, 0].astype(F32)
        out[0, pair, 0] = block.astype(LOW)


def input_kernel(own, last_up, last_down, up, down, x, d_res, gain, out):
    d_in = summed_parts(own, last_up, last_down, up, down)
    normed, inv_std = center(x[...].astype(F32))
    out[...] = d_res[...] + norm_back(d_in, normed, inv_std, gain[...])


VECTOR_ROWS = dict(
    ln1_gain=(0, 16),
    ln1_bias=(16, 16),
    b_query=(32, 16),
    b_value=(48, 1),
    b_out=(56, 16),
    ln2_gain=(72, 16),
    ln2_bias=(88, 16),
    b_fc2=(104, 16),
    b_fc=(120, 64),
)


def vectors_kernel(rank_ref, ln1_sums, totals, ln2_sums, fc_sums, gain, shift, out):
    out[...] = jnp.zeros_like(out)

    def put(name, offset, values):
        row = VECTOR_ROWS[name][0] + offset
        for i in range(values.shape[1] // 128):
            out[row + i : row + i + 1, :] = values[:, i * 128 : (i + 1) * 128]

    def put_mine(name, values):
        size = values.shape[1] // PAIRS
        for pair in range(PAIRS):
            for member in range(TEAM):
                block = values[:, pair * size : (pair + 1) * size]
                block = jnp.where(rank_ref[0] == member, block, 0.0)
                put(name, (pair * TEAM + member) * size // 128, block)

    put("ln1_gain", 0, (ln1_sums[0:1, :] - shift[...] * ln1_sums[1:2, :]) / gain[...])
    put("ln1_bias", 0, ln1_sums[1:2, :])
    wide = totals.shape[1] // PAIRS
    q_cols = wide * 2 // 3
    put_mine("b_query", jnp.concatenate([totals[:, :q_cols], totals[:, wide : wide + q_cols]], axis=1))
    put("b_value", 0, totals[:, wide + q_cols :])
    for i, name in enumerate(("b_out", "ln2_gain", "ln2_bias", "b_fc2")):
        put(name, 0, ln2_sums[i : i + 1, :])
    put_mine("b_fc", fc_sums[...])


def shaped(shape, kind=LOW):
    return jax.ShapeDtypeStruct(shape, kind)


def run(kernel, name, outs, args, flops=0, vmem=32, scalars=0, **more):
    size = sum(a.size * a.dtype.itemsize for a in args)
    size += sum(o.size * o.dtype.itemsize for o in outs)
    if scalars and "grid" not in more and "grid_spec" not in more:
        more["in_specs"] = [pl.BlockSpec(memory_space=pltpu.SMEM)] * scalars + [
            pl.BlockSpec(memory_space=pltpu.VMEM)
        ] * (len(args) - scalars)
    result = pl.pallas_call(
        kernel,
        out_shape=tuple(outs),
        compiler_params=pltpu.CompilerParams(vmem_limit_bytes=vmem * 2**20),
        cost_estimate=pl.CostEstimate(flops=flops, bytes_accessed=size, transcendentals=0),
        name=name,
        **more,
    )(*args)
    return result


def part_shapes(own, width):
    half = own // 2
    return [shaped((n, width)) for n in (own, half, own, own, half)]


def whole_block(array):
    return pl.BlockSpec(array.shape, lambda *_: (0,) * array.ndim)


def add_low(left, right):
    return (left.astype(F32) + right.astype(F32)).astype(LOW)


def after(values, *earlier):
    return lax.optimization_barrier((values, earlier))[0]


def shift(values, axis, step):
    return lax.ppermute(values, axis, [(i, (i + step) % TEAM) for i in range(TEAM)])


def other_core(values):
    return lax.ppermute(values, "c", [(0, 1), (1, 0)])


def ring_pieces(values, axis, *meanwhile):
    half = values.shape[0] // 2
    ahead = shift(values, axis, -1)
    behind = shift(values, axis, 1)
    if meanwhile:
        ahead, behind = after((ahead, behind), *meanwhile)
    top = shift(ahead[:half], axis, -1)
    low = shift(behind[half:], axis, 1)
    return values, ahead, top, low, behind


def ring_sum(parts, axis, *meanwhile):
    own, ahead, up, down, behind = parts
    half = ahead.shape[0]
    up = shift(up, axis, 1)
    down = shift(down, axis, -1)
    if meanwhile:
        up, down = after((up, down), *meanwhile)
    last_up = shift(add_low(ahead, up[half:]), axis, 1)
    last_down = shift(add_low(behind, down[:half]), axis, -1)
    return own, last_up, last_down, up, down


def ring_scatter(blocks, axis):
    own, ahead, far, behind = blocks
    half = own.shape[0] // 2
    up = jnp.concatenate([ahead[half:], far[:half]])
    down = jnp.concatenate([far[half:], behind[:half]])
    own, last_up, last_down, up, down = ring_sum(
        (own, ahead[:half], up, down, behind[half:]), axis
    )
    top = own[:half].astype(F32) + last_up.astype(F32) + down[half:].astype(F32)
    low = own[half:].astype(F32) + last_down.astype(F32) + up[:half].astype(F32)
    return jnp.concatenate([top, low])


def relative(values, axis, dim):
    me = lax.axis_index(axis)
    return [
        lax.dynamic_index_in_dim(values, (me + r) % TEAM, dim, keepdims=False) for r in range(TEAM)
    ]


def scatter_z_first(blocks):
    rows = ring_scatter(relative(blocks, Z, 0), Z).astype(LOW)
    return ring_scatter(relative(rows, "x", 0), "x")


def grad_rows(name, core, left, right, extra=None):
    rows = left.shape[1] // 16
    wide = right.shape[1] // PAIRS
    block = (1, PAIRS, 1, rows, wide)
    args = [left, right] + ([] if extra is None else [extra])
    specs = [
        pl.BlockSpec((left.shape[0], rows), lambda i, core: (0, 2 * i + core[0])),
        pl.BlockSpec(right.shape, lambda i, core: (0, 0)),
    ]
    place = pl.BlockSpec(block, lambda i, core: (i // 4, 0, i % 4, 0, 0))
    if extra is not None:
        specs.append(place)
    (result,) = run(
        grad_rows_kernel,
        name,
        [shaped((2, PAIRS, 4, rows, wide))],
        [core] + args,
        flops=left.size * right.shape[1],
        grid_spec=pltpu.PrefetchScalarGridSpec(
            num_scalar_prefetch=1, grid=(8,), in_specs=specs, out_specs=[place]
        ),
    )
    return result


def plane_scatter(blocks):
    blocks = jnp.transpose(blocks, (0, 2, 1, 3, 4)).reshape(16, *blocks.shape[3:])
    return jnp.sum(lax.all_to_all(blocks, PLANE, 0, 0, tiled=True).astype(F32), axis=0)


def body(
    tokens,
    segment_ids,
    ln1_gain,
    ln1_bias,
    w_query,
    b_query,
    w_kv,
    b_value,
    w_out,
    b_out,
    ln2_gain,
    ln2_bias,
    w_fc,
    b_fc,
    w_fc2,
    b_fc2,
    cotangent,
):
    micro, _, rows, width = tokens.shape
    head_dim = b_value.shape[0]
    q_cols = w_query.shape[1]
    heads = q_cols // head_dim
    hidden = w_fc.shape[1]
    wide = q_cols + head_dim
    own = micro * rows
    team_rows = TEAM * own
    rank = lax.axis_index("y")
    core_id = lax.axis_index("c")
    core = core_id.reshape(1)

    def row_of(vector):
        return vector.reshape(1, -1)

    def my_columns(vector):
        blocks = vector.reshape(PAIRS, TEAM, -1)
        return lax.dynamic_index_in_dim(blocks, rank, 1, keepdims=False)

    x_own = tokens.reshape(own, width)
    (norm_own,) = run(
        norm_kernel, "norm", [shaped((own, width))], [x_own, row_of(ln1_gain), row_of(ln1_bias)]
    )
    kv_spread = jnp.broadcast_to(w_kv.T[None], (TEAM,) + w_kv.T.shape)
    kv_block = lax.all_to_all(kv_spread, "y", 0, 0, tiled=True).reshape(-1, w_kv.shape[0]).T
    norm_pieces = ring_pieces(norm_own, "y")

    def from_plane(block):
        spread = jnp.broadcast_to(block[None], (16,) + block.shape)
        mine = lax.all_to_all(spread, PLANE, 0, 0, tiled=True)
        return mine.reshape(8, PAIRS, *block.shape)

    def both_cores(name, mine):
        rows, cols = mine.shape[2:]
        block = pl.BlockSpec((1,) + mine.shape[1:], lambda i, core: (i, 0, 0, 0))
        return run(
            weights_kernel,
            name,
            [shaped((width, cols))] * PAIRS,
            [core, mine, other_core(mine)],
            vmem=16,
            grid_spec=pltpu.PrefetchScalarGridSpec(
                num_scalar_prefetch=1,
                grid=(8,),
                in_specs=[block, block],
                out_specs=[pl.BlockSpec((2 * rows, cols), lambda i, core: (i, 0))] * PAIRS,
            ),
        )

    qkv_mine = from_plane(jnp.concatenate([w_query, kv_block], axis=1))
    w_qkv0, w_qkv1 = both_cores("w_qkv", qkv_mine)
    out_mine = from_plane(after(w_out, qkv_mine).T)
    packed = jnp.concatenate([w_fc, w_fc2.T], axis=1)
    w_wide = lax.all_gather(after(packed, qkv_mine), SHARERS, axis=0, tiled=True)

    bias_q = my_columns(b_query)
    bias0 = jnp.concatenate([bias_q[0], jnp.zeros((head_dim,), F32)])
    bias1 = jnp.concatenate([bias_q[1], b_value])
    normed_in, qkv_out = run(
        qkv_kernel,
        "qkv",
        [shaped((team_rows, width)), shaped((16, rows, 2 * q_cols))],
        [*norm_pieces, w_qkv0, w_qkv1, row_of(bias0), row_of(bias1)],
        flops=4 * team_rows * width * wide,
    )
    cot_own = cotangent.reshape(own, width)
    cot = jnp.concatenate(ring_pieces(after(cot_own, qkv_out), "y"))
    qkv = lax.all_to_all(after(qkv_out, out_mine), BLK, 0, 0, tiled=True)
    qkv = qkv.reshape(16 * rows, 2 * q_cols)
    w_out0, w_out1 = both_cores("w_out", after(out_mine, qkv_out))

    seq_rank = lax.axis_index("zl") * TEAM + (rank + lax.axis_index("x")) % TEAM
    segments = lax.dynamic_slice(
        segment_ids,
        (lax.axis_index("zh"), seq_rank, 0),
        (1, 1, segment_ids.shape[2]),
    ).reshape(-1, 1)
    length = qkv.shape[0]
    (attended,) = run(
        functools.partial(attend_kernel, heads, head_dim),
        "attend",
        [shaped((length, q_cols))],
        [segments, after(qkv, cot, w_out0)],
        flops=3 * length * length * q_cols,
    )
    attended = lax.all_to_all(attended.reshape(16, rows, q_cols), BLK, 0, 0, tiled=True)

    attention, *parts = run(
        project_kernel,
        "project",
        [shaped((team_rows, 2 * q_cols))] + part_shapes(own, width),
        [attended, w_out0, w_out1],
        flops=4 * team_rows * width * q_cols,
    )
    residual, hidden_own = run(
        residual_kernel,
        "residual",
        [shaped((own, width), F32), shaped((own, width))],
        [*ring_sum(parts, "y"), x_own, row_of(b_out), row_of(ln2_gain), row_of(ln2_bias)],
    )
    hidden_pieces = ring_pieces(hidden_own, "y")

    step = 256
    steps = PAIRS * hidden // step
    bias_fc = my_columns(b_fc).reshape(1, -1)
    piece_specs = [whole_block(piece) for piece in hidden_pieces]
    col_block = pl.BlockSpec((team_rows, step), lambda i: (0, i))
    row_block = pl.BlockSpec((1, step), lambda i: (0, i))
    per = hidden // step
    hidden_in, act, d_pre, fc_sums = run(
        hidden_kernel,
        "hidden",
        [shaped((team_rows, width))]
        + [shaped((team_rows, PAIRS * hidden))] * 2
        + [shaped((1, PAIRS * hidden), F32)],
        [*hidden_pieces, cot, w_wide, w_wide, bias_fc],
        flops=8 * team_rows * width * hidden,
        grid=(steps,),
        in_specs=piece_specs
        + [
            whole_block(cot),
            pl.BlockSpec((width, step), lambda i: (i // per, i % per)),
            pl.BlockSpec((width, step), lambda i: (i // per, per + i % per)),
            row_block,
        ],
        out_specs=[pl.BlockSpec((team_rows, width), lambda i: (0, 0)), col_block, col_block, row_block],
    )
    w_pair = w_wide.reshape(PAIRS, width, 2 * hidden)

    def wide_product(name, values, half):
        outs = part_shapes(own, width)
        return run(
            wide_kernel,
            name,
            outs,
            [values, w_pair],
            flops=4 * team_rows * width * hidden,
            grid=(width // step,),
            in_specs=[
                whole_block(values),
                pl.BlockSpec((PAIRS, step, hidden), lambda i: (0, i, half)),
            ],
            out_specs=[pl.BlockSpec((o.shape[0], step), lambda i: (0, i)) for o in outs],
        )

    d_hidden_parts = wide_product("d_hidden", d_pre, 0)
    (g_wide,) = run(
        wide_grad_kernel,
        "wide_grad",
        [shaped((width, 2 * PAIRS * hidden))],
        after([hidden_in, cot, d_pre, act], *d_hidden_parts),
        flops=8 * team_rows * width * hidden,
        grid=(width // step,),
        in_specs=[col_block, col_block, whole_block(d_pre), whole_block(act)],
        out_specs=[pl.BlockSpec((step, 2 * PAIRS * hidden), lambda i: (i, 0))],
    )
    g_sum = lax.psum_scatter(g_wide, BLK, scatter_dimension=0, tiled=True)
    g_sum = jnp.transpose(g_sum.reshape(-1, 2, PAIRS, hidden), (2, 0, 1, 3))
    z_lo = lax.axis_index("zl")
    g_kept = lax.dynamic_index_in_dim(g_sum, z_lo, 0, keepdims=False)
    g_sent = lax.dynamic_index_in_dim(g_sum, 1 - z_lo, 0, keepdims=False)
    g_other = lax.ppermute(g_sent, "zl", [(0, 1), (1, 0)])
    d_wide = g_kept.astype(F32) + g_other.astype(F32)

    d_res, d_res_own, ln2_sums = run(
        residual_back_kernel,
        "residual_back",
        [shaped((own, width), F32), shaped((own, width)), shaped((4, width), F32)],
        [*ring_sum(d_hidden_parts, "y", g_wide), cot_own, residual, row_of(ln2_gain)],
    )
    mlp_parts = wide_product("mlp", after(act, d_res_own), 1)
    d_res_low, d_att = run(
        d_att_kernel,
        "d_att",
        [shaped((team_rows, width)), shaped((16, rows, q_cols))],
        [*ring_pieces(d_res_own, "y", *mlp_parts), w_out0, w_out1],
        flops=4 * team_rows * width * q_cols,
    )
    d_att_seq = lax.all_to_all(d_att, BLK, 0, 0, tiled=True).reshape(length, q_cols)
    g_out_sent = grad_rows("g_out_sent", 1 - core, d_res_low, attention)
    mlp_parts = after(mlp_parts, d_att)

    (d_qkv_seq,) = run(
        functools.partial(attend_back_kernel, heads, head_dim),
        "attend_back",
        [shaped((length, 2 * q_cols))],
        [segments, qkv, after(d_att_seq, g_out_sent)],
        flops=6 * length * length * q_cols,
        scratch_shapes=[pltpu.VMEM((length, 2 * head_dim), F32)],
    )
    g_out = grad_rows(
        "g_out_kept", core, after(d_res_low, d_qkv_seq), attention, other_core(g_out_sent)
    )
    mlp_sums = ring_sum(mlp_parts, "y")
    output = (residual + summed_parts(*mlp_sums) + b_fc2).astype(LOW).reshape(tokens.shape)
    d_qkv_seq = lax.all_to_all(d_qkv_seq.reshape(16, rows, 2 * q_cols), BLK, 0, 0, tiled=True)
    d_qkv_seq = after(d_qkv_seq, g_out, output)
    d_qkv, ln1_sums, totals, *d_in_parts = run(
        d_in_kernel,
        "d_in",
        [shaped((team_rows, PAIRS * wide)), shaped((2, width), F32), shaped((1, PAIRS * wide), F32)]
        + part_shapes(own, width),
        [d_qkv_seq, w_qkv0, w_qkv1, normed_in],
        flops=4 * team_rows * width * wide,
    )
    g_qkv_sent = grad_rows("g_qkv_sent", 1 - core, normed_in, after(d_qkv, *d_in_parts))
    d_in_sums = ring_sum(d_in_parts, "y", g_qkv_sent)
    g_qkv = grad_rows("g_qkv_kept", core, normed_in, d_qkv, other_core(g_qkv_sent))
    d_out = scatter_z_first(g_out.reshape(4, *g_out.shape[2:]))
    (input_grad,) = run(
        input_kernel,
        "input",
        [shaped((own, width), F32)],
        [*d_in_sums, x_own, d_res, row_of(ln1_gain)],
    )
    d_small = plane_scatter(g_qkv)
    kv_parts = d_small[:, q_cols:].T.astype(LOW).reshape(TEAM, -1, d_small.shape[0])
    kv_parts = lax.all_to_all(kv_parts, "y", 0, 0, tiled=True)
    d_wkv = jnp.sum(kv_parts.astype(F32), axis=0).T

    (flat,) = run(
        vectors_kernel,
        "vectors",
        [shaped((256, 128), F32)],
        [
            rank.reshape(1),
            ln1_sums,
            totals,
            ln2_sums,
            fc_sums,
            row_of(ln1_gain),
            row_of(ln1_bias),
        ],
        scalars=1,
    )
    flat = lax.all_to_all(flat.reshape(128, 2, 128), ALL, 0, 0, tiled=True)
    flat = jnp.broadcast_to(jnp.sum(flat, axis=0, keepdims=True), flat.shape)
    flat = lax.all_to_all(flat, ALL, 0, 0, tiled=True).reshape(256, 128)
    vector = {
        name: flat[start : start + size].reshape(-1) for name, (start, size) in VECTOR_ROWS.items()
    }
    return (
        output,
        input_grad.reshape(tokens.shape),
        vector["ln1_gain"],
        vector["ln1_bias"],
        d_small[:, :q_cols],
        vector["b_query"],
        d_wkv,
        vector["b_value"],
        d_out.T,
        vector["b_out"],
        vector["ln2_gain"],
        vector["ln2_bias"],
        d_wide[:, 0],
        vector["b_fc"],
        d_wide[:, 1].T,
        vector["b_fc2"],
    )


def solution(mesh):
    fine = Mesh(mesh.devices.reshape(2, 4, 2, 2, 4), ALL)
    activations = P(None, HEAD, BLK, None)
    rows_first, cols_first = P(BLK, HEAD), P(HEAD, BLK)
    return jax.shard_map(
        body,
        mesh=fine,
        in_specs=(
            activations,
            P(),
            P(),
            P(),
            rows_first,
            P(),
            rows_first,
            P(),
            cols_first,
            P(),
            P(),
            P(),
            rows_first,
            P(),
            cols_first,
            P(),
            activations,
        ),
        out_specs=(
            activations,
            activations,
            P(),
            P(),
            rows_first,
            P(),
            rows_first,
            P(),
            cols_first,
            P(),
            P(),
            P(),
            rows_first,
            P(),
            cols_first,
            P(),
        ),
        check_vma=False,
    )
```

```python
import functools

import jax
import jax.numpy as jnp
from jax import lax
from jax.experimental import pallas as pl
from jax.experimental.pallas import tpu as pltpu
from jax.sharding import Mesh
from jax.sharding import PartitionSpec as P

EPS = 1e-05
NEG = -1e30
F32 = jnp.float32
LOW = jnp.bfloat16
BLK = ("zh", "x", "c")
HEAD = ("zl", "y")
PLANE = ("zh", "x", "zl")
SHARERS = ("zl", "zh", "x", "c")
Z = ("zh", "zl")
ALL = ("zh", "x", "c", "zl", "y")
Q_BLOCK = 256
TEAM = 4
PAIRS = 2


def dot(left, right, left_dim, right_dim):
    return lax.dot_general(
        left, right, (((left_dim,), (right_dim,)), ((), ())), preferred_element_type=F32
    )


def center(values):
    centered = values - jnp.mean(values, axis=-1, keepdims=True)
    inv_std = lax.rsqrt(jnp.mean(centered * centered, axis=-1, keepdims=True) + EPS)
    return centered * inv_std, inv_std


def norm_back(grad, normed, inv_std, gain):
    scaled = grad * gain
    first_mean = jnp.mean(scaled, axis=-1, keepdims=True)
    second_mean = jnp.mean(scaled * normed, axis=-1, keepdims=True)
    return inv_std * (scaled - first_mean - normed * second_mean)


def join_pieces(pieces, whole):
    row = 0
    for piece in pieces:
        whole[row : row + piece.shape[0], :] = piece[...]
        row += piece.shape[0]


def write_parts(block, parts, cols):
    row = 0
    for part in parts:
        part[:, cols] = block[row : row + part.shape[0], :]
        row += part.shape[0]


def summed_parts(own, last_up, last_down, up, down):
    half = own.shape[0] // 2
    top = own[:half].astype(F32) + last_up[...].astype(F32) + down[half:].astype(F32)
    low = own[half:].astype(F32) + last_down[...].astype(F32) + up[:half].astype(F32)
    return jnp.concatenate([top, low], axis=0)


def slots(rows):
    for member in range(TEAM):
        for micro in range(2):
            yield (member * 2 + micro) * rows, (micro * TEAM + member) * PAIRS


def norm_kernel(x_ref, gain_ref, shift_ref, out_ref):
    normed, _ = center(x_ref[...].astype(F32))
    out_ref[...] = (normed * gain_ref[...] + shift_ref[...]).astype(LOW)


def weights_kernel(core_ref, mine_ref, other_ref, *outs):
    first = core_ref[0] == 0
    rows = mine_ref.shape[2]
    for pair in range(PAIRS):
        mine, other = mine_ref[0, pair], other_ref[0, pair]
        for start, block in ((0, jnp.where(first, mine, other)), (rows, jnp.where(first, other, mine))):
            wide = outs[pair].shape[1]
            outs[pair][start : start + rows, :] = block[:, :wide]
            outs[PAIRS + pair][start : start + rows, :] = block[:, wide:]


def qkv_kernel(rank_ref, gathered, w0, w1, b0, b1, whole, out):
    size = gathered.shape[1]
    for step in range(TEAM):
        whole[step * size : (step + 1) * size, :] = gathered[lax.rem(rank_ref[0] + step, TEAM)]
    x = whole[...]
    rows, size = out.shape[1], b0.shape[1]
    first = (dot(x, w0[...], 1, 0) + b0[...]).astype(LOW)
    second = (dot(x, w1[...], 1, 0) + b1[...]).astype(LOW)
    q_cols = out.shape[2] - 2 * (size - out.shape[2] // 2)
    for row, slot in slots(rows):
        cut = slice(row, row + rows)
        shared = jnp.concatenate([first[cut, q_cols:], second[cut, q_cols:]], axis=1)
        out[slot, :, :q_cols] = first[cut, :q_cols]
        out[slot, :, q_cols:] = shared
        out[slot + 1, :, :q_cols] = second[cut, :q_cols]
        out[slot + 1, :, q_cols:] = shared


def block_probs(seg_ref, q_ref, keys, row, head, head_dim, scale):
    end = row + Q_BLOCK
    queries = q_ref[row:end, head * head_dim : (head + 1) * head_dim]
    scores = dot(queries, keys, 1, 1) * scale
    key_pos = lax.broadcasted_iota(jnp.int32, scores.shape, 1)
    query_pos = lax.broadcasted_iota(jnp.int32, scores.shape, 0) + row
    allowed = (key_pos <= query_pos) & (key_pos >= seg_ref[row:end, :])
    masked = jnp.where(allowed, scores, NEG)
    terms = jnp.exp(masked - jnp.max(masked, axis=1, keepdims=True))
    return queries, terms * (1.0 / jnp.sum(terms, axis=1, keepdims=True))


def attend_kernel(heads, head_dim, seg_ref, qkv_ref, out_ref):
    wide = heads * head_dim
    scale = head_dim**-0.5
    for row in range(0, qkv_ref.shape[0], Q_BLOCK):
        end = row + Q_BLOCK
        keys = qkv_ref[:end, wide : wide + head_dim]
        values = qkv_ref[:end, wide + head_dim :]
        for head in range(heads):
            _, probs = block_probs(seg_ref, qkv_ref, keys, row, head, head_dim, scale)
            out_ref[row:end, head * head_dim : (head + 1) * head_dim] = dot(
                probs.astype(LOW), values, 1, 0
            ).astype(LOW)


def attend_back_kernel(heads, head_dim, seg_ref, qkv_ref, grad_ref, out_ref, dkv_ref):
    wide = heads * head_dim
    scale = head_dim**-0.5
    dkv_ref[...] = jnp.zeros_like(dkv_ref)
    for row in range(0, qkv_ref.shape[0], Q_BLOCK):
        end = row + Q_BLOCK
        keys = qkv_ref[:end, wide : wide + head_dim]
        values = qkv_ref[:end, wide + head_dim :]
        for head in range(heads):
            cols = slice(head * head_dim, (head + 1) * head_dim)
            queries, probs = block_probs(seg_ref, qkv_ref, keys, row, head, head_dim, scale)
            grad = grad_ref[row:end, cols]
            d_probs = dot(grad, values, 1, 1)
            delta = jnp.sum(probs * d_probs, axis=1, keepdims=True)
            d_scores = (probs * (d_probs - delta)).astype(LOW)
            out_ref[row:end, cols] = (dot(d_scores, keys, 1, 0) * scale).astype(LOW)
            dkv_ref[:end, :head_dim] += dot(d_scores, queries, 0, 0)
            dkv_ref[:end, head_dim:] += dot(probs.astype(LOW), grad, 0, 0)
    out_ref[:, wide : wide + head_dim] = (dkv_ref[:, :head_dim] * scale).astype(LOW)
    out_ref[:, wide + head_dim :] = dkv_ref[:, head_dim:].astype(LOW)


def project_kernel(att, w0, w1, whole, *parts):
    rows, wide = att.shape[1], att.shape[2]
    for row, slot in slots(rows):
        for pair in range(PAIRS):
            whole[row : row + rows, pair * wide : (pair + 1) * wide] = att[slot + pair]
    for start in range(0, w0.shape[0], 512):
        cols = slice(start, start + 512)
        block = dot(whole[:, :wide], w0[cols, :], 1, 1) + dot(whole[:, wide:], w1[cols, :], 1, 1)
        write_parts(block.astype(LOW), parts, cols)


def residual_kernel(own, last_up, last_down, up, down, x, bias, gain, shift, residual, out):
    total = summed_parts(own, last_up, last_down, up, down)
    total = x[...].astype(F32) + total + bias[...]
    residual[...] = total
    normed, _ = center(total)
    out[...] = (normed * gain[...] + shift[...]).astype(LOW)


def hidden_kernel(own, after, top, low, before, cot, up, down, bias, whole, act, d_pre, sums):
    @pl.when(pl.program_id(0) == 0)
    def _():
        join_pieces((own, after, top, low, before), whole)

    u = dot(whole[...], up[...], 1, 0) + bias[...]
    slope = 2.0 ** 0.5 * jnp.pi ** -0.5
    square = u * u
    bent = jnp.tanh(slope * (u + 0.044715 * (square * u)))
    half = 0.5 * (1.0 + bent)
    act[...] = (u * half).astype(LOW)
    gate = half + 0.5 * u * (1.0 - bent * bent) * (slope * (1.0 + 3.0 * 0.044715 * square))
    grad = (dot(cot[...], down[...], 1, 0) * gate).astype(LOW)
    d_pre[...] = grad
    sums[...] = jnp.sum(grad.astype(F32), axis=0, keepdims=True)


def wide_kernel(x, w, *parts):
    wide = w.shape[2]
    block = dot(x[:, :wide], w[0], 1, 1) + dot(x[:, wide:], w[1], 1, 1)
    write_parts(block.astype(LOW), parts, slice(None))


def wide_grad_kernel(hid, cot, d_pre, act, out):
    cores, pairs, rows, cols = out.shape
    wide = cols // 2
    for half, left, right in ((0, hid, d_pre), (1, cot, act)):
        for pair in range(pairs):
            block = dot(left[...], right[:, pair * wide : (pair + 1) * wide], 0, 0).astype(LOW)
            for core in range(cores):
                out[core, pair, :, half * wide : (half + 1) * wide] = block[
                    core * rows : (core + 1) * rows, :
                ]


def wide_out_kernel(total, up, down):
    wide = up.shape[1]
    up[...] = total[:, :wide].astype(F32)
    down[...] = total[:, wide:].astype(F32).T


def residual_back_kernel(
    own, last_up, last_down, up, down, cot, residual, gain, d_res, d_low, sums
):
    d_hidden = summed_parts(own, last_up, last_down, up, down)
    normed, inv_std = center(residual[...])
    cot_float = cot[...].astype(F32)
    total = cot_float + norm_back(d_hidden, normed, inv_std, gain[...])
    d_res[...] = total
    d_low[...] = total.astype(LOW)
    rows = (total, d_hidden * normed, d_hidden, cot_float)
    for i, values in enumerate(rows):
        sums[i : i + 1, :] = jnp.sum(values, axis=0, keepdims=True)


def d_att_kernel(own, after, top, low, before, w0, w1, whole, out):
    join_pieces((own, after, top, low, before), whole)
    rows = out.shape[1]
    for pair, weight in enumerate((w0, w1)):
        grads = dot(whole[...], weight[...], 1, 0).astype(LOW)
        for row, slot in slots(rows):
            out[slot + pair] = grads[row : row + rows, :]


def d_in_kernel(grads, w0, w1, normed, whole, sums, totals, *parts):
    rows, wide = grads.shape[1], w0.shape[1]
    q_cols = grads.shape[2] // 2
    key_cols = wide - q_cols
    for row, slot in slots(rows):
        cut = slice(row, row + rows)
        for pair in range(PAIRS):
            start = pair * wide
            from_col = q_cols + pair * key_cols
            shared = grads[slot, :, from_col : from_col + key_cols].astype(F32) + grads[
                slot + 1, :, from_col : from_col + key_cols
            ].astype(F32)
            whole[cut, start : start + q_cols] = grads[slot + pair, :, :q_cols]
            whole[cut, start + q_cols : start + wide] = shared.astype(LOW)
    totals[...] = jnp.sum(whole[...].astype(F32), axis=0, keepdims=True)
    for start in range(0, w0.shape[0], 512):
        cols = slice(start, start + 512)
        block = dot(whole[:, :wide], w0[cols, :], 1, 1) + dot(whole[:, wide:], w1[cols, :], 1, 1)
        write_parts(block.astype(LOW), parts, cols)
        sums[0:1, cols] = jnp.sum(block * normed[:, cols].astype(F32), axis=0, keepdims=True)
        sums[1:2, cols] = jnp.sum(block, axis=0, keepdims=True)


def grad_rows_kernel(core_ref, left, right, *refs):
    *extra, out = refs
    wide = out.shape[-1]
    for pair in range(PAIRS):
        block = dot(left[...], right[:, pair * wide : (pair + 1) * wide], 0, 0)
        if extra:
            block = block + extra[0][0, 0, pair].astype(F32)
        out[0, 0, pair] = block.astype(LOW)


def input_kernel(own, last_up, last_down, up, down, x, d_res, gain, out):
    d_in = summed_parts(own, last_up, last_down, up, down)
    normed, inv_std = center(x[...].astype(F32))
    out[...] = d_res[...] + norm_back(d_in, normed, inv_std, gain[...])


VECTOR_ROWS = dict(
    ln1_gain=(0, 16),
    ln1_bias=(16, 16),
    b_query=(32, 16),
    b_out=(48, 16),
    ln2_gain=(64, 16),
    ln2_bias=(80, 16),
    b_fc2=(96, 16),
    b_fc=(112, 64),
    b_value=(176, 1),
)
VECTOR_TOTAL = 184


def vectors_kernel(rank_ref, ln1_sums, totals, ln2_sums, fc_sums, gain, shift, out):
    out[...] = jnp.zeros_like(out)

    def put(name, offset, values):
        row = VECTOR_ROWS[name][0] + offset
        for i in range(values.shape[1] // 128):
            out[row + i : row + i + 1, :] = values[:, i * 128 : (i + 1) * 128]

    def put_mine(name, values):
        size = values.shape[1] // PAIRS
        for pair in range(PAIRS):
            for member in range(TEAM):
                block = values[:, pair * size : (pair + 1) * size]
                block = jnp.where(rank_ref[0] == member, block, 0.0)
                put(name, (pair * TEAM + member) * size // 128, block)

    put("ln1_gain", 0, (ln1_sums[0:1, :] - shift[...] * ln1_sums[1:2, :]) / gain[...])
    put("ln1_bias", 0, ln1_sums[1:2, :])
    wide = totals.shape[1] // PAIRS
    q_cols = wide * 2 // 3
    put_mine("b_query", jnp.concatenate([totals[:, :q_cols], totals[:, wide : wide + q_cols]], axis=1))
    put("b_value", 0, totals[:, wide + q_cols :])
    for i, name in enumerate(("b_out", "ln2_gain", "ln2_bias", "b_fc2")):
        put(name, 0, ln2_sums[i : i + 1, :])
    put_mine("b_fc", fc_sums[...])


def plane_sum_kernel(cut, blocks, first, second):
    total = jnp.sum(blocks[...].astype(F32), axis=0)
    first[...] = total[:, :cut]
    second[...] = total[:, cut:].T.astype(second.dtype)


def shaped(shape, kind=LOW):
    return jax.ShapeDtypeStruct(shape, kind)


def run(kernel, name, outs, args, flops=0, vmem=32, scalars=0, **more):
    size = sum(a.size * a.dtype.itemsize for a in args)
    size += sum(o.size * o.dtype.itemsize for o in outs)
    if scalars and "grid" not in more and "grid_spec" not in more:
        more["in_specs"] = [pl.BlockSpec(memory_space=pltpu.SMEM)] * scalars + [
            pl.BlockSpec(memory_space=pltpu.VMEM)
        ] * (len(args) - scalars)
    result = pl.pallas_call(
        kernel,
        out_shape=tuple(outs),
        compiler_params=pltpu.CompilerParams(vmem_limit_bytes=vmem * 2**20),
        cost_estimate=pl.CostEstimate(flops=flops, bytes_accessed=size, transcendentals=0),
        name=name,
        **more,
    )(*args)
    return result


def part_shapes(own, width):
    half = own // 2
    return [shaped((n, width)) for n in (own, half, own, own, half)]


def whole_block(array):
    return pl.BlockSpec(array.shape, lambda *_: (0,) * array.ndim)


def add_low(left, right):
    return (left.astype(F32) + right.astype(F32)).astype(LOW)


def after(values, *earlier):
    return lax.optimization_barrier((values, earlier))[0]


def shift(values, axis, step):
    return lax.ppermute(values, axis, [(i, (i + step) % TEAM) for i in range(TEAM)])


def other_core(values):
    return lax.ppermute(values, "c", [(0, 1), (1, 0)])


def ring_pieces(values, axis, *meanwhile):
    half = values.shape[0] // 2
    ahead = shift(values, axis, -1)
    behind = shift(values, axis, 1)
    if meanwhile:
        ahead, behind = after((ahead, behind), *meanwhile)
    top = shift(ahead[:half], axis, -1)
    low = shift(behind[half:], axis, 1)
    return values, ahead, top, low, behind


def ring_sum(parts, axis, *meanwhile):
    own, ahead, up, down, behind = parts
    half = ahead.shape[0]
    up = shift(up, axis, 1)
    down = shift(down, axis, -1)
    if meanwhile:
        up, down = after((up, down), *meanwhile)
    last_up = shift(add_low(ahead, up[half:]), axis, 1)
    last_down = shift(add_low(behind, down[:half]), axis, -1)
    return own, last_up, last_down, up, down


def plane_scatter(blocks):
    return lax.all_to_all(blocks.reshape(16, *blocks.shape[3:]), PLANE, 0, 0, tiled=True)


def sum_over(values, axis):
    size = lax.axis_size(axis)
    found = [values] + [
        lax.ppermute(values, axis, [(i, i ^ bits) for i in range(size)]) for bits in range(1, size)
    ]
    if size == 2:
        return found[0] + found[1]
    return (found[0] + found[1]) + (found[2] + found[3])


def grad_rows(name, core, left, right, extra=None):
    rows = left.shape[1] // 16
    wide = right.shape[1] // PAIRS
    block = (1, 1, PAIRS, rows, wide)
    args = [left, right] + ([] if extra is None else [extra])
    specs = [
        pl.BlockSpec((left.shape[0], rows), lambda i, core: (0, 2 * i + core[0])),
        pl.BlockSpec(right.shape, lambda i, core: (0, 0)),
    ]
    place = pl.BlockSpec(block, lambda i, core: (i // 4, i % 4, 0, 0, 0))
    if extra is not None:
        specs.append(place)
    (result,) = run(
        grad_rows_kernel,
        name,
        [shaped((2, 4, PAIRS, rows, wide))],
        [core] + args,
        flops=left.size * right.shape[1],
        grid_spec=pltpu.PrefetchScalarGridSpec(
            num_scalar_prefetch=1, grid=(8,), in_specs=specs, out_specs=[place]
        ),
    )
    return result


def body(
    tokens,
    segment_ids,
    ln1_gain,
    ln1_bias,
    w_query,
    b_query,
    w_kv,
    b_value,
    w_out,
    b_out,
    ln2_gain,
    ln2_bias,
    w_fc,
    b_fc,
    w_fc2,
    b_fc2,
    cotangent,
):
    micro, _, rows, width = tokens.shape
    head_dim = b_value.shape[0]
    q_cols = w_query.shape[1]
    heads = q_cols // head_dim
    hidden = w_fc.shape[1]
    wide = q_cols + head_dim
    own = micro * rows
    team_rows = TEAM * own
    rank = lax.axis_index("y")
    core_id = lax.axis_index("c")
    core = core_id.reshape(1)

    def row_of(vector):
        return vector.reshape(1, -1)

    def my_columns(vector):
        blocks = vector.reshape(PAIRS, TEAM, -1)
        return lax.dynamic_index_in_dim(blocks, rank, 1, keepdims=False)

    x_own = tokens.reshape(own, width)
    (norm_own,) = run(
        norm_kernel, "norm", [shaped((own, width))], [x_own, row_of(ln1_gain), row_of(ln1_bias)]
    )
    kv_spread = jnp.broadcast_to(w_kv.T[None], (TEAM,) + w_kv.T.shape)
    kv_block = lax.all_to_all(kv_spread, "y", 0, 0, tiled=True).reshape(-1, w_kv.shape[0]).T
    gathered = lax.all_gather(norm_own, "y")

    small = jnp.concatenate([w_query, kv_block, w_out.T], axis=1)
    spread = jnp.broadcast_to(small[None], (16,) + small.shape)
    small_mine = lax.all_to_all(spread, PLANE, 0, 0, tiled=True).reshape(8, PAIRS, *small.shape)
    block = pl.BlockSpec((1, PAIRS) + small.shape, lambda i, core: (i, 0, 0, 0))
    w_qkv0, w_qkv1, w_out0, w_out1 = run(
        weights_kernel,
        "weights",
        [shaped((width, wide))] * PAIRS + [shaped((width, q_cols))] * PAIRS,
        [core, small_mine, other_core(small_mine)],
        grid_spec=pltpu.PrefetchScalarGridSpec(
            num_scalar_prefetch=1,
            grid=(8,),
            in_specs=[block, block],
            out_specs=[
                pl.BlockSpec((2 * small.shape[0], cols), lambda i, core: (i, 0))
                for cols in (wide, wide, q_cols, q_cols)
            ],
        ),
    )
    packed = jnp.concatenate([w_fc, w_fc2.T], axis=1)
    w_wide = lax.all_gather(after(packed, small_mine, gathered), SHARERS, axis=0, tiled=True)

    bias_q = my_columns(b_query)
    bias0 = jnp.concatenate([bias_q[0], jnp.zeros((head_dim,), F32)])
    bias1 = jnp.concatenate([bias_q[1], b_value])
    normed_in, qkv_out = run(
        qkv_kernel,
        "qkv",
        [shaped((team_rows, width)), shaped((16, rows, 2 * q_cols))],
        [rank.reshape(1), gathered, w_qkv0, w_qkv1, row_of(bias0), row_of(bias1)],
        flops=4 * team_rows * width * wide,
        scalars=1,
    )
    cot_own = cotangent.reshape(own, width)
    cot = jnp.concatenate(ring_pieces(after(cot_own, qkv_out), "y"))
    qkv = lax.all_to_all(qkv_out, BLK, 0, 0, tiled=True)
    qkv = qkv.reshape(16 * rows, 2 * q_cols)

    seq_rank = lax.axis_index("zl") * TEAM + (rank + lax.axis_index("x")) % TEAM
    segments = lax.dynamic_slice(
        segment_ids,
        (lax.axis_index("zh"), seq_rank, 0),
        (1, 1, segment_ids.shape[2]),
    ).reshape(-1, 1)
    length = qkv.shape[0]
    (attended,) = run(
        functools.partial(attend_kernel, heads, head_dim),
        "attend",
        [shaped((length, q_cols))],
        [segments, after(qkv, cot)],
        flops=3 * length * length * q_cols,
    )
    attended = lax.all_to_all(attended.reshape(16, rows, q_cols), BLK, 0, 0, tiled=True)

    attention, *parts = run(
        project_kernel,
        "project",
        [shaped((team_rows, 2 * q_cols))] + part_shapes(own, width),
        [attended, w_out0, w_out1],
        flops=4 * team_rows * width * q_cols,
    )
    residual, hidden_own = run(
        residual_kernel,
        "residual",
        [shaped((own, width), F32), shaped((own, width))],
        [*ring_sum(parts, "y"), x_own, row_of(b_out), row_of(ln2_gain), row_of(ln2_bias)],
    )
    hidden_pieces = ring_pieces(hidden_own, "y")

    step = 256
    steps = PAIRS * hidden // step
    bias_fc = my_columns(b_fc).reshape(1, -1)
    piece_specs = [whole_block(piece) for piece in hidden_pieces]
    col_block = pl.BlockSpec((team_rows, step), lambda i: (0, i))
    row_block = pl.BlockSpec((1, step), lambda i: (0, i))
    per = hidden // step
    hidden_in, act, d_pre, fc_sums = run(
        hidden_kernel,
        "hidden",
        [shaped((team_rows, width))]
        + [shaped((team_rows, PAIRS * hidden))] * 2
        + [shaped((1, PAIRS * hidden), F32)],
        [*hidden_pieces, cot, w_wide, w_wide, bias_fc],
        flops=8 * team_rows * width * hidden,
        grid=(steps,),
        in_specs=piece_specs
        + [
            whole_block(cot),
            pl.BlockSpec((width, step), lambda i: (i // per, i % per)),
            pl.BlockSpec((width, step), lambda i: (i // per, per + i % per)),
            row_block,
        ],
        out_specs=[pl.BlockSpec((team_rows, width), lambda i: (0, 0)), col_block, col_block, row_block],
    )
    w_pair = w_wide.reshape(PAIRS, width, 2 * hidden)

    column = 512

    def wide_product(name, values, half):
        outs = part_shapes(own, width)
        return run(
            wide_kernel,
            name,
            outs,
            [values, w_pair],
            flops=4 * team_rows * width * hidden,
            vmem=48,
            grid=(width // column,),
            in_specs=[
                whole_block(values),
                pl.BlockSpec((PAIRS, column, hidden), lambda i: (0, i, half)),
            ],
            out_specs=[pl.BlockSpec((o.shape[0], column), lambda i: (0, i)) for o in outs],
        )

    (g_wide,) = run(
        wide_grad_kernel,
        "wide_grad",
        [shaped((8, 4, width // 16, 2 * hidden))],
        [hidden_in, cot, d_pre, act],
        flops=8 * team_rows * width * hidden,
        grid=(width // step,),
        in_specs=[col_block, col_block, whole_block(d_pre), whole_block(act)],
        out_specs=[
            pl.BlockSpec((2, PAIRS, width // 16, 2 * hidden), lambda i: (i % 4, i // 4, 0, 0))
        ],
    )
    g_sum = lax.psum_scatter(
        g_wide.reshape(-1, 2 * hidden), ("x", "c"), scatter_dimension=0, tiled=True
    )
    g_sum = lax.psum_scatter(g_sum, Z, scatter_dimension=0, tiled=True)
    d_up, d_down = run(
        wide_out_kernel,
        "wide_out",
        [shaped(w_fc.shape, F32), shaped(w_fc2.shape, F32)],
        [g_sum],
    )
    d_hidden_parts = wide_product("d_hidden", after(d_pre, g_wide), 0)

    d_res, d_res_own, ln2_sums = run(
        residual_back_kernel,
        "residual_back",
        [shaped((own, width), F32), shaped((own, width)), shaped((4, width), F32)],
        [*ring_sum(d_hidden_parts, "y"), cot_own, residual, row_of(ln2_gain)],
    )
    mlp_parts = wide_product("mlp", after(act, d_res_own), 1)
    d_res_low, d_att = run(
        d_att_kernel,
        "d_att",
        [shaped((team_rows, width)), shaped((16, rows, q_cols))],
        [*ring_pieces(d_res_own, "y", mlp_parts[0]), w_out0, w_out1],
        flops=4 * team_rows * width * q_cols,
    )
    d_att_seq = lax.all_to_all(d_att, BLK, 0, 0, tiled=True).reshape(length, q_cols)
    g_out_sent = grad_rows("g_out_sent", 1 - core, d_res_low, attention)
    mlp_parts = after(mlp_parts, d_att)

    (d_qkv_seq,) = run(
        functools.partial(attend_back_kernel, heads, head_dim),
        "attend_back",
        [shaped((length, 2 * q_cols))],
        [segments, qkv, after(d_att_seq, g_out_sent)],
        flops=6 * length * length * q_cols,
        scratch_shapes=[pltpu.VMEM((length, 2 * head_dim), F32)],
    )
    g_out = grad_rows(
        "g_out_kept", core, after(d_res_low, d_qkv_seq), attention, other_core(g_out_sent)
    )
    mlp_sums = ring_sum(mlp_parts, "y")
    output = (residual + summed_parts(*mlp_sums) + b_fc2).astype(LOW).reshape(tokens.shape)
    d_qkv_seq = lax.all_to_all(d_qkv_seq.reshape(16, rows, 2 * q_cols), BLK, 0, 0, tiled=True)
    d_qkv_seq = after(d_qkv_seq, g_out, mlp_sums)
    g_out = plane_scatter(after(g_out, d_qkv_seq))
    d_qkv, ln1_sums, totals, *d_in_parts = run(
        d_in_kernel,
        "d_in",
        [shaped((team_rows, PAIRS * wide)), shaped((2, width), F32), shaped((1, PAIRS * wide), F32)]
        + part_shapes(own, width),
        [d_qkv_seq, w_qkv0, w_qkv1, normed_in],
        flops=4 * team_rows * width * wide,
    )
    (flat,) = run(
        vectors_kernel,
        "vectors",
        [shaped((VECTOR_TOTAL, 128), F32)],
        [
            rank.reshape(1),
            ln1_sums,
            totals,
            ln2_sums,
            fc_sums,
            row_of(ln1_gain),
            row_of(ln1_bias),
        ],
        scalars=1,
    )
    g_qkv_sent = grad_rows("g_qkv_sent", 1 - core, normed_in, d_qkv)
    g_qkv = grad_rows("g_qkv_kept", core, normed_in, d_qkv, other_core(g_qkv_sent))
    flat = sum_over(sum_over(after(flat, g_qkv), "y"), "c")
    g_qkv_here = plane_scatter(after(g_qkv, g_out))
    d_in_sums = ring_sum(d_in_parts, "y")
    (input_grad,) = run(
        input_kernel,
        "input",
        [shaped((own, width), F32)],
        [*d_in_sums, x_own, d_res, row_of(ln1_gain)],
    )

    rows_here = width // 16
    d_wout = jnp.sum(g_out.astype(F32), axis=0).T
    d_wq, kv_rows = run(
        functools.partial(plane_sum_kernel, q_cols),
        "plane_sum",
        [shaped((rows_here, q_cols), F32), shaped((head_dim, rows_here))],
        [g_qkv_here],
    )
    kv_rows = lax.all_to_all(kv_rows.reshape(TEAM, -1, rows_here), "y", 0, 0, tiled=True)
    d_wkv = jnp.sum(kv_rows.astype(F32), axis=0).T
    flat = sum_over(after(sum_over(flat, Z), d_wq), "x")
    vector = {
        name: flat[start : start + size].reshape(-1) for name, (start, size) in VECTOR_ROWS.items()
    }
    return (
        output,
        input_grad.reshape(tokens.shape),
        vector["ln1_gain"],
        vector["ln1_bias"],
        d_wq,
        vector["b_query"],
        d_wkv,
        vector["b_value"],
        d_wout,
        vector["b_out"],
        vector["ln2_gain"],
        vector["ln2_bias"],
        d_up,
        vector["b_fc"],
        d_down,
        vector["b_fc2"],
    )


def solution(mesh):
    fine = Mesh(mesh.devices.reshape(2, 4, 2, 2, 4), ALL)
    activations = P(None, HEAD, BLK, None)
    rows_first, cols_first = P(BLK, HEAD), P(HEAD, BLK)
    return jax.shard_map(
        body,
        mesh=fine,
        in_specs=(
            activations,
            P(),
            P(),
            P(),
            rows_first,
            P(),
            rows_first,
            P(),
            cols_first,
            P(),
            P(),
            P(),
            rows_first,
            P(),
            cols_first,
            P(),
            activations,
        ),
        out_specs=(
            activations,
            activations,
            P(),
            P(),
            rows_first,
            P(),
            rows_first,
            P(),
            cols_first,
            P(),
            P(),
            P(),
            rows_first,
            P(),
            cols_first,
            P(),
        ),
        check_vma=False,
    )
```

```python
import functools

import jax
import jax.numpy as jnp
from jax import lax
from jax.experimental import pallas as pl
from jax.experimental.pallas import tpu as pltpu
from jax.sharding import Mesh
from jax.sharding import PartitionSpec as P

EPS = 1e-05
NEG = -1e30
F32 = jnp.float32
LOW = jnp.bfloat16
BLK = ("zh", "x", "c")
HEAD = ("zl", "y")
PLANE = ("zh", "x", "zl")
SHARERS = ("zl", "zh", "x", "c")
Z = ("zh", "zl")
ALL = ("zh", "x", "c", "zl", "y")
Q_BLOCK = 256
TEAM = 4
PAIRS = 2


def dot(left, right, left_dim, right_dim):
    return lax.dot_general(
        left, right, (((left_dim,), (right_dim,)), ((), ())), preferred_element_type=F32
    )


def center(values):
    centered = values - jnp.mean(values, axis=-1, keepdims=True)
    inv_std = lax.rsqrt(jnp.mean(centered * centered, axis=-1, keepdims=True) + EPS)
    return centered * inv_std, inv_std


def norm_back(grad, normed, inv_std, gain):
    scaled = grad * gain
    first_mean = jnp.mean(scaled, axis=-1, keepdims=True)
    second_mean = jnp.mean(scaled * normed, axis=-1, keepdims=True)
    return inv_std * (scaled - first_mean - normed * second_mean)


def join_pieces(pieces, whole, sems):
    copies = []
    for i, piece in enumerate(pieces):
        size = piece.shape[0]
        copy = pltpu.make_async_copy(piece, whole.at[pl.ds(i * size, size)], sems.at[i])
        copy.start()
        copies.append(copy)
    for copy in copies:
        copy.wait()


def write_parts(block, parts, cols):
    row = 0
    for part in parts:
        part[:, cols] = block[row : row + part.shape[0], :]
        row += part.shape[0]


def summed_parts(own, last_up, last_down, up, down):
    half = own.shape[0] // 2
    top = own[:half].astype(F32) + last_up[...].astype(F32) + down[...].astype(F32)
    low = own[half:].astype(F32) + last_down[...].astype(F32) + up[...].astype(F32)
    return jnp.concatenate([top, low], axis=0)


def slots(rows):
    for member in range(TEAM):
        for micro in range(2):
            yield (member * 2 + micro) * rows, (micro * TEAM + member) * PAIRS


def norm_kernel(x_ref, gain_ref, shift_ref, out_ref):
    normed, _ = center(x_ref[...].astype(F32))
    out_ref[...] = (normed * gain_ref[...] + shift_ref[...]).astype(LOW)


def weights_kernel(core_ref, mine_ref, other_ref, *outs):
    first = core_ref[0] == 0
    rows = mine_ref.shape[2]
    for pair in range(PAIRS):
        mine, other = mine_ref[0, pair], other_ref[0, pair]
        for start, block in ((0, jnp.where(first, mine, other)), (rows, jnp.where(first, other, mine))):
            wide = outs[pair].shape[1]
            outs[pair][start : start + rows, :] = block[:, :wide]
            outs[PAIRS + pair][start : start + rows, :] = block[:, wide:]


def qkv_kernel(rank_ref, gathered, w0, w1, b0, b1, whole, out):
    size = gathered.shape[1]
    for step in range(TEAM):
        whole[step * size : (step + 1) * size, :] = gathered[lax.rem(rank_ref[0] + step, TEAM)]
    x = whole[...]
    rows, size = out.shape[1], b0.shape[1]
    first = (dot(x, w0[...], 1, 0) + b0[...]).astype(LOW)
    second = (dot(x, w1[...], 1, 0) + b1[...]).astype(LOW)
    q_cols = out.shape[2] - 2 * (size - out.shape[2] // 2)
    for row, slot in slots(rows):
        cut = slice(row, row + rows)
        shared = jnp.concatenate([first[cut, q_cols:], second[cut, q_cols:]], axis=1)
        out[slot, :, :q_cols] = first[cut, :q_cols]
        out[slot, :, q_cols:] = shared
        out[slot + 1, :, :q_cols] = second[cut, :q_cols]
        out[slot + 1, :, q_cols:] = shared


def block_probs(seg_ref, q_ref, keys, row, head, head_dim, scale):
    end = row + Q_BLOCK
    queries = q_ref[row:end, head * head_dim : (head + 1) * head_dim]
    scores = dot(queries, keys, 1, 1) * scale
    key_pos = lax.broadcasted_iota(jnp.int32, scores.shape, 1)
    query_pos = lax.broadcasted_iota(jnp.int32, scores.shape, 0) + row
    allowed = (key_pos <= query_pos) & (key_pos >= seg_ref[row:end, :])
    masked = jnp.where(allowed, scores, NEG)
    terms = jnp.exp(masked - jnp.max(masked, axis=1, keepdims=True))
    return queries, terms * (1.0 / jnp.sum(terms, axis=1, keepdims=True))


def attend_kernel(heads, head_dim, seg_ref, qkv_ref, out_ref):
    wide = heads * head_dim
    scale = head_dim**-0.5
    for row in range(0, qkv_ref.shape[0], Q_BLOCK):
        end = row + Q_BLOCK
        keys = qkv_ref[:end, wide : wide + head_dim]
        values = qkv_ref[:end, wide + head_dim :]
        for head in range(heads):
            _, probs = block_probs(seg_ref, qkv_ref, keys, row, head, head_dim, scale)
            out_ref[row:end, head * head_dim : (head + 1) * head_dim] = dot(
                probs.astype(LOW), values, 1, 0
            ).astype(LOW)


def attend_back_kernel(heads, head_dim, seg_ref, qkv_ref, grad_ref, out_ref, dkv_ref):
    wide = heads * head_dim
    scale = head_dim**-0.5
    dkv_ref[...] = jnp.zeros_like(dkv_ref)
    for row in range(0, qkv_ref.shape[0], Q_BLOCK):
        end = row + Q_BLOCK
        keys = qkv_ref[:end, wide : wide + head_dim]
        values = qkv_ref[:end, wide + head_dim :]
        for head in range(heads):
            cols = slice(head * head_dim, (head + 1) * head_dim)
            queries, probs = block_probs(seg_ref, qkv_ref, keys, row, head, head_dim, scale)
            grad = grad_ref[row:end, cols]
            d_probs = dot(grad, values, 1, 1)
            delta = jnp.sum(probs * d_probs, axis=1, keepdims=True)
            d_scores = (probs * (d_probs - delta)).astype(LOW)
            out_ref[row:end, cols] = (dot(d_scores, keys, 1, 0) * scale).astype(LOW)
            dkv_ref[:end, :head_dim] += dot(d_scores, queries, 0, 0)
            dkv_ref[:end, head_dim:] += dot(probs.astype(LOW), grad, 0, 0)
    out_ref[:, wide : wide + head_dim] = (dkv_ref[:, :head_dim] * scale).astype(LOW)
    out_ref[:, wide + head_dim :] = dkv_ref[:, head_dim:].astype(LOW)


def project_kernel(att, w0, w1, whole, *parts):
    rows, wide = att.shape[1], att.shape[2]
    for row, slot in slots(rows):
        for pair in range(PAIRS):
            whole[row : row + rows, pair * wide : (pair + 1) * wide] = att[slot + pair]
    for start in range(0, w0.shape[0], 512):
        cols = slice(start, start + 512)
        block = dot(whole[:, :wide], w0[cols, :], 1, 1) + dot(whole[:, wide:], w1[cols, :], 1, 1)
        write_parts(block.astype(LOW), parts, cols)


def residual_kernel(own, last_up, last_down, up, down, x, bias, gain, shift, residual, top, low):
    total = summed_parts(own, last_up, last_down, up, down)
    total = x[...].astype(F32) + total + bias[...]
    residual[...] = total
    normed, _ = center(total)
    out = (normed * gain[...] + shift[...]).astype(LOW)
    half = top.shape[0]
    top[...] = out[:half]
    low[...] = out[half:]


def hidden_kernel(*refs):
    pieces, (cot_far, up, down, bias, whole, act, d_pre, sums, cot, sems) = refs[:8], refs[8:]

    @pl.when(pl.program_id(0) == 0)
    def _():
        copy = pltpu.make_async_copy(cot_far, cot, sems.at[8])
        copy.start()
        join_pieces(pieces, whole, sems)
        copy.wait()

    u = dot(whole[...], up[...], 1, 0) + bias[...]
    slope = 2.0 ** 0.5 * jnp.pi ** -0.5
    square = u * u
    bent = jnp.tanh(slope * (u + 0.044715 * (square * u)))
    half = 0.5 * (1.0 + bent)
    act[...] = (u * half).astype(LOW)
    gate = half + 0.5 * u * (1.0 - bent * bent) * (slope * (1.0 + 3.0 * 0.044715 * square))
    grad = (dot(cot[...], down[...], 1, 0) * gate).astype(LOW)
    d_pre[...] = grad
    sums[...] = jnp.sum(grad.astype(F32), axis=0, keepdims=True)


def wide_kernel(x, w, *parts):
    wide = w.shape[2]
    block = dot(x[:, :wide], w[0], 1, 1) + dot(x[:, wide:], w[1], 1, 1)
    write_parts(block.astype(LOW), parts, slice(None))


def wide_grad_kernel(hid, cot, d_pre, act, out):
    cores, pairs, rows, cols = out.shape
    wide = cols // 2
    for half, left, right in ((0, hid, d_pre), (1, cot, act)):
        for pair in range(pairs):
            block = dot(left[...], right[:, pair * wide : (pair + 1) * wide], 0, 0).astype(LOW)
            for core in range(cores):
                out[core, pair, :, half * wide : (half + 1) * wide] = block[
                    core * rows : (core + 1) * rows, :
                ]


def wide_out_kernel(total, up, down):
    wide = up.shape[1]
    up[...] = total[:, :wide].astype(F32)
    down[...] = total[:, wide:].astype(F32).T


def residual_back_kernel(
    own, last_up, last_down, up, down, cot, residual, gain, d_res, top, low, sums
):
    d_hidden = summed_parts(own, last_up, last_down, up, down)
    normed, inv_std = center(residual[...])
    cot_float = cot[...].astype(F32)
    total = cot_float + norm_back(d_hidden, normed, inv_std, gain[...])
    d_res[...] = total
    half = top.shape[0]
    top[...] = total[:half].astype(LOW)
    low[...] = total[half:].astype(LOW)
    rows = (total, d_hidden * normed, d_hidden, cot_float)
    for i, values in enumerate(rows):
        sums[i : i + 1, :] = jnp.sum(values, axis=0, keepdims=True)


def d_att_kernel(*refs):
    pieces, (w0, w1, whole, out, sems) = refs[:8], refs[8:]
    join_pieces(pieces, whole, sems)
    rows = out.shape[1]
    for pair, weight in enumerate((w0, w1)):
        grads = dot(whole[...], weight[...], 1, 0).astype(LOW)
        for row, slot in slots(rows):
            out[slot + pair] = grads[row : row + rows, :]


def d_in_kernel(grads, w0_far, w1_far, normed, whole, sums, totals, *more):
    *parts, w0, w1, sems = more
    copies = [
        pltpu.make_async_copy(far, near, sems.at[i])
        for i, (far, near) in enumerate(((w0_far, w0), (w1_far, w1)))
    ]
    for copy in copies:
        copy.start()
    rows, wide = grads.shape[1], w0.shape[1]
    q_cols = grads.shape[2] // 2
    key_cols = wide - q_cols
    for row, slot in slots(rows):
        cut = slice(row, row + rows)
        for pair in range(PAIRS):
            start = pair * wide
            from_col = q_cols + pair * key_cols
            shared = grads[slot, :, from_col : from_col + key_cols].astype(F32) + grads[
                slot + 1, :, from_col : from_col + key_cols
            ].astype(F32)
            whole[cut, start : start + q_cols] = grads[slot + pair, :, :q_cols]
            whole[cut, start + q_cols : start + wide] = shared.astype(LOW)
    totals[...] = jnp.sum(whole[...].astype(F32), axis=0, keepdims=True)
    for copy in copies:
        copy.wait()
    for start in range(0, w0.shape[0], 512):
        cols = slice(start, start + 512)
        block = dot(whole[:, :wide], w0[cols, :], 1, 1) + dot(whole[:, wide:], w1[cols, :], 1, 1)
        write_parts(block.astype(LOW), parts, cols)
        sums[0:1, cols] = jnp.sum(block * normed[:, cols].astype(F32), axis=0, keepdims=True)
        sums[1:2, cols] = jnp.sum(block, axis=0, keepdims=True)


def grad_rows_kernel(core_ref, left, right, *refs):
    *extra, out = refs
    wide = right.shape[1] // PAIRS
    for pair in range(PAIRS):
        block = dot(left[...], right[:, pair * wide : (pair + 1) * wide], 0, 0)
        if extra:
            block = block + extra[0][0, 0, pair].astype(F32)
        out[0, 0, pair, :, :wide] = block.astype(LOW)
        if len(extra) > 1:
            out[0, 0, pair, :, wide:] = extra[1][0, 0, pair]


def output_kernel(own, last_up, last_down, up, down, residual, bias, out):
    mlp = summed_parts(own, last_up, last_down, up, down)
    out[...] = (residual[...] + mlp + bias[...]).astype(LOW)


def input_kernel(own, last_up, last_down, up, down, x, d_res, gain, out):
    d_in = summed_parts(own, last_up, last_down, up, down)
    normed, inv_std = center(x[...].astype(F32))
    out[...] = d_res[...] + norm_back(d_in, normed, inv_std, gain[...])


VECTOR_ROWS = dict(
    ln1_gain=(0, 16),
    ln1_bias=(16, 16),
    b_query=(32, 16),
    b_out=(48, 16),
    ln2_gain=(64, 16),
    ln2_bias=(80, 16),
    b_fc2=(96, 16),
    b_fc=(112, 64),
    b_value=(176, 1),
)
VECTOR_TOTAL = 184


def vectors_kernel(rank_ref, ln1_sums, totals, ln2_sums, fc_sums, gain, shift, out):
    out[...] = jnp.zeros_like(out)

    def put(name, offset, values):
        row = VECTOR_ROWS[name][0] + offset
        for i in range(values.shape[1] // 128):
            out[row + i : row + i + 1, :] = values[:, i * 128 : (i + 1) * 128]

    def put_mine(name, values):
        size = values.shape[1] // PAIRS
        for pair in range(PAIRS):
            for member in range(TEAM):
                block = values[:, pair * size : (pair + 1) * size]
                block = jnp.where(rank_ref[0] == member, block, 0.0)
                put(name, (pair * TEAM + member) * size // 128, block)

    put("ln1_gain", 0, (ln1_sums[0:1, :] - shift[...] * ln1_sums[1:2, :]) / gain[...])
    put("ln1_bias", 0, ln1_sums[1:2, :])
    wide = totals.shape[1] // PAIRS
    q_cols = wide * 2 // 3
    put_mine("b_query", jnp.concatenate([totals[:, :q_cols], totals[:, wide : wide + q_cols]], axis=1))
    put("b_value", 0, totals[:, wide + q_cols :])
    for i, name in enumerate(("b_out", "ln2_gain", "ln2_bias", "b_fc2")):
        put(name, 0, ln2_sums[i : i + 1, :])
    put_mine("b_fc", fc_sums[...])


def plane_sum_kernel(blocks, d_query, kv_rows, d_out):
    total = jnp.sum(blocks[...].astype(F32), axis=0)
    cut = d_query.shape[1]
    edge = cut + kv_rows.shape[0]
    d_query[...] = total[:, :cut]
    kv_rows[...] = total[:, cut:edge].T.astype(LOW)
    d_out[...] = total[:, edge:].T


def shaped(shape, kind=LOW):
    return jax.ShapeDtypeStruct(shape, kind)


def run(kernel, name, outs, args, flops=0, vmem=32, scalars=0, **more):
    size = sum(a.size * a.dtype.itemsize for a in args)
    size += sum(o.size * o.dtype.itemsize for o in outs)
    if scalars and "grid" not in more and "grid_spec" not in more:
        more["in_specs"] = [pl.BlockSpec(memory_space=pltpu.SMEM)] * scalars + [
            pl.BlockSpec(memory_space=pltpu.VMEM)
        ] * (len(args) - scalars)
    result = pl.pallas_call(
        kernel,
        out_shape=tuple(outs),
        compiler_params=pltpu.CompilerParams(vmem_limit_bytes=vmem * 2**20),
        cost_estimate=pl.CostEstimate(flops=flops, bytes_accessed=size, transcendentals=0),
        name=name,
        **more,
    )(*args)
    return result


def part_shapes(own, width):
    return [shaped((own, width))] + [shaped((own // 2, width))] * 6


def whole_block(array):
    return pl.BlockSpec(array.shape, lambda *_: (0,) * array.ndim)


def add_low(left, right):
    return (left.astype(F32) + right.astype(F32)).astype(LOW)


def after(values, *earlier):
    return lax.optimization_barrier((values, earlier))[0]


def shift(values, axis, step):
    return lax.ppermute(values, axis, [(i, (i + step) % TEAM) for i in range(TEAM)])


def other_core(values):
    return lax.ppermute(values, "c", [(0, 1), (1, 0)])


def ring_pieces(halves, axis, *meanwhile):
    top, low = halves
    ahead_top = shift(top, axis, -1)
    behind_low = shift(low, axis, 1)
    ahead_low = shift(low, axis, -1)
    behind_top = shift(top, axis, 1)
    sent_top, sent_low = ahead_top, behind_low
    if meanwhile:
        sent_top, sent_low = after((ahead_top, behind_low), *meanwhile)
    far_top = shift(sent_top, axis, -1)
    far_low = shift(sent_low, axis, 1)
    return top, low, ahead_top, ahead_low, far_top, far_low, behind_top, behind_low


def ring_sum(parts, axis):
    own, ahead_top, ahead_low, far_top, far_low, behind_top, behind_low = parts
    up = shift(far_top, axis, 1)
    down = shift(far_low, axis, -1)
    up_near = shift(ahead_low, axis, 1)
    down_near = shift(behind_top, axis, -1)
    last_up = shift(add_low(ahead_top, up), axis, 1)
    last_down = shift(add_low(behind_low, down), axis, -1)
    return own, last_up, last_down, up_near, down_near


def plane_scatter(blocks):
    return lax.all_to_all(blocks.reshape(16, *blocks.shape[3:]), PLANE, 0, 0, tiled=True)


def sum_over(values, axis):
    size = lax.axis_size(axis)
    found = [values] + [
        lax.ppermute(values, axis, [(i, i ^ bits) for i in range(size)]) for bits in range(1, size)
    ]
    if size == 2:
        return found[0] + found[1]
    return (found[0] + found[1]) + (found[2] + found[3])


def grad_rows(name, core, left, right, *extra):
    rows = left.shape[1] // 16
    wide = right.shape[1] // PAIRS
    cols = wide + sum(more.shape[-1] for more in extra[1:])

    def place(cols):
        return pl.BlockSpec(
            (1, 1, PAIRS, rows, cols), lambda i, core: (i // 4, i % 4, 0, 0, 0)
        )

    (result,) = run(
        grad_rows_kernel,
        name,
        [shaped((2, 4, PAIRS, rows, cols))],
        [core, left, right, *extra],
        flops=left.size * right.shape[1],
        grid_spec=pltpu.PrefetchScalarGridSpec(
            num_scalar_prefetch=1,
            grid=(8,),
            in_specs=[
                pl.BlockSpec((left.shape[0], rows), lambda i, core: (0, 2 * i + core[0])),
                pl.BlockSpec(right.shape, lambda i, core: (0, 0)),
            ]
            + [place(more.shape[-1]) for more in extra],
            out_specs=[place(cols)],
        ),
    )
    return result


def body(
    tokens,
    segment_ids,
    ln1_gain,
    ln1_bias,
    w_query,
    b_query,
    w_kv,
    b_value,
    w_out,
    b_out,
    ln2_gain,
    ln2_bias,
    w_fc,
    b_fc,
    w_fc2,
    b_fc2,
    cotangent,
):
    micro, _, rows, width = tokens.shape
    head_dim = b_value.shape[0]
    q_cols = w_query.shape[1]
    heads = q_cols // head_dim
    hidden = w_fc.shape[1]
    wide = q_cols + head_dim
    own = micro * rows
    team_rows = TEAM * own
    rank = lax.axis_index("y")
    core_id = lax.axis_index("c")
    core = core_id.reshape(1)

    def row_of(vector):
        return vector.reshape(1, -1)

    def my_columns(vector):
        blocks = vector.reshape(PAIRS, TEAM, -1)
        return lax.dynamic_index_in_dim(blocks, rank, 1, keepdims=False)

    x_own = tokens.reshape(own, width)
    (norm_own,) = run(
        norm_kernel, "norm", [shaped((own, width))], [x_own, row_of(ln1_gain), row_of(ln1_bias)]
    )
    kv_spread = jnp.broadcast_to(w_kv.T[None], (TEAM,) + w_kv.T.shape)
    kv_block = lax.all_to_all(kv_spread, "y", 0, 0, tiled=True).reshape(-1, w_kv.shape[0]).T
    gathered = lax.all_gather(norm_own, "y")

    small = jnp.concatenate([w_query, kv_block, w_out.T], axis=1)
    spread = jnp.broadcast_to(small[None], (16,) + small.shape)
    small_mine = lax.all_to_all(spread, PLANE, 0, 0, tiled=True).reshape(8, PAIRS, *small.shape)
    block = pl.BlockSpec((1, PAIRS) + small.shape, lambda i, core: (i, 0, 0, 0))
    w_qkv0, w_qkv1, w_out0, w_out1 = run(
        weights_kernel,
        "weights",
        [shaped((width, wide))] * PAIRS + [shaped((width, q_cols))] * PAIRS,
        [core, small_mine, other_core(small_mine)],
        grid_spec=pltpu.PrefetchScalarGridSpec(
            num_scalar_prefetch=1,
            grid=(8,),
            in_specs=[block, block],
            out_specs=[
                pl.BlockSpec((2 * small.shape[0], cols), lambda i, core: (i, 0))
                for cols in (wide, wide, q_cols, q_cols)
            ],
        ),
    )
    packed = jnp.concatenate([w_fc, w_fc2.T], axis=1)
    w_wide = lax.all_gather(after(packed, small_mine, gathered), SHARERS, axis=0, tiled=True)

    bias_q = my_columns(b_query)
    bias0 = jnp.concatenate([bias_q[0], jnp.zeros((head_dim,), F32)])
    bias1 = jnp.concatenate([bias_q[1], b_value])
    normed_in, qkv_out = run(
        qkv_kernel,
        "qkv",
        [shaped((team_rows, width)), shaped((16, rows, 2 * q_cols))],
        [rank.reshape(1), gathered, w_qkv0, w_qkv1, row_of(bias0), row_of(bias1)],
        flops=4 * team_rows * width * wide,
        scalars=1,
    )
    cot_own = cotangent.reshape(own, width)
    half_rows = own // 2
    cot_halves = after((cot_own[:half_rows], cot_own[half_rows:]), qkv_out)
    cot = jnp.concatenate(ring_pieces(cot_halves, "y"))
    qkv = lax.all_to_all(qkv_out, BLK, 0, 0, tiled=True)
    qkv = qkv.reshape(16 * rows, 2 * q_cols)

    seq_rank = lax.axis_index("zl") * TEAM + (rank + lax.axis_index("x")) % TEAM
    segments = lax.dynamic_slice(
        segment_ids,
        (lax.axis_index("zh"), seq_rank, 0),
        (1, 1, segment_ids.shape[2]),
    ).reshape(-1, 1)
    length = qkv.shape[0]
    (attended,) = run(
        functools.partial(attend_kernel, heads, head_dim),
        "attend",
        [shaped((length, q_cols))],
        [segments, after(qkv, cot)],
        flops=3 * length * length * q_cols,
    )
    attended = lax.all_to_all(attended.reshape(16, rows, q_cols), BLK, 0, 0, tiled=True)

    attention, *parts = run(
        project_kernel,
        "project",
        [shaped((team_rows, 2 * q_cols))] + part_shapes(own, width),
        [attended, w_out0, w_out1],
        flops=4 * team_rows * width * q_cols,
    )
    residual, *hidden_own = run(
        residual_kernel,
        "residual",
        [shaped((own, width), F32)] + [shaped((half_rows, width))] * 2,
        [*ring_sum(parts, "y"), x_own, row_of(b_out), row_of(ln2_gain), row_of(ln2_bias)],
    )
    hidden_pieces = ring_pieces(hidden_own, "y")

    step = 512
    steps = PAIRS * hidden // step
    bias_fc = my_columns(b_fc).reshape(1, -1)
    piece_specs = [pl.BlockSpec(memory_space=pl.ANY)] * 8
    col_block = pl.BlockSpec((team_rows, step), lambda i: (0, i))
    row_block = pl.BlockSpec((1, step), lambda i: (0, i))
    per = hidden // step
    hidden_in, act, d_pre, fc_sums = run(
        hidden_kernel,
        "hidden",
        [shaped((team_rows, width))]
        + [shaped((team_rows, PAIRS * hidden))] * 2
        + [shaped((1, PAIRS * hidden), F32)],
        [*hidden_pieces, cot, w_wide, w_wide, bias_fc],
        flops=8 * team_rows * width * hidden,
        grid=(steps,),
        in_specs=piece_specs
        + [
            pl.BlockSpec(memory_space=pltpu.HBM),
            pl.BlockSpec((width, step), lambda i: (i // per, i % per)),
            pl.BlockSpec((width, step), lambda i: (i // per, per + i % per)),
            row_block,
        ],
        out_specs=[pl.BlockSpec((team_rows, width), lambda i: (0, 0)), col_block, col_block, row_block],
        scratch_shapes=[pltpu.VMEM(cot.shape, LOW), pltpu.SemaphoreType.DMA((9,))],
        vmem=40,
    )
    column = step = 512
    col_block = pl.BlockSpec((team_rows, step), lambda i: (0, i))
    w_pair = w_wide.reshape(PAIRS, width, 2 * hidden)


    def wide_product(name, values, half):
        outs = part_shapes(own, width)
        return run(
            wide_kernel,
            name,
            outs,
            [values, w_pair],
            flops=4 * team_rows * width * hidden,
            vmem=48,
            grid=(width // column,),
            in_specs=[
                whole_block(values),
                pl.BlockSpec((PAIRS, column, hidden), lambda i: (0, i, half)),
            ],
            out_specs=[pl.BlockSpec((o.shape[0], column), lambda i: (0, i)) for o in outs],
        )

    (g_wide,) = run(
        wide_grad_kernel,
        "wide_grad",
        [shaped((8, 4, width // 16, 2 * hidden))],
        [hidden_in, cot, d_pre, act],
        flops=8 * team_rows * width * hidden,
        vmem=40,
        grid=(width // step,),
        in_specs=[col_block, col_block, whole_block(d_pre), whole_block(act)],
        out_specs=[
            pl.BlockSpec((4, PAIRS, width // 16, 2 * hidden), lambda i: (i % 2, i // 2, 0, 0))
        ],
    )
    g_sum = lax.psum_scatter(
        g_wide.reshape(-1, 2 * hidden), ("x", "c"), scatter_dimension=0, tiled=True
    )
    g_sum = lax.psum_scatter(g_sum, Z, scatter_dimension=0, tiled=True)
    d_up, d_down = run(
        wide_out_kernel,
        "wide_out",
        [shaped(w_fc.shape, F32), shaped(w_fc2.shape, F32)],
        [g_sum],
    )
    d_hidden_parts = wide_product("d_hidden", after(d_pre, g_wide), 0)

    d_res, *d_res_own, ln2_sums = run(
        residual_back_kernel,
        "residual_back",
        [shaped((own, width), F32)]
        + [shaped((half_rows, width))] * 2
        + [shaped((4, width), F32)],
        [*ring_sum(d_hidden_parts, "y"), cot_own, residual, row_of(ln2_gain)],
    )
    mlp_parts = wide_product("mlp", after(act, d_res_own[0]), 1)
    d_res_low, d_att = run(
        d_att_kernel,
        "d_att",
        [shaped((team_rows, width)), shaped((16, rows, q_cols))],
        [*ring_pieces(d_res_own, "y", mlp_parts[0]), w_out0, w_out1],
        flops=4 * team_rows * width * q_cols,
        in_specs=[pl.BlockSpec(memory_space=pl.ANY)] * 8
        + [pl.BlockSpec(memory_space=pltpu.VMEM)] * 2,
        scratch_shapes=[pltpu.SemaphoreType.DMA((8,))],
    )
    d_att_seq = lax.all_to_all(d_att, BLK, 0, 0, tiled=True).reshape(length, q_cols)
    g_out_sent = grad_rows("g_out_sent", 1 - core, d_res_low, attention)
    mlp_parts = after(mlp_parts, d_att)

    (d_qkv_seq,) = run(
        functools.partial(attend_back_kernel, heads, head_dim),
        "attend_back",
        [shaped((length, 2 * q_cols))],
        [segments, qkv, after(d_att_seq, g_out_sent)],
        flops=6 * length * length * q_cols,
        scratch_shapes=[pltpu.VMEM((length, 2 * head_dim), F32)],
    )
    g_out = grad_rows(
        "g_out_kept", core, after(d_res_low, d_qkv_seq), attention, other_core(g_out_sent)
    )
    mlp_sums = ring_sum(mlp_parts, "y")
    (output,) = run(
        output_kernel, "output", [shaped((own, width))], [*mlp_sums, residual, row_of(b_fc2)]
    )
    output = output.reshape(tokens.shape)
    d_qkv_seq = lax.all_to_all(d_qkv_seq.reshape(16, rows, 2 * q_cols), BLK, 0, 0, tiled=True)
    d_qkv_seq = after(d_qkv_seq, g_out, mlp_sums)
    d_qkv, ln1_sums, totals, *d_in_parts = run(
        d_in_kernel,
        "d_in",
        [shaped((team_rows, PAIRS * wide)), shaped((2, width), F32), shaped((1, PAIRS * wide), F32)]
        + part_shapes(own, width),
        [d_qkv_seq, w_qkv0, w_qkv1, normed_in],
        flops=4 * team_rows * width * wide,
        in_specs=[
            pl.BlockSpec(memory_space=pltpu.VMEM),
            pl.BlockSpec(memory_space=pl.ANY),
            pl.BlockSpec(memory_space=pl.ANY),
            pl.BlockSpec(memory_space=pltpu.VMEM),
        ],
        scratch_shapes=[pltpu.VMEM((width, wide), LOW)] * 2 + [pltpu.SemaphoreType.DMA((2,))],
    )
    (flat,) = run(
        vectors_kernel,
        "vectors",
        [shaped((VECTOR_TOTAL, 128), F32)],
        [
            rank.reshape(1),
            ln1_sums,
            totals,
            ln2_sums,
            fc_sums,
            row_of(ln1_gain),
            row_of(ln1_bias),
        ],
        scalars=1,
    )
    g_qkv_sent = grad_rows("g_qkv_sent", 1 - core, normed_in, d_qkv)
    small = grad_rows("small_grads", core, normed_in, d_qkv, other_core(g_qkv_sent), g_out)
    small_here = plane_scatter(small)
    d_in_sums = ring_sum(after(d_in_parts, small), "y")
    flat = sum_over(sum_over(after(flat, d_in_sums[3]), "y"), "c")
    (input_grad,) = run(
        input_kernel,
        "input",
        [shaped((own, width), F32)],
        [*d_in_sums, x_own, d_res, row_of(ln1_gain)],
    )

    rows_here = width // 16
    d_wq, kv_rows, d_wout = run(
        plane_sum_kernel,
        "plane_sum",
        [
            shaped((rows_here, q_cols), F32),
            shaped((head_dim, rows_here)),
            shaped((q_cols, rows_here), F32),
        ],
        [after(small_here, input_grad, output)],
    )
    kv_rows = lax.all_to_all(kv_rows.reshape(TEAM, -1, rows_here), "y", 0, 0, tiled=True)
    d_wkv = jnp.sum(kv_rows.astype(F32), axis=0).T
    flat = sum_over(sum_over(after(flat, d_wq), Z), "x")
    vector = {
        name: flat[start : start + size].reshape(-1) for name, (start, size) in VECTOR_ROWS.items()
    }
    return (
        output,
        input_grad.reshape(tokens.shape),
        vector["ln1_gain"],
        vector["ln1_bias"],
        d_wq,
        vector["b_query"],
        d_wkv,
        vector["b_value"],
        d_wout,
        vector["b_out"],
        vector["ln2_gain"],
        vector["ln2_bias"],
        d_up,
        vector["b_fc"],
        d_down,
        vector["b_fc2"],
    )


def solution(mesh):
    fine = Mesh(mesh.devices.reshape(2, 4, 2, 2, 4), ALL)
    activations = P(None, HEAD, BLK, None)
    rows_first, cols_first = P(BLK, HEAD), P(HEAD, BLK)
    return jax.shard_map(
        body,
        mesh=fine,
        in_specs=(
            activations,
            P(),
            P(),
            P(),
            rows_first,
            P(),
            rows_first,
            P(),
            cols_first,
            P(),
            P(),
            P(),
            rows_first,
            P(),
            cols_first,
            P(),
            activations,
        ),
        out_specs=(
            activations,
            activations,
            P(),
            P(),
            rows_first,
            P(),
            rows_first,
            P(),
            cols_first,
            P(),
            P(),
            P(),
            rows_first,
            P(),
            cols_first,
            P(),
        ),
        check_vma=False,
    )
```

```python
import functools

import jax
import jax.numpy as jnp
from jax import lax
from jax.experimental import pallas as pl
from jax.experimental.pallas import tpu as pltpu
from jax.sharding import Mesh
from jax.sharding import PartitionSpec as P

EPS = 1e-05
NEG = -1e30
F32 = jnp.float32
LOW = jnp.bfloat16
BLK = ("zh", "x", "c")
HEAD = ("zl", "y")
PLANE = ("zh", "x", "zl")
SHARERS = ("zl", "zh", "x", "c")
Z = ("zh", "zl")
ALL = ("zh", "x", "c", "zl", "y")
Q_BLOCK = 256
TEAM = 4
PAIRS = 2


def dot(left, right, left_dim, right_dim):
    return lax.dot_general(
        left, right, (((left_dim,), (right_dim,)), ((), ())), preferred_element_type=F32
    )


def center(values):
    centered = values - jnp.mean(values, axis=-1, keepdims=True)
    inv_std = lax.rsqrt(jnp.mean(centered * centered, axis=-1, keepdims=True) + EPS)
    return centered * inv_std, inv_std


def norm_back(grad, normed, inv_std, gain):
    scaled = grad * gain
    first_mean = jnp.mean(scaled, axis=-1, keepdims=True)
    second_mean = jnp.mean(scaled * normed, axis=-1, keepdims=True)
    return inv_std * (scaled - first_mean - normed * second_mean)


def join_pieces(pieces, whole, sems):
    copies = []
    for i, piece in enumerate(pieces):
        size = piece.shape[0]
        copy = pltpu.make_async_copy(piece, whole.at[pl.ds(i * size, size)], sems.at[i])
        copy.start()
        copies.append(copy)
    for copy in copies:
        copy.wait()


def write_parts(block, parts, cols):
    row = 0
    for part in parts:
        part[:, cols] = block[row : row + part.shape[0], :]
        row += part.shape[0]


def summed_parts(own, last_up, last_down, up, down):
    half = own.shape[0] // 2
    top = own[:half].astype(F32) + last_up[...].astype(F32) + down[...].astype(F32)
    low = own[half:].astype(F32) + last_down[...].astype(F32) + up[...].astype(F32)
    return jnp.concatenate([top, low], axis=0)


def slots(rows):
    for member in range(TEAM):
        for micro in range(2):
            yield (member * 2 + micro) * rows, (micro * TEAM + member) * PAIRS


def norm_kernel(x_ref, gain_ref, shift_ref, out_ref):
    normed, _ = center(x_ref[...].astype(F32))
    out_ref[...] = (normed * gain_ref[...] + shift_ref[...]).astype(LOW)


def weights_kernel(core_ref, mine_ref, other_ref, *outs):
    first = core_ref[0] == 0
    rows = mine_ref.shape[2]
    for pair in range(PAIRS):
        mine, other = mine_ref[0, pair], other_ref[0, pair]
        for start, block in ((0, jnp.where(first, mine, other)), (rows, jnp.where(first, other, mine))):
            wide = outs[pair].shape[1]
            outs[pair][start : start + rows, :] = block[:, :wide]
            outs[PAIRS + pair][start : start + rows, :] = block[:, wide:]


def qkv_kernel(rank_ref, gathered, w0, w1, b0, b1, whole, out):
    size = gathered.shape[1]
    for step in range(TEAM):
        whole[step * size : (step + 1) * size, :] = gathered[lax.rem(rank_ref[0] + step, TEAM)]
    x = whole[...]
    rows, size = out.shape[1], b0.shape[1]
    first = (dot(x, w0[...], 1, 0) + b0[...]).astype(LOW)
    second = (dot(x, w1[...], 1, 0) + b1[...]).astype(LOW)
    q_cols = out.shape[2] - 2 * (size - out.shape[2] // 2)
    for row, slot in slots(rows):
        cut = slice(row, row + rows)
        shared = jnp.concatenate([first[cut, q_cols:], second[cut, q_cols:]], axis=1)
        out[slot, :, :q_cols] = first[cut, :q_cols]
        out[slot, :, q_cols:] = shared
        out[slot + 1, :, :q_cols] = second[cut, :q_cols]
        out[slot + 1, :, q_cols:] = shared


def block_probs(seg_ref, q_ref, keys, row, head, head_dim, scale):
    end = row + Q_BLOCK
    queries = q_ref[row:end, head * head_dim : (head + 1) * head_dim]
    scores = dot(queries, keys, 1, 1) * scale
    key_pos = lax.broadcasted_iota(jnp.int32, scores.shape, 1)
    query_pos = lax.broadcasted_iota(jnp.int32, scores.shape, 0) + row
    allowed = (key_pos <= query_pos) & (key_pos >= seg_ref[row:end, :])
    masked = jnp.where(allowed, scores, NEG)
    terms = jnp.exp(masked - jnp.max(masked, axis=1, keepdims=True))
    return queries, terms * (1.0 / jnp.sum(terms, axis=1, keepdims=True))


def attend_kernel(heads, head_dim, seg_ref, qkv_ref, out_ref):
    wide = heads * head_dim
    scale = head_dim**-0.5
    for row in range(0, qkv_ref.shape[0], Q_BLOCK):
        end = row + Q_BLOCK
        keys = qkv_ref[:end, wide : wide + head_dim]
        values = qkv_ref[:end, wide + head_dim :]
        for head in range(heads):
            _, probs = block_probs(seg_ref, qkv_ref, keys, row, head, head_dim, scale)
            out_ref[row:end, head * head_dim : (head + 1) * head_dim] = dot(
                probs.astype(LOW), values, 1, 0
            ).astype(LOW)


def attend_back_kernel(heads, head_dim, seg_ref, qkv_ref, grad_ref, out_ref, dkv_ref):
    wide = heads * head_dim
    scale = head_dim**-0.5
    dkv_ref[...] = jnp.zeros_like(dkv_ref)
    for row in range(0, qkv_ref.shape[0], Q_BLOCK):
        end = row + Q_BLOCK
        keys = qkv_ref[:end, wide : wide + head_dim]
        values = qkv_ref[:end, wide + head_dim :]
        for head in range(heads):
            cols = slice(head * head_dim, (head + 1) * head_dim)
            queries, probs = block_probs(seg_ref, qkv_ref, keys, row, head, head_dim, scale)
            grad = grad_ref[row:end, cols]
            d_probs = dot(grad, values, 1, 1)
            delta = jnp.sum(probs * d_probs, axis=1, keepdims=True)
            d_scores = (probs * (d_probs - delta)).astype(LOW)
            out_ref[row:end, cols] = (dot(d_scores, keys, 1, 0) * scale).astype(LOW)
            dkv_ref[:end, :head_dim] += dot(d_scores, queries, 0, 0)
            dkv_ref[:end, head_dim:] += dot(probs.astype(LOW), grad, 0, 0)
    out_ref[:, wide : wide + head_dim] = (dkv_ref[:, :head_dim] * scale).astype(LOW)
    out_ref[:, wide + head_dim :] = dkv_ref[:, head_dim:].astype(LOW)


def project_kernel(att, w0, w1, whole, *parts):
    rows, wide = att.shape[1], att.shape[2]
    for row, slot in slots(rows):
        for pair in range(PAIRS):
            whole[row : row + rows, pair * wide : (pair + 1) * wide] = att[slot + pair]
    for start in range(0, w0.shape[0], 512):
        cols = slice(start, start + 512)
        block = dot(whole[:, :wide], w0[cols, :], 1, 1) + dot(whole[:, wide:], w1[cols, :], 1, 1)
        write_parts(block.astype(LOW), parts, cols)


def residual_kernel(own, last_up, last_down, up, down, x, bias, gain, shift, residual, top, low):
    total = summed_parts(own, last_up, last_down, up, down)
    total = x[...].astype(F32) + total + bias[...]
    residual[...] = total
    normed, _ = center(total)
    out = (normed * gain[...] + shift[...]).astype(LOW)
    half = top.shape[0]
    top[...] = out[:half]
    low[...] = out[half:]


def hidden_kernel(*refs):
    pieces, (cot_far, up, down, bias, whole, act, d_pre, sums, cot, sems) = refs[:8], refs[8:]

    @pl.when(pl.program_id(0) == 0)
    def _():
        copy = pltpu.make_async_copy(cot_far, cot, sems.at[8])
        copy.start()
        join_pieces(pieces, whole, sems)
        copy.wait()

    u = dot(whole[...], up[...], 1, 0) + bias[...]
    slope = 2.0 ** 0.5 * jnp.pi ** -0.5
    square = u * u
    bent = jnp.tanh(slope * (u + 0.044715 * (square * u)))
    half = 0.5 * (1.0 + bent)
    act[...] = (u * half).astype(LOW)
    gate = half + 0.5 * u * (1.0 - bent * bent) * (slope * (1.0 + 3.0 * 0.044715 * square))
    grad = (dot(cot[...], down[...], 1, 0) * gate).astype(LOW)
    d_pre[...] = grad
    sums[...] = jnp.sum(grad.astype(F32), axis=0, keepdims=True)


def wide_kernel(x, w, *parts):
    wide = w.shape[2]
    block = dot(x[:, :wide], w[0], 1, 1) + dot(x[:, wide:], w[1], 1, 1)
    write_parts(block.astype(LOW), parts, slice(None))


def wide_grad_kernel(hid, cot, d_pre, act, out):
    cores, pairs, rows, cols = out.shape
    wide = cols // 2
    for half, left, right in ((0, hid, d_pre), (1, cot, act)):
        for pair in range(pairs):
            block = dot(left[...], right[:, pair * wide : (pair + 1) * wide], 0, 0).astype(LOW)
            for core in range(cores):
                out[core, pair, :, half * wide : (half + 1) * wide] = block[
                    core * rows : (core + 1) * rows, :
                ]


def wide_out_kernel(total, up, down):
    wide = up.shape[1]
    up[...] = total[:, :wide].astype(F32)
    down[...] = total[:, wide:].astype(F32).T


def residual_back_kernel(
    own, last_up, last_down, up, down, cot, residual, gain, d_res, top, low, sums
):
    d_hidden = summed_parts(own, last_up, last_down, up, down)
    normed, inv_std = center(residual[...])
    cot_float = cot[...].astype(F32)
    total = cot_float + norm_back(d_hidden, normed, inv_std, gain[...])
    d_res[...] = total
    half = top.shape[0]
    top[...] = total[:half].astype(LOW)
    low[...] = total[half:].astype(LOW)
    rows = (total, d_hidden * normed, d_hidden, cot_float)
    for i, values in enumerate(rows):
        sums[i : i + 1, :] = jnp.sum(values, axis=0, keepdims=True)


def d_att_kernel(*refs):
    pieces, (w0, w1, whole, out, sems) = refs[:8], refs[8:]
    join_pieces(pieces, whole, sems)
    rows = out.shape[1]
    for pair, weight in enumerate((w0, w1)):
        grads = dot(whole[...], weight[...], 1, 0).astype(LOW)
        for row, slot in slots(rows):
            out[slot + pair] = grads[row : row + rows, :]


def d_in_kernel(grads, w0_far, w1_far, normed, whole, sums, totals, *more):
    *parts, w0, w1, sems = more
    copies = [
        pltpu.make_async_copy(far, near, sems.at[i])
        for i, (far, near) in enumerate(((w0_far, w0), (w1_far, w1)))
    ]
    for copy in copies:
        copy.start()
    rows, wide = grads.shape[1], w0.shape[1]
    q_cols = grads.shape[2] // 2
    key_cols = wide - q_cols
    for row, slot in slots(rows):
        cut = slice(row, row + rows)
        for pair in range(PAIRS):
            start = pair * wide
            from_col = q_cols + pair * key_cols
            shared = grads[slot, :, from_col : from_col + key_cols].astype(F32) + grads[
                slot + 1, :, from_col : from_col + key_cols
            ].astype(F32)
            whole[cut, start : start + q_cols] = grads[slot + pair, :, :q_cols]
            whole[cut, start + q_cols : start + wide] = shared.astype(LOW)
    totals[...] = jnp.sum(whole[...].astype(F32), axis=0, keepdims=True)
    for copy in copies:
        copy.wait()
    for start in range(0, w0.shape[0], 512):
        cols = slice(start, start + 512)
        block = dot(whole[:, :wide], w0[cols, :], 1, 1) + dot(whole[:, wide:], w1[cols, :], 1, 1)
        write_parts(block.astype(LOW), parts, cols)
        sums[0:1, cols] = jnp.sum(block * normed[:, cols].astype(F32), axis=0, keepdims=True)
        sums[1:2, cols] = jnp.sum(block, axis=0, keepdims=True)


def grad_rows_kernel(core_ref, left0, left1, right, *refs):
    *extra, out = refs
    wide, rows = right.shape[1] // PAIRS, left0.shape[1]
    left = jnp.concatenate([left0[...], left1[...]], axis=1)
    for pair in range(PAIRS):
        both = dot(left, right[:, pair * wide : (pair + 1) * wide], 0, 0)
        for i in range(2):
            block = both[i * rows : (i + 1) * rows, :]
            if extra:
                block = block + extra[0][0, i, pair].astype(F32)
            out[0, i, pair, :, :wide] = block.astype(LOW)
            if len(extra) > 1:
                out[0, i, pair, :, wide:] = extra[1][0, i, pair]


def output_kernel(own, last_up, last_down, up, down, residual, bias, out):
    mlp = summed_parts(own, last_up, last_down, up, down)
    out[...] = (residual[...] + mlp + bias[...]).astype(LOW)


def input_kernel(own, last_up, last_down, up, down, x, d_res, gain, out):
    d_in = summed_parts(own, last_up, last_down, up, down)
    normed, inv_std = center(x[...].astype(F32))
    out[...] = d_res[...] + norm_back(d_in, normed, inv_std, gain[...])


VECTOR_ROWS = dict(
    ln1_gain=(0, 16),
    ln1_bias=(16, 16),
    b_query=(32, 16),
    b_out=(48, 16),
    ln2_gain=(64, 16),
    ln2_bias=(80, 16),
    b_fc2=(96, 16),
    b_fc=(112, 64),
    b_value=(176, 1),
)
VECTOR_TOTAL = 184


def vectors_kernel(rank_ref, ln1_sums, totals, ln2_sums, fc_sums, gain, shift, out):
    out[...] = jnp.zeros_like(out)

    def put(name, offset, values):
        row = VECTOR_ROWS[name][0] + offset
        for i in range(values.shape[1] // 128):
            out[row + i : row + i + 1, :] = values[:, i * 128 : (i + 1) * 128]

    def put_mine(name, values):
        size = values.shape[1] // PAIRS
        for pair in range(PAIRS):
            for member in range(TEAM):
                block = values[:, pair * size : (pair + 1) * size]
                block = jnp.where(rank_ref[0] == member, block, 0.0)
                put(name, (pair * TEAM + member) * size // 128, block)

    put("ln1_gain", 0, (ln1_sums[0:1, :] - shift[...] * ln1_sums[1:2, :]) / gain[...])
    put("ln1_bias", 0, ln1_sums[1:2, :])
    wide = totals.shape[1] // PAIRS
    q_cols = wide * 2 // 3
    put_mine("b_query", jnp.concatenate([totals[:, :q_cols], totals[:, wide : wide + q_cols]], axis=1))
    put("b_value", 0, totals[:, wide + q_cols :])
    for i, name in enumerate(("b_out", "ln2_gain", "ln2_bias", "b_fc2")):
        put(name, 0, ln2_sums[i : i + 1, :])
    put_mine("b_fc", fc_sums[...])


def plane_sum_kernel(blocks, d_query, kv_rows, d_out):
    total = jnp.sum(blocks[...].astype(F32), axis=0)
    cut = d_query.shape[1]
    edge = cut + kv_rows.shape[0]
    d_query[...] = total[:, :cut]
    kv_rows[...] = total[:, cut:edge].T.astype(LOW)
    d_out[...] = total[:, edge:].T


def shaped(shape, kind=LOW):
    return jax.ShapeDtypeStruct(shape, kind)


ALONE = ("attend_back", "small_grads")


def run(kernel, name, outs, args, flops=0, vmem=None, scalars=0, **more):
    vmem = vmem or (58 if name in ALONE else 20)
    size = sum(a.size * a.dtype.itemsize for a in args)
    size += sum(o.size * o.dtype.itemsize for o in outs)
    if scalars and "grid" not in more and "grid_spec" not in more:
        more["in_specs"] = [pl.BlockSpec(memory_space=pltpu.SMEM)] * scalars + [
            pl.BlockSpec(memory_space=pltpu.VMEM)
        ] * (len(args) - scalars)
    result = pl.pallas_call(
        kernel,
        out_shape=tuple(outs),
        compiler_params=pltpu.CompilerParams(vmem_limit_bytes=vmem * 2**20),
        cost_estimate=pl.CostEstimate(flops=flops, bytes_accessed=size, transcendentals=0),
        name=name,
        **more,
    )(*args)
    return result


def part_shapes(own, width):
    return [shaped((own, width))] + [shaped((own // 2, width))] * 6


def whole_block(array):
    return pl.BlockSpec(array.shape, lambda *_: (0,) * array.ndim)


def add_low(left, right):
    return (left.astype(F32) + right.astype(F32)).astype(LOW)


def after(values, *earlier):
    return lax.optimization_barrier((values, earlier))[0]


def shift(values, axis, step):
    return lax.ppermute(values, axis, [(i, (i + step) % TEAM) for i in range(TEAM)])


def other_core(values):
    return lax.ppermute(values, "c", [(0, 1), (1, 0)])


def ring_pieces(halves, axis, *meanwhile):
    top, low = halves
    ahead_top = shift(top, axis, -1)
    behind_low = shift(low, axis, 1)
    ahead_low = shift(low, axis, -1)
    behind_top = shift(top, axis, 1)
    sent_top, sent_low = ahead_top, behind_low
    if meanwhile:
        sent_top, sent_low = after((ahead_top, behind_low), *meanwhile)
    far_top = shift(sent_top, axis, -1)
    far_low = shift(sent_low, axis, 1)
    return top, low, ahead_top, ahead_low, far_top, far_low, behind_top, behind_low


def ring_sum(parts, axis):
    own, ahead_top, ahead_low, far_top, far_low, behind_top, behind_low = parts
    up = shift(far_top, axis, 1)
    down = shift(far_low, axis, -1)
    up_near = shift(ahead_low, axis, 1)
    down_near = shift(behind_top, axis, -1)
    last_up = shift(add_low(ahead_top, up), axis, 1)
    last_down = shift(add_low(behind_low, down), axis, -1)
    return own, last_up, last_down, up_near, down_near


def plane_scatter(blocks):
    return lax.all_to_all(blocks.reshape(16, *blocks.shape[3:]), PLANE, 0, 0, tiled=True)


def sum_over(values, axis):
    size = lax.axis_size(axis)
    found = [values] + [
        lax.ppermute(values, axis, [(i, i ^ bits) for i in range(size)]) for bits in range(1, size)
    ]
    if size == 2:
        return found[0] + found[1]
    return (found[0] + found[1]) + (found[2] + found[3])


def grad_rows(name, core, left, right, *extra):
    rows = left.shape[1] // 16
    wide = right.shape[1] // PAIRS
    cols = wide + sum(more.shape[-1] for more in extra[1:])

    def place(cols):
        return pl.BlockSpec(
            (1, 2, PAIRS, rows, cols), lambda i, core: (i // 2, i % 2, 0, 0, 0)
        )

    (result,) = run(
        grad_rows_kernel,
        name,
        [shaped((2, 4, PAIRS, rows, cols))],
        [core, left, left, right, *extra],
        flops=left.size * right.shape[1],
        grid_spec=pltpu.PrefetchScalarGridSpec(
            num_scalar_prefetch=1,
            grid=(4,),
            in_specs=[
                pl.BlockSpec((left.shape[0], rows), lambda i, core: (0, 4 * i + core[0])),
                pl.BlockSpec((left.shape[0], rows), lambda i, core: (0, 4 * i + 2 + core[0])),
                pl.BlockSpec(right.shape, lambda i, core: (0, 0)),
            ]
            + [place(more.shape[-1]) for more in extra],
            out_specs=[place(cols)],
        ),
    )
    return result


def body(
    tokens,
    segment_ids,
    ln1_gain,
    ln1_bias,
    w_query,
    b_query,
    w_kv,
    b_value,
    w_out,
    b_out,
    ln2_gain,
    ln2_bias,
    w_fc,
    b_fc,
    w_fc2,
    b_fc2,
    cotangent,
):
    micro, _, rows, width = tokens.shape
    head_dim = b_value.shape[0]
    q_cols = w_query.shape[1]
    heads = q_cols // head_dim
    hidden = w_fc.shape[1]
    wide = q_cols + head_dim
    own = micro * rows
    team_rows = TEAM * own
    rank = lax.axis_index("y")
    core_id = lax.axis_index("c")
    core = core_id.reshape(1)

    def row_of(vector):
        return vector.reshape(1, -1)

    def my_columns(vector):
        blocks = vector.reshape(PAIRS, TEAM, -1)
        return lax.dynamic_index_in_dim(blocks, rank, 1, keepdims=False)

    x_own = tokens.reshape(own, width)
    (norm_own,) = run(
        norm_kernel, "norm", [shaped((own, width))], [x_own, row_of(ln1_gain), row_of(ln1_bias)]
    )
    kv_spread = jnp.broadcast_to(w_kv.T[None], (TEAM,) + w_kv.T.shape)
    kv_block = lax.all_to_all(kv_spread, "y", 0, 0, tiled=True).reshape(-1, w_kv.shape[0]).T
    gathered = lax.all_gather(norm_own, "y")

    small = jnp.concatenate([w_query, kv_block, w_out.T], axis=1)
    spread = jnp.broadcast_to(small[None], (16,) + small.shape)
    small_mine = lax.all_to_all(spread, PLANE, 0, 0, tiled=True).reshape(8, PAIRS, *small.shape)
    block = pl.BlockSpec((1, PAIRS) + small.shape, lambda i, core: (i, 0, 0, 0))
    w_qkv0, w_qkv1, w_out0, w_out1 = run(
        weights_kernel,
        "weights",
        [shaped((width, wide))] * PAIRS + [shaped((width, q_cols))] * PAIRS,
        [core, small_mine, other_core(small_mine)],
        grid_spec=pltpu.PrefetchScalarGridSpec(
            num_scalar_prefetch=1,
            grid=(8,),
            in_specs=[block, block],
            out_specs=[
                pl.BlockSpec((2 * small.shape[0], cols), lambda i, core: (i, 0))
                for cols in (wide, wide, q_cols, q_cols)
            ],
        ),
    )
    packed = jnp.concatenate([w_fc, w_fc2.T], axis=1)
    w_wide = lax.all_gather(after(packed, small_mine, gathered), SHARERS, axis=0, tiled=True)

    bias_q = my_columns(b_query)
    bias0 = jnp.concatenate([bias_q[0], jnp.zeros((head_dim,), F32)])
    bias1 = jnp.concatenate([bias_q[1], b_value])
    normed_in, qkv_out = run(
        qkv_kernel,
        "qkv",
        [shaped((team_rows, width)), shaped((16, rows, 2 * q_cols))],
        [rank.reshape(1), gathered, w_qkv0, w_qkv1, row_of(bias0), row_of(bias1)],
        flops=4 * team_rows * width * wide,
        scalars=1,
    )
    cot_own = cotangent.reshape(own, width)
    half_rows = own // 2
    cot_halves = after((cot_own[:half_rows], cot_own[half_rows:]), qkv_out)
    cot = jnp.concatenate(ring_pieces(cot_halves, "y"))
    qkv = lax.all_to_all(qkv_out, BLK, 0, 0, tiled=True)
    qkv = qkv.reshape(16 * rows, 2 * q_cols)

    seq_rank = lax.axis_index("zl") * TEAM + (rank + lax.axis_index("x")) % TEAM
    segments = lax.dynamic_slice(
        segment_ids,
        (lax.axis_index("zh"), seq_rank, 0),
        (1, 1, segment_ids.shape[2]),
    ).reshape(-1, 1)
    length = qkv.shape[0]
    (attended,) = run(
        functools.partial(attend_kernel, heads, head_dim),
        "attend",
        [shaped((length, q_cols))],
        [segments, after(qkv, cot)],
        flops=3 * length * length * q_cols,
    )
    attended = lax.all_to_all(attended.reshape(16, rows, q_cols), BLK, 0, 0, tiled=True)

    attention, *parts = run(
        project_kernel,
        "project",
        [shaped((team_rows, 2 * q_cols))] + part_shapes(own, width),
        [attended, w_out0, w_out1],
        flops=4 * team_rows * width * q_cols,
    )
    residual, *hidden_own = run(
        residual_kernel,
        "residual",
        [shaped((own, width), F32)] + [shaped((half_rows, width))] * 2,
        [*ring_sum(parts, "y"), x_own, row_of(b_out), row_of(ln2_gain), row_of(ln2_bias)],
    )
    hidden_pieces = ring_pieces(hidden_own, "y")

    step = 512
    steps = PAIRS * hidden // step
    bias_fc = my_columns(b_fc).reshape(1, -1)
    piece_specs = [pl.BlockSpec(memory_space=pl.ANY)] * 8
    col_block = pl.BlockSpec((team_rows, step), lambda i: (0, i))
    row_block = pl.BlockSpec((1, step), lambda i: (0, i))
    per = hidden // step
    hidden_in, act, d_pre, fc_sums = run(
        hidden_kernel,
        "hidden",
        [shaped((team_rows, width))]
        + [shaped((team_rows, PAIRS * hidden))] * 2
        + [shaped((1, PAIRS * hidden), F32)],
        [*hidden_pieces, cot, w_wide, w_wide, bias_fc],
        flops=8 * team_rows * width * hidden,
        grid=(steps,),
        in_specs=piece_specs
        + [
            pl.BlockSpec(memory_space=pltpu.HBM),
            pl.BlockSpec((width, step), lambda i: (i // per, i % per)),
            pl.BlockSpec((width, step), lambda i: (i // per, per + i % per)),
            row_block,
        ],
        out_specs=[pl.BlockSpec((team_rows, width), lambda i: (0, 0)), col_block, col_block, row_block],
        scratch_shapes=[pltpu.VMEM(cot.shape, LOW), pltpu.SemaphoreType.DMA((9,))],
        vmem=40,
    )
    column = step = 512
    col_block = pl.BlockSpec((team_rows, step), lambda i: (0, i))
    w_pair = w_wide.reshape(PAIRS, width, 2 * hidden)


    def wide_product(name, values, half):
        outs = part_shapes(own, width)
        return run(
            wide_kernel,
            name,
            outs,
            [values, w_pair],
            flops=4 * team_rows * width * hidden,
            vmem=45,
            grid=(width // column,),
            in_specs=[
                whole_block(values),
                pl.BlockSpec((PAIRS, column, hidden), lambda i: (0, i, half)),
            ],
            out_specs=[pl.BlockSpec((o.shape[0], column), lambda i: (0, i)) for o in outs],
        )

    (g_wide,) = run(
        wide_grad_kernel,
        "wide_grad",
        [shaped((8, 4, width // 16, 2 * hidden))],
        [hidden_in, cot, d_pre, act],
        flops=8 * team_rows * width * hidden,
        vmem=40,
        grid=(width // step,),
        in_specs=[col_block, col_block, whole_block(d_pre), whole_block(act)],
        out_specs=[
            pl.BlockSpec((4, PAIRS, width // 16, 2 * hidden), lambda i: (i % 2, i // 2, 0, 0))
        ],
    )
    g_sum = lax.psum_scatter(
        g_wide.reshape(-1, 2 * hidden), ("x", "c"), scatter_dimension=0, tiled=True
    )
    g_sum = lax.psum_scatter(g_sum, Z, scatter_dimension=0, tiled=True)
    d_up, d_down = run(
        wide_out_kernel,
        "wide_out",
        [shaped(w_fc.shape, F32), shaped(w_fc2.shape, F32)],
        [g_sum],
    )
    d_hidden_parts = wide_product("d_hidden", after(d_pre, g_wide), 0)

    d_res, *d_res_own, ln2_sums = run(
        residual_back_kernel,
        "residual_back",
        [shaped((own, width), F32)]
        + [shaped((half_rows, width))] * 2
        + [shaped((4, width), F32)],
        [*ring_sum(d_hidden_parts, "y"), cot_own, residual, row_of(ln2_gain)],
    )
    mlp_parts = wide_product("mlp", after(act, d_res_own[0]), 1)
    d_res_low, d_att = run(
        d_att_kernel,
        "d_att",
        [shaped((team_rows, width)), shaped((16, rows, q_cols))],
        [*ring_pieces(d_res_own, "y", mlp_parts[0]), w_out0, w_out1],
        flops=4 * team_rows * width * q_cols,
        in_specs=[pl.BlockSpec(memory_space=pl.ANY)] * 8
        + [pl.BlockSpec(memory_space=pltpu.VMEM)] * 2,
        scratch_shapes=[pltpu.SemaphoreType.DMA((8,))],
    )
    d_att_seq = lax.all_to_all(d_att, BLK, 0, 0, tiled=True).reshape(length, q_cols)
    g_out_sent = grad_rows("g_out_sent", 1 - core, d_res_low, attention)
    mlp_parts = after(mlp_parts, d_att)

    (d_qkv_seq,) = run(
        functools.partial(attend_back_kernel, heads, head_dim),
        "attend_back",
        [shaped((length, 2 * q_cols))],
        [segments, qkv, after(d_att_seq, g_out_sent)],
        flops=6 * length * length * q_cols,
        scratch_shapes=[pltpu.VMEM((length, 2 * head_dim), F32)],
    )
    g_out = grad_rows(
        "g_out_kept", core, after(d_res_low, d_qkv_seq), attention, other_core(g_out_sent)
    )
    mlp_sums = ring_sum(mlp_parts, "y")
    (output,) = run(
        output_kernel, "output", [shaped((own, width))], [*mlp_sums, residual, row_of(b_fc2)]
    )
    d_qkv_seq = lax.all_to_all(d_qkv_seq.reshape(16, rows, 2 * q_cols), BLK, 0, 0, tiled=True)
    d_qkv_seq = after(d_qkv_seq, g_out, mlp_sums)
    d_qkv, ln1_sums, totals, *d_in_parts = run(
        d_in_kernel,
        "d_in",
        [shaped((team_rows, PAIRS * wide)), shaped((2, width), F32), shaped((1, PAIRS * wide), F32)]
        + part_shapes(own, width),
        [d_qkv_seq, w_qkv0, w_qkv1, normed_in],
        flops=4 * team_rows * width * wide,
        in_specs=[
            pl.BlockSpec(memory_space=pltpu.VMEM),
            pl.BlockSpec(memory_space=pl.ANY),
            pl.BlockSpec(memory_space=pl.ANY),
            pl.BlockSpec(memory_space=pltpu.VMEM),
        ],
        scratch_shapes=[pltpu.VMEM((width, wide), LOW)] * 2 + [pltpu.SemaphoreType.DMA((2,))],
    )
    (flat,) = run(
        vectors_kernel,
        "vectors",
        [shaped((VECTOR_TOTAL, 128), F32)],
        [
            rank.reshape(1),
            ln1_sums,
            totals,
            ln2_sums,
            fc_sums,
            row_of(ln1_gain),
            row_of(ln1_bias),
        ],
        scalars=1,
    )
    g_qkv_sent = grad_rows("g_qkv_sent", 1 - core, normed_in, d_qkv)
    small = grad_rows("small_grads", core, normed_in, d_qkv, other_core(g_qkv_sent), g_out)
    small_here = plane_scatter(small)
    d_in_sums = ring_sum(after(d_in_parts, small), "y")
    flat = sum_over(sum_over(after(flat, d_in_sums[3]), "y"), "c")
    (input_grad,) = run(
        input_kernel,
        "input",
        [shaped((own, width), F32)],
        [*d_in_sums, x_own, d_res, row_of(ln1_gain)],
    )

    rows_here = width // 16
    d_wq, kv_rows, d_wout = run(
        plane_sum_kernel,
        "plane_sum",
        [
            shaped((rows_here, q_cols), F32),
            shaped((head_dim, rows_here)),
            shaped((q_cols, rows_here), F32),
        ],
        [after(small_here, input_grad, output)],
    )
    kv_rows = lax.all_to_all(kv_rows.reshape(TEAM, -1, rows_here), "y", 0, 0, tiled=True)
    d_wkv = jnp.sum(after(kv_rows, d_up, d_down).astype(F32), axis=0).T
    flat = sum_over(after(sum_over(flat, Z), d_wq), "x")
    vector = {
        name: flat[start : start + size].reshape(-1) for name, (start, size) in VECTOR_ROWS.items()
    }
    return (
        output.reshape(tokens.shape),
        input_grad.reshape(tokens.shape),
        vector["ln1_gain"],
        vector["ln1_bias"],
        d_wq,
        vector["b_query"],
        d_wkv,
        vector["b_value"],
        d_wout,
        vector["b_out"],
        vector["ln2_gain"],
        vector["ln2_bias"],
        d_up,
        vector["b_fc"],
        d_down,
        vector["b_fc2"],
    )


def solution(mesh):
    fine = Mesh(mesh.devices.reshape(2, 4, 2, 2, 4), ALL)
    activations = P(None, HEAD, BLK, None)
    rows_first, cols_first = P(BLK, HEAD), P(HEAD, BLK)
    return jax.shard_map(
        body,
        mesh=fine,
        in_specs=(
            activations,
            P(),
            P(),
            P(),
            rows_first,
            P(),
            rows_first,
            P(),
            cols_first,
            P(),
            P(),
            P(),
            rows_first,
            P(),
            cols_first,
            P(),
            activations,
        ),
        out_specs=(
            activations,
            activations,
            P(),
            P(),
            rows_first,
            P(),
            rows_first,
            P(),
            cols_first,
            P(),
            P(),
            P(),
            rows_first,
            P(),
            cols_first,
            P(),
        ),
        check_vma=False,
    )
```

```python
import functools

import jax
import jax.numpy as jnp
from jax import lax
from jax.experimental import pallas as pl
from jax.experimental.pallas import tpu as pltpu
from jax.sharding import Mesh
from jax.sharding import PartitionSpec as P

EPS = 1e-05
NEG = -1e30
F32 = jnp.float32
LOW = jnp.bfloat16
BLK = ("zh", "x", "c")
HEAD = ("zl", "y")
PLANE = ("zh", "x", "zl")
SHARERS = ("zl", "zh", "x", "c")
Z = ("zh", "zl")
ALL = ("zh", "x", "c", "zl", "y")
Q_BLOCK = 256
TEAM = 4
PAIRS = 2


def dot(left, right, left_dim, right_dim):
    return lax.dot_general(
        left, right, (((left_dim,), (right_dim,)), ((), ())), preferred_element_type=F32
    )


def center(values):
    centered = values - jnp.mean(values, axis=-1, keepdims=True)
    inv_std = lax.rsqrt(jnp.mean(centered * centered, axis=-1, keepdims=True) + EPS)
    return centered * inv_std, inv_std


def norm_back(grad, normed, inv_std, gain):
    scaled = grad * gain
    first_mean = jnp.mean(scaled, axis=-1, keepdims=True)
    second_mean = jnp.mean(scaled * normed, axis=-1, keepdims=True)
    return inv_std * (scaled - first_mean - normed * second_mean)


def join_pieces(pieces, whole, sems):
    copies = []
    for i, piece in enumerate(pieces):
        size = piece.shape[0]
        copy = pltpu.make_async_copy(piece, whole.at[pl.ds(i * size, size)], sems.at[i])
        copy.start()
        copies.append(copy)
    for copy in copies:
        copy.wait()


def write_parts(block, parts, cols):
    row = 0
    for part in parts:
        part[:, cols] = block[row : row + part.shape[0], :]
        row += part.shape[0]


def summed_parts(own, last_up, last_down, up, down):
    half = own.shape[0] // 2
    top = own[:half].astype(F32) + last_up[...].astype(F32) + down[...].astype(F32)
    low = own[half:].astype(F32) + last_down[...].astype(F32) + up[...].astype(F32)
    return jnp.concatenate([top, low], axis=0)


def slots(rows):
    for member in range(TEAM):
        for micro in range(2):
            yield (member * 2 + micro) * rows, (micro * TEAM + member) * PAIRS


def norm_kernel(x_ref, gain_ref, shift_ref, out_ref):
    normed, _ = center(x_ref[...].astype(F32))
    out_ref[...] = (normed * gain_ref[...] + shift_ref[...]).astype(LOW)


def weights_kernel(core_ref, mine_ref, other_ref, *outs):
    first = core_ref[0] == 0
    rows = mine_ref.shape[2]
    for pair in range(PAIRS):
        mine, other = mine_ref[0, pair], other_ref[0, pair]
        for start, block in ((0, jnp.where(first, mine, other)), (rows, jnp.where(first, other, mine))):
            wide = outs[pair].shape[1]
            outs[pair][start : start + rows, :] = block[:, :wide]
            outs[PAIRS + pair][start : start + rows, :] = block[:, wide:]


def qkv_kernel(rank_ref, gathered, w0, w1, b0, b1, whole, out):
    size = gathered.shape[1]
    for step in range(TEAM):
        whole[step * size : (step + 1) * size, :] = gathered[lax.rem(rank_ref[0] + step, TEAM)]
    x = whole[...]
    rows, size = out.shape[1], b0.shape[1]
    first = (dot(x, w0[...], 1, 0) + b0[...]).astype(LOW)
    second = (dot(x, w1[...], 1, 0) + b1[...]).astype(LOW)
    q_cols = out.shape[2] - 2 * (size - out.shape[2] // 2)
    for row, slot in slots(rows):
        cut = slice(row, row + rows)
        shared = jnp.concatenate([first[cut, q_cols:], second[cut, q_cols:]], axis=1)
        out[slot, :, :q_cols] = first[cut, :q_cols]
        out[slot, :, q_cols:] = shared
        out[slot + 1, :, :q_cols] = second[cut, :q_cols]
        out[slot + 1, :, q_cols:] = shared


def block_probs(seg_ref, q_ref, keys, row, head, head_dim, scale):
    end = row + Q_BLOCK
    queries = q_ref[row:end, head * head_dim : (head + 1) * head_dim]
    scores = dot(queries, keys, 1, 1) * scale
    key_pos = lax.broadcasted_iota(jnp.int32, scores.shape, 1)
    query_pos = lax.broadcasted_iota(jnp.int32, scores.shape, 0) + row
    allowed = (key_pos <= query_pos) & (key_pos >= seg_ref[row:end, :])
    masked = jnp.where(allowed, scores, NEG)
    terms = jnp.exp(masked - jnp.max(masked, axis=1, keepdims=True))
    return queries, terms * (1.0 / jnp.sum(terms, axis=1, keepdims=True))


def attend_kernel(heads, head_dim, seg_ref, qkv_ref, out_ref):
    wide = heads * head_dim
    scale = head_dim**-0.5
    for row in range(0, qkv_ref.shape[0], Q_BLOCK):
        end = row + Q_BLOCK
        keys = qkv_ref[:end, wide : wide + head_dim]
        values = qkv_ref[:end, wide + head_dim :]
        for head in range(heads):
            _, probs = block_probs(seg_ref, qkv_ref, keys, row, head, head_dim, scale)
            out_ref[row:end, head * head_dim : (head + 1) * head_dim] = dot(
                probs.astype(LOW), values, 1, 0
            ).astype(LOW)


def attend_back_kernel(heads, head_dim, seg_ref, qkv_ref, grad_ref, out_ref, dkv_ref):
    wide = heads * head_dim
    scale = head_dim**-0.5
    dkv_ref[...] = jnp.zeros_like(dkv_ref)
    for row in range(0, qkv_ref.shape[0], Q_BLOCK):
        end = row + Q_BLOCK
        keys = qkv_ref[:end, wide : wide + head_dim]
        values = qkv_ref[:end, wide + head_dim :]
        for head in range(heads):
            cols = slice(head * head_dim, (head + 1) * head_dim)
            queries, probs = block_probs(seg_ref, qkv_ref, keys, row, head, head_dim, scale)
            grad = grad_ref[row:end, cols]
            d_probs = dot(grad, values, 1, 1)
            delta = jnp.sum(probs * d_probs, axis=1, keepdims=True)
            d_scores = (probs * (d_probs - delta)).astype(LOW)
            out_ref[row:end, cols] = (dot(d_scores, keys, 1, 0) * scale).astype(LOW)
            dkv_ref[:end, :head_dim] += dot(d_scores, queries, 0, 0)
            dkv_ref[:end, head_dim:] += dot(probs.astype(LOW), grad, 0, 0)
    out_ref[:, wide : wide + head_dim] = (dkv_ref[:, :head_dim] * scale).astype(LOW)
    out_ref[:, wide + head_dim :] = dkv_ref[:, head_dim:].astype(LOW)


def project_kernel(att, w0, w1, whole, *parts):
    rows, wide = att.shape[1], att.shape[2]
    for row, slot in slots(rows):
        for pair in range(PAIRS):
            whole[row : row + rows, pair * wide : (pair + 1) * wide] = att[slot + pair]
    for start in range(0, w0.shape[0], 512):
        cols = slice(start, start + 512)
        block = dot(whole[:, :wide], w0[cols, :], 1, 1) + dot(whole[:, wide:], w1[cols, :], 1, 1)
        write_parts(block.astype(LOW), parts, cols)


def residual_kernel(own, last_up, last_down, up, down, x, bias, gain, shift, residual, top, low):
    total = summed_parts(own, last_up, last_down, up, down)
    total = x[...].astype(F32) + total + bias[...]
    residual[...] = total
    normed, _ = center(total)
    out = (normed * gain[...] + shift[...]).astype(LOW)
    half = top.shape[0]
    top[...] = out[:half]
    low[...] = out[half:]


def hidden_kernel(*refs):
    pieces, cot_pieces = refs[:8], refs[8:16]
    up, down, bias, whole, cot, act, d_pre, sums, sems, cot_sems = refs[16:]

    @pl.when(pl.program_id(0) == 0)
    def _():
        join_pieces(cot_pieces, cot, cot_sems)
        join_pieces(pieces, whole, sems)

    u = dot(whole[...], up[...], 1, 0) + bias[...]
    slope = 2.0 ** 0.5 * jnp.pi ** -0.5
    square = u * u
    bent = jnp.tanh(slope * (u + 0.044715 * (square * u)))
    half = 0.5 * (1.0 + bent)
    act[...] = (u * half).astype(LOW)
    gate = half + 0.5 * u * (1.0 - bent * bent) * (slope * (1.0 + 3.0 * 0.044715 * square))
    grad = (dot(cot[...], down[...], 1, 0) * gate).astype(LOW)
    d_pre[...] = grad
    sums[...] = jnp.sum(grad.astype(F32), axis=0, keepdims=True)


def wide_kernel(x, w, *parts):
    wide = w.shape[2]
    block = dot(x[:, :wide], w[0], 1, 1) + dot(x[:, wide:], w[1], 1, 1)
    write_parts(block.astype(LOW), parts, slice(None))


def wide_grad_kernel(hid, cot, d_pre, act, out):
    cores, pairs, rows, cols = out.shape
    wide = cols // 2
    for half, left, right in ((0, hid, d_pre), (1, cot, act)):
        for pair in range(pairs):
            block = dot(left[...], right[:, pair * wide : (pair + 1) * wide], 0, 0).astype(LOW)
            for core in range(cores):
                out[core, pair, :, half * wide : (half + 1) * wide] = block[
                    core * rows : (core + 1) * rows, :
                ]


def wide_out_kernel(total, up, down):
    wide = up.shape[1]
    up[...] = total[:, :wide].astype(F32)
    down[...] = total[:, wide:].astype(F32).T


def residual_back_kernel(
    own, last_up, last_down, up, down, cot, residual, gain, d_res, top, low, sums
):
    d_hidden = summed_parts(own, last_up, last_down, up, down)
    normed, inv_std = center(residual[...])
    cot_float = cot[...].astype(F32)
    total = cot_float + norm_back(d_hidden, normed, inv_std, gain[...])
    d_res[...] = total
    half = top.shape[0]
    top[...] = total[:half].astype(LOW)
    low[...] = total[half:].astype(LOW)
    rows = (total, d_hidden * normed, d_hidden, cot_float)
    for i, values in enumerate(rows):
        sums[i : i + 1, :] = jnp.sum(values, axis=0, keepdims=True)


def d_att_kernel(*refs):
    pieces, (w0, w1, whole, out, sems) = refs[:8], refs[8:]
    join_pieces(pieces, whole, sems)
    rows = out.shape[1]
    for pair, weight in enumerate((w0, w1)):
        grads = dot(whole[...], weight[...], 1, 0).astype(LOW)
        for row, slot in slots(rows):
            out[slot + pair] = grads[row : row + rows, :]


def d_in_kernel(grads, w0_far, w1_far, normed, whole, sums, totals, *more):
    *parts, w0, w1, sems = more
    copies = [
        pltpu.make_async_copy(far, near, sems.at[i])
        for i, (far, near) in enumerate(((w0_far, w0), (w1_far, w1)))
    ]
    for copy in copies:
        copy.start()
    rows, wide = grads.shape[1], w0.shape[1]
    q_cols = grads.shape[2] // 2
    key_cols = wide - q_cols
    for row, slot in slots(rows):
        cut = slice(row, row + rows)
        for pair in range(PAIRS):
            start = pair * wide
            from_col = q_cols + pair * key_cols
            shared = grads[slot, :, from_col : from_col + key_cols].astype(F32) + grads[
                slot + 1, :, from_col : from_col + key_cols
            ].astype(F32)
            whole[cut, start : start + q_cols] = grads[slot + pair, :, :q_cols]
            whole[cut, start + q_cols : start + wide] = shared.astype(LOW)
    totals[...] = jnp.sum(whole[...].astype(F32), axis=0, keepdims=True)
    for copy in copies:
        copy.wait()
    for start in range(0, w0.shape[0], 512):
        cols = slice(start, start + 512)
        block = dot(whole[:, :wide], w0[cols, :], 1, 1) + dot(whole[:, wide:], w1[cols, :], 1, 1)
        write_parts(block.astype(LOW), parts, cols)
        sums[0:1, cols] = jnp.sum(block * normed[:, cols].astype(F32), axis=0, keepdims=True)
        sums[1:2, cols] = jnp.sum(block, axis=0, keepdims=True)


def grad_rows_kernel(core_ref, left0, left1, right, *refs):
    *extra, out = refs
    wide, rows = right.shape[1] // PAIRS, left0.shape[1]
    left = jnp.concatenate([left0[...], left1[...]], axis=1)
    for pair in range(PAIRS):
        both = dot(left, right[:, pair * wide : (pair + 1) * wide], 0, 0)
        for i in range(2):
            block = both[i * rows : (i + 1) * rows, :]
            if extra:
                block = block + extra[0][0, i, pair].astype(F32)
            out[0, i, pair, :, :wide] = block.astype(LOW)
            if len(extra) > 1:
                out[0, i, pair, :, wide:] = extra[1][0, i, pair]


def output_kernel(own, last_up, last_down, up, down, residual, bias, out):
    mlp = summed_parts(own, last_up, last_down, up, down)
    out[...] = (residual[...] + mlp + bias[...]).astype(LOW)


def input_kernel(own, last_up, last_down, up, down, x, d_res, gain, out):
    d_in = summed_parts(own, last_up, last_down, up, down)
    normed, inv_std = center(x[...].astype(F32))
    out[...] = d_res[...] + norm_back(d_in, normed, inv_std, gain[...])


VECTOR_ROWS = dict(
    ln1_gain=(0, 16),
    ln1_bias=(16, 16),
    b_query=(32, 16),
    b_out=(48, 16),
    ln2_gain=(64, 16),
    ln2_bias=(80, 16),
    b_fc2=(96, 16),
    b_fc=(112, 64),
    b_value=(176, 1),
)
VECTOR_TOTAL = 184


def vectors_kernel(rank_ref, ln1_sums, totals, ln2_sums, fc_sums, gain, shift, out):
    out[...] = jnp.zeros_like(out)

    def put(name, offset, values):
        row = VECTOR_ROWS[name][0] + offset
        for i in range(values.shape[1] // 128):
            out[row + i : row + i + 1, :] = values[:, i * 128 : (i + 1) * 128]

    def put_mine(name, values):
        size = values.shape[1] // PAIRS
        for pair in range(PAIRS):
            for member in range(TEAM):
                block = values[:, pair * size : (pair + 1) * size]
                block = jnp.where(rank_ref[0] == member, block, 0.0)
                put(name, (pair * TEAM + member) * size // 128, block)

    put("ln1_gain", 0, (ln1_sums[0:1, :] - shift[...] * ln1_sums[1:2, :]) / gain[...])
    put("ln1_bias", 0, ln1_sums[1:2, :])
    wide = totals.shape[1] // PAIRS
    q_cols = wide * 2 // 3
    put_mine("b_query", jnp.concatenate([totals[:, :q_cols], totals[:, wide : wide + q_cols]], axis=1))
    put("b_value", 0, totals[:, wide + q_cols :])
    for i, name in enumerate(("b_out", "ln2_gain", "ln2_bias", "b_fc2")):
        put(name, 0, ln2_sums[i : i + 1, :])
    put_mine("b_fc", fc_sums[...])


def plane_sum_kernel(blocks, d_query, kv_rows, d_out):
    total = jnp.sum(blocks[...].astype(F32), axis=0)
    cut = d_query.shape[1]
    edge = cut + kv_rows.shape[0]
    d_query[...] = total[:, :cut]
    kv_rows[...] = total[:, cut:edge].T.astype(LOW)
    d_out[...] = total[:, edge:].T


def shaped(shape, kind=LOW):
    return jax.ShapeDtypeStruct(shape, kind)


ALONE = ("attend_back", "small_grads")


def run(kernel, name, outs, args, flops=0, vmem=None, scalars=0, **more):
    vmem = vmem or (58 if name in ALONE else 20)
    size = sum(a.size * a.dtype.itemsize for a in args)
    size += sum(o.size * o.dtype.itemsize for o in outs)
    if scalars and "grid" not in more and "grid_spec" not in more:
        more["in_specs"] = [pl.BlockSpec(memory_space=pltpu.SMEM)] * scalars + [
            pl.BlockSpec(memory_space=pltpu.VMEM)
        ] * (len(args) - scalars)
    result = pl.pallas_call(
        kernel,
        out_shape=tuple(outs),
        compiler_params=pltpu.CompilerParams(vmem_limit_bytes=vmem * 2**20),
        cost_estimate=pl.CostEstimate(flops=flops, bytes_accessed=size, transcendentals=0),
        name=name,
        **more,
    )(*args)
    return result


def part_shapes(own, width):
    return [shaped((own, width))] + [shaped((own // 2, width))] * 6


def whole_block(array):
    return pl.BlockSpec(array.shape, lambda *_: (0,) * array.ndim)


def add_low(left, right):
    return (left.astype(F32) + right.astype(F32)).astype(LOW)


def after(values, *earlier):
    return lax.optimization_barrier((values, earlier))[0]


def shift(values, axis, step):
    return lax.ppermute(values, axis, [(i, (i + step) % TEAM) for i in range(TEAM)])


def other_core(values):
    return lax.ppermute(values, "c", [(0, 1), (1, 0)])


def ring_pieces(halves, axis, *meanwhile):
    top, low = halves
    ahead_top = shift(top, axis, -1)
    behind_low = shift(low, axis, 1)
    ahead_low = shift(low, axis, -1)
    behind_top = shift(top, axis, 1)
    sent_top, sent_low = ahead_top, behind_low
    if meanwhile:
        sent_top, sent_low = after((ahead_top, behind_low), *meanwhile)
    far_top = shift(sent_top, axis, -1)
    far_low = shift(sent_low, axis, 1)
    return top, low, ahead_top, ahead_low, far_top, far_low, behind_top, behind_low


def ring_sum(parts, axis):
    own, ahead_top, ahead_low, far_top, far_low, behind_top, behind_low = parts
    up = shift(far_top, axis, 1)
    down = shift(far_low, axis, -1)
    up_near = shift(ahead_low, axis, 1)
    down_near = shift(behind_top, axis, -1)
    last_up = shift(add_low(ahead_top, up), axis, 1)
    last_down = shift(add_low(behind_low, down), axis, -1)
    return own, last_up, last_down, up_near, down_near


def plane_scatter(blocks):
    return lax.all_to_all(blocks.reshape(16, *blocks.shape[3:]), PLANE, 0, 0, tiled=True)


def sum_over(values, axis):
    size = lax.axis_size(axis)
    found = [values] + [
        lax.ppermute(values, axis, [(i, i ^ bits) for i in range(size)]) for bits in range(1, size)
    ]
    if size == 2:
        return found[0] + found[1]
    return (found[0] + found[1]) + (found[2] + found[3])


def grad_rows(name, core, left, right, *extra):
    rows = left.shape[1] // 16
    wide = right.shape[1] // PAIRS
    cols = wide + sum(more.shape[-1] for more in extra[1:])

    def place(cols):
        return pl.BlockSpec(
            (1, 2, PAIRS, rows, cols), lambda i, core: (i // 2, i % 2, 0, 0, 0)
        )

    (result,) = run(
        grad_rows_kernel,
        name,
        [shaped((2, 4, PAIRS, rows, cols))],
        [core, left, left, right, *extra],
        flops=left.size * right.shape[1],
        grid_spec=pltpu.PrefetchScalarGridSpec(
            num_scalar_prefetch=1,
            grid=(4,),
            in_specs=[
                pl.BlockSpec((left.shape[0], rows), lambda i, core: (0, 4 * i + core[0])),
                pl.BlockSpec((left.shape[0], rows), lambda i, core: (0, 4 * i + 2 + core[0])),
                pl.BlockSpec(right.shape, lambda i, core: (0, 0)),
            ]
            + [place(more.shape[-1]) for more in extra],
            out_specs=[place(cols)],
        ),
    )
    return result


def body(
    tokens,
    segment_ids,
    ln1_gain,
    ln1_bias,
    w_query,
    b_query,
    w_kv,
    b_value,
    w_out,
    b_out,
    ln2_gain,
    ln2_bias,
    w_fc,
    b_fc,
    w_fc2,
    b_fc2,
    cotangent,
):
    micro, _, rows, width = tokens.shape
    head_dim = b_value.shape[0]
    q_cols = w_query.shape[1]
    heads = q_cols // head_dim
    hidden = w_fc.shape[1]
    wide = q_cols + head_dim
    own = micro * rows
    team_rows = TEAM * own
    rank = lax.axis_index("y")
    core_id = lax.axis_index("c")
    core = core_id.reshape(1)

    def row_of(vector):
        return vector.reshape(1, -1)

    def my_columns(vector):
        blocks = vector.reshape(PAIRS, TEAM, -1)
        return lax.dynamic_index_in_dim(blocks, rank, 1, keepdims=False)

    x_own = tokens.reshape(own, width)
    (norm_own,) = run(
        norm_kernel, "norm", [shaped((own, width))], [x_own, row_of(ln1_gain), row_of(ln1_bias)]
    )
    kv_spread = jnp.broadcast_to(w_kv.T[None], (TEAM,) + w_kv.T.shape)
    kv_block = lax.all_to_all(kv_spread, "y", 0, 0, tiled=True).reshape(-1, w_kv.shape[0]).T
    gathered = lax.all_gather(norm_own, "y")

    small = jnp.concatenate([w_query, kv_block, w_out.T], axis=1)
    spread = jnp.broadcast_to(small[None], (16,) + small.shape)
    small_mine = lax.all_to_all(spread, PLANE, 0, 0, tiled=True).reshape(8, PAIRS, *small.shape)
    cot_own = cotangent.reshape(own, width)
    half_rows = own // 2
    cot_halves = after((cot_own[:half_rows], cot_own[half_rows:]), gathered)
    cot_pieces = ring_pieces(cot_halves, "y")
    small_mine = after(small_mine, cot_pieces)
    block = pl.BlockSpec((1, PAIRS) + small.shape, lambda i, core: (i, 0, 0, 0))
    w_qkv0, w_qkv1, w_out0, w_out1 = run(
        weights_kernel,
        "weights",
        [shaped((width, wide))] * PAIRS + [shaped((width, q_cols))] * PAIRS,
        [core, small_mine, other_core(small_mine)],
        grid_spec=pltpu.PrefetchScalarGridSpec(
            num_scalar_prefetch=1,
            grid=(8,),
            in_specs=[block, block],
            out_specs=[
                pl.BlockSpec((2 * small.shape[0], cols), lambda i, core: (i, 0))
                for cols in (wide, wide, q_cols, q_cols)
            ],
        ),
    )
    packed = jnp.concatenate([w_fc, w_fc2.T], axis=1)
    w_wide = lax.all_gather(after(packed, small_mine, gathered), SHARERS, axis=0, tiled=True)

    bias_q = my_columns(b_query)
    bias0 = jnp.concatenate([bias_q[0], jnp.zeros((head_dim,), F32)])
    bias1 = jnp.concatenate([bias_q[1], b_value])
    normed_in, qkv_out = run(
        qkv_kernel,
        "qkv",
        [shaped((team_rows, width)), shaped((16, rows, 2 * q_cols))],
        [rank.reshape(1), gathered, w_qkv0, w_qkv1, row_of(bias0), row_of(bias1)],
        flops=4 * team_rows * width * wide,
        scalars=1,
    )
    qkv = lax.all_to_all(qkv_out, BLK, 0, 0, tiled=True)
    qkv = qkv.reshape(16 * rows, 2 * q_cols)

    seq_rank = lax.axis_index("zl") * TEAM + (rank + lax.axis_index("x")) % TEAM
    segments = lax.dynamic_slice(
        segment_ids,
        (lax.axis_index("zh"), seq_rank, 0),
        (1, 1, segment_ids.shape[2]),
    ).reshape(-1, 1)
    length = qkv.shape[0]
    (attended,) = run(
        functools.partial(attend_kernel, heads, head_dim),
        "attend",
        [shaped((length, q_cols))],
        [segments, qkv],
        flops=3 * length * length * q_cols,
    )
    attended = lax.all_to_all(attended.reshape(16, rows, q_cols), BLK, 0, 0, tiled=True)

    attention, *parts = run(
        project_kernel,
        "project",
        [shaped((team_rows, 2 * q_cols))] + part_shapes(own, width),
        [attended, w_out0, w_out1],
        flops=4 * team_rows * width * q_cols,
    )
    residual, *hidden_own = run(
        residual_kernel,
        "residual",
        [shaped((own, width), F32)] + [shaped((half_rows, width))] * 2,
        [*ring_sum(parts, "y"), x_own, row_of(b_out), row_of(ln2_gain), row_of(ln2_bias)],
    )
    hidden_pieces = ring_pieces(hidden_own, "y")

    step = 512
    steps = PAIRS * hidden // step
    bias_fc = my_columns(b_fc).reshape(1, -1)
    piece_specs = [pl.BlockSpec(memory_space=pl.ANY)] * 16
    col_block = pl.BlockSpec((team_rows, step), lambda i: (0, i))
    row_block = pl.BlockSpec((1, step), lambda i: (0, i))
    per = hidden // step
    hidden_in, cot, act, d_pre, fc_sums = run(
        hidden_kernel,
        "hidden",
        [shaped((team_rows, width))] * 2
        + [shaped((team_rows, PAIRS * hidden))] * 2
        + [shaped((1, PAIRS * hidden), F32)],
        [*hidden_pieces, *cot_pieces, w_wide, w_wide, bias_fc],
        flops=8 * team_rows * width * hidden,
        grid=(steps,),
        in_specs=piece_specs
        + [
            pl.BlockSpec((width, step), lambda i: (i // per, i % per)),
            pl.BlockSpec((width, step), lambda i: (i // per, per + i % per)),
            row_block,
        ],
        out_specs=[pl.BlockSpec((team_rows, width), lambda i: (0, 0))] * 2
        + [col_block, col_block, row_block],
        scratch_shapes=[pltpu.SemaphoreType.DMA((8,))] * 2,
        vmem=40,
    )
    column = step = 512
    col_block = pl.BlockSpec((team_rows, step), lambda i: (0, i))
    w_pair = w_wide.reshape(PAIRS, width, 2 * hidden)


    def wide_product(name, values, half):
        outs = part_shapes(own, width)
        return run(
            wide_kernel,
            name,
            outs,
            [values, w_pair],
            flops=4 * team_rows * width * hidden,
            vmem=45,
            grid=(width // column,),
            in_specs=[
                whole_block(values),
                pl.BlockSpec((PAIRS, column, hidden), lambda i: (0, i, half)),
            ],
            out_specs=[pl.BlockSpec((o.shape[0], column), lambda i: (0, i)) for o in outs],
        )

    (g_wide,) = run(
        wide_grad_kernel,
        "wide_grad",
        [shaped((8, 4, width // 16, 2 * hidden))],
        [hidden_in, cot, d_pre, act],
        flops=8 * team_rows * width * hidden,
        vmem=40,
        grid=(width // step,),
        in_specs=[col_block, col_block, whole_block(d_pre), whole_block(act)],
        out_specs=[
            pl.BlockSpec((4, PAIRS, width // 16, 2 * hidden), lambda i: (i % 2, i // 2, 0, 0))
        ],
    )
    g_sum = lax.psum_scatter(
        g_wide.reshape(-1, 2 * hidden), ("x", "c"), scatter_dimension=0, tiled=True
    )
    g_sum = lax.psum_scatter(g_sum, Z, scatter_dimension=0, tiled=True)
    d_up, d_down = run(
        wide_out_kernel,
        "wide_out",
        [shaped(w_fc.shape, F32), shaped(w_fc2.shape, F32)],
        [g_sum],
    )
    d_hidden_parts = wide_product("d_hidden", after(d_pre, g_wide), 0)

    d_res, *d_res_own, ln2_sums = run(
        residual_back_kernel,
        "residual_back",
        [shaped((own, width), F32)]
        + [shaped((half_rows, width))] * 2
        + [shaped((4, width), F32)],
        [*ring_sum(d_hidden_parts, "y"), cot_own, residual, row_of(ln2_gain)],
    )
    mlp_parts = wide_product("mlp", after(act, d_res_own[0]), 1)
    d_res_low, d_att = run(
        d_att_kernel,
        "d_att",
        [shaped((team_rows, width)), shaped((16, rows, q_cols))],
        [*ring_pieces(d_res_own, "y", mlp_parts[0]), w_out0, w_out1],
        flops=4 * team_rows * width * q_cols,
        in_specs=[pl.BlockSpec(memory_space=pl.ANY)] * 8
        + [pl.BlockSpec(memory_space=pltpu.VMEM)] * 2,
        scratch_shapes=[pltpu.SemaphoreType.DMA((8,))],
    )
    d_att_seq = lax.all_to_all(d_att, BLK, 0, 0, tiled=True).reshape(length, q_cols)
    g_out_sent = grad_rows("g_out_sent", 1 - core, d_res_low, attention)
    mlp_parts = after(mlp_parts, d_att)

    (d_qkv_seq,) = run(
        functools.partial(attend_back_kernel, heads, head_dim),
        "attend_back",
        [shaped((length, 2 * q_cols))],
        [segments, qkv, after(d_att_seq, g_out_sent)],
        flops=6 * length * length * q_cols,
        scratch_shapes=[pltpu.VMEM((length, 2 * head_dim), F32)],
    )
    g_out = grad_rows(
        "g_out_kept", core, after(d_res_low, d_qkv_seq), attention, other_core(g_out_sent)
    )
    mlp_sums = ring_sum(mlp_parts, "y")
    (output,) = run(
        output_kernel, "output", [shaped((own, width))], [*mlp_sums, residual, row_of(b_fc2)]
    )
    d_qkv_seq = lax.all_to_all(d_qkv_seq.reshape(16, rows, 2 * q_cols), BLK, 0, 0, tiled=True)
    d_qkv_seq = after(d_qkv_seq, g_out, mlp_sums)
    d_qkv, ln1_sums, totals, *d_in_parts = run(
        d_in_kernel,
        "d_in",
        [shaped((team_rows, PAIRS * wide)), shaped((2, width), F32), shaped((1, PAIRS * wide), F32)]
        + part_shapes(own, width),
        [d_qkv_seq, w_qkv0, w_qkv1, normed_in],
        flops=4 * team_rows * width * wide,
        in_specs=[
            pl.BlockSpec(memory_space=pltpu.VMEM),
            pl.BlockSpec(memory_space=pl.ANY),
            pl.BlockSpec(memory_space=pl.ANY),
            pl.BlockSpec(memory_space=pltpu.VMEM),
        ],
        scratch_shapes=[pltpu.VMEM((width, wide), LOW)] * 2 + [pltpu.SemaphoreType.DMA((2,))],
    )
    (flat,) = run(
        vectors_kernel,
        "vectors",
        [shaped((VECTOR_TOTAL, 128), F32)],
        [
            rank.reshape(1),
            ln1_sums,
            totals,
            ln2_sums,
            fc_sums,
            row_of(ln1_gain),
            row_of(ln1_bias),
        ],
        scalars=1,
    )
    g_qkv_sent = grad_rows("g_qkv_sent", 1 - core, normed_in, d_qkv)
    small = grad_rows("small_grads", core, normed_in, d_qkv, other_core(g_qkv_sent), g_out)
    small_here = plane_scatter(small)
    d_in_sums = ring_sum(after(d_in_parts, small), "y")
    flat = sum_over(sum_over(after(flat, d_in_sums[3]), "y"), "c")
    (input_grad,) = run(
        input_kernel,
        "input",
        [shaped((own, width), F32)],
        [*d_in_sums, x_own, d_res, row_of(ln1_gain)],
    )

    rows_here = width // 16
    d_wq, kv_rows, d_wout = run(
        plane_sum_kernel,
        "plane_sum",
        [
            shaped((rows_here, q_cols), F32),
            shaped((head_dim, rows_here)),
            shaped((q_cols, rows_here), F32),
        ],
        [after(small_here, input_grad, output)],
    )
    kv_rows = lax.all_to_all(kv_rows.reshape(TEAM, -1, rows_here), "y", 0, 0, tiled=True)
    d_wkv = jnp.sum(after(kv_rows, d_up, d_down).astype(F32), axis=0).T
    flat = sum_over(after(sum_over(flat, Z), d_wq), "x")
    vector = {
        name: flat[start : start + size].reshape(-1) for name, (start, size) in VECTOR_ROWS.items()
    }
    return (
        output.reshape(tokens.shape),
        input_grad.reshape(tokens.shape),
        vector["ln1_gain"],
        vector["ln1_bias"],
        d_wq,
        vector["b_query"],
        d_wkv,
        vector["b_value"],
        d_wout,
        vector["b_out"],
        vector["ln2_gain"],
        vector["ln2_bias"],
        d_up,
        vector["b_fc"],
        d_down,
        vector["b_fc2"],
    )


def solution(mesh):
    fine = Mesh(mesh.devices.reshape(2, 4, 2, 2, 4), ALL)
    activations = P(None, HEAD, BLK, None)
    rows_first, cols_first = P(BLK, HEAD), P(HEAD, BLK)
    return jax.shard_map(
        body,
        mesh=fine,
        in_specs=(
            activations,
            P(),
            P(),
            P(),
            rows_first,
            P(),
            rows_first,
            P(),
            cols_first,
            P(),
            P(),
            P(),
            rows_first,
            P(),
            cols_first,
            P(),
            activations,
        ),
        out_specs=(
            activations,
            activations,
            P(),
            P(),
            rows_first,
            P(),
            rows_first,
            P(),
            cols_first,
            P(),
            P(),
            P(),
            rows_first,
            P(),
            cols_first,
            P(),
        ),
        check_vma=False,
    )
```

```python
import functools

import jax
import jax.numpy as jnp
from jax import lax
from jax.experimental import pallas as pl
from jax.experimental.pallas import tpu as pltpu
from jax.sharding import Mesh
from jax.sharding import PartitionSpec as P

EPS = 1e-05
NEG = -1e30
F32 = jnp.float32
LOW = jnp.bfloat16
BLK = ("zh", "x", "c")
HEAD = ("zl", "y")
PLANE = ("zh", "x", "zl")
SHARERS = ("zl", "zh", "x", "c")
Z = ("zh", "zl")
ALL = ("zh", "x", "c", "zl", "y")
Q_BLOCK = 256
TEAM = 4
PAIRS = 2


def dot(left, right, left_dim, right_dim):
    return lax.dot_general(
        left, right, (((left_dim,), (right_dim,)), ((), ())), preferred_element_type=F32
    )


def center(values):
    centered = values - jnp.mean(values, axis=-1, keepdims=True)
    inv_std = lax.rsqrt(jnp.mean(centered * centered, axis=-1, keepdims=True) + EPS)
    return centered * inv_std, inv_std


def norm_back(grad, normed, inv_std, gain):
    scaled = grad * gain
    first_mean = jnp.mean(scaled, axis=-1, keepdims=True)
    second_mean = jnp.mean(scaled * normed, axis=-1, keepdims=True)
    return inv_std * (scaled - first_mean - normed * second_mean)


def join_pieces(pieces, whole, sems):
    copies = []
    for i, piece in enumerate(pieces):
        size = piece.shape[0]
        copy = pltpu.make_async_copy(piece, whole.at[pl.ds(i * size, size)], sems.at[i])
        copy.start()
        copies.append(copy)
    for copy in copies:
        copy.wait()


def write_parts(block, parts, cols):
    row = 0
    for part in parts:
        part[:, cols] = block[row : row + part.shape[0], :]
        row += part.shape[0]


def summed_parts(own, last_up, last_down, up, down):
    half = own.shape[0] // 2
    top = own[:half].astype(F32) + last_up[...].astype(F32) + down[...].astype(F32)
    low = own[half:].astype(F32) + last_down[...].astype(F32) + up[...].astype(F32)
    return jnp.concatenate([top, low], axis=0)


def slots(rows):
    for member in range(TEAM):
        for micro in range(2):
            yield (member * 2 + micro) * rows, (micro * TEAM + member) * PAIRS


def norm_kernel(x_ref, gain_ref, shift_ref, out_ref):
    normed, _ = center(x_ref[...].astype(F32))
    out_ref[...] = (normed * gain_ref[...] + shift_ref[...]).astype(LOW)


def spread_kernel(query, shared, out_rows, spread):
    shared_cols = shared[...].reshape(-1, shared.shape[-1]).T
    block = jnp.concatenate([query[...], shared_cols, out_rows[...].T], axis=1)
    for i in range(spread.shape[0]):
        spread[i] = block


def weights_kernel(core_ref, mine_ref, other_ref, *outs):
    first = core_ref[0] == 0
    rows = mine_ref.shape[2]
    for pair in range(PAIRS):
        mine, other = mine_ref[0, pair], other_ref[0, pair]
        for start, block in ((0, jnp.where(first, mine, other)), (rows, jnp.where(first, other, mine))):
            wide = outs[pair].shape[1]
            outs[pair][start : start + rows, :] = block[:, :wide]
            outs[PAIRS + pair][start : start + rows, :] = block[:, wide:]


def qkv_kernel(rank_ref, gathered, w0, w1, b0, b1, whole, out):
    size = gathered.shape[1]
    for step in range(TEAM):
        whole[step * size : (step + 1) * size, :] = gathered[lax.rem(rank_ref[0] + step, TEAM)]
    x = whole[...]
    rows, size = out.shape[1], b0.shape[1]
    first = (dot(x, w0[...], 1, 0) + b0[...]).astype(LOW)
    second = (dot(x, w1[...], 1, 0) + b1[...]).astype(LOW)
    q_cols = out.shape[2] - 2 * (size - out.shape[2] // 2)
    for row, slot in slots(rows):
        cut = slice(row, row + rows)
        shared = jnp.concatenate([first[cut, q_cols:], second[cut, q_cols:]], axis=1)
        out[slot, :, :q_cols] = first[cut, :q_cols]
        out[slot, :, q_cols:] = shared
        out[slot + 1, :, :q_cols] = second[cut, :q_cols]
        out[slot + 1, :, q_cols:] = shared


def block_probs(seg_ref, q_ref, keys, row, head, head_dim, scale):
    end = row + Q_BLOCK
    queries = q_ref[row:end, head * head_dim : (head + 1) * head_dim]
    scores = dot(queries, keys, 1, 1) * scale
    key_pos = lax.broadcasted_iota(jnp.int32, scores.shape, 1)
    query_pos = lax.broadcasted_iota(jnp.int32, scores.shape, 0) + row
    allowed = (key_pos <= query_pos) & (key_pos >= seg_ref[row:end, :])
    masked = jnp.where(allowed, scores, NEG)
    terms = jnp.exp(masked - jnp.max(masked, axis=1, keepdims=True))
    return queries, terms * (1.0 / jnp.sum(terms, axis=1, keepdims=True))


def attend_kernel(heads, head_dim, seg_ref, qkv_ref, out_ref):
    wide = heads * head_dim
    scale = head_dim**-0.5
    for row in range(0, qkv_ref.shape[0], Q_BLOCK):
        end = row + Q_BLOCK
        keys = qkv_ref[:end, wide : wide + head_dim]
        values = qkv_ref[:end, wide + head_dim :]
        for head in range(heads):
            _, probs = block_probs(seg_ref, qkv_ref, keys, row, head, head_dim, scale)
            out_ref[row:end, head * head_dim : (head + 1) * head_dim] = dot(
                probs.astype(LOW), values, 1, 0
            ).astype(LOW)


def attend_back_kernel(heads, head_dim, seg_ref, qkv_ref, grad_ref, out_ref, dkv_ref):
    wide = heads * head_dim
    scale = head_dim**-0.5
    dkv_ref[...] = jnp.zeros_like(dkv_ref)
    for row in range(0, qkv_ref.shape[0], Q_BLOCK):
        end = row + Q_BLOCK
        keys = qkv_ref[:end, wide : wide + head_dim]
        values = qkv_ref[:end, wide + head_dim :]
        for head in range(heads):
            cols = slice(head * head_dim, (head + 1) * head_dim)
            queries, probs = block_probs(seg_ref, qkv_ref, keys, row, head, head_dim, scale)
            grad = grad_ref[row:end, cols]
            d_probs = dot(grad, values, 1, 1)
            delta = jnp.sum(probs * d_probs, axis=1, keepdims=True)
            d_scores = (probs * (d_probs - delta)).astype(LOW)
            out_ref[row:end, cols] = (dot(d_scores, keys, 1, 0) * scale).astype(LOW)
            dkv_ref[:end, :head_dim] += dot(d_scores, queries, 0, 0)
            dkv_ref[:end, head_dim:] += dot(probs.astype(LOW), grad, 0, 0)
    out_ref[:, wide : wide + head_dim] = (dkv_ref[:, :head_dim] * scale).astype(LOW)
    out_ref[:, wide + head_dim :] = dkv_ref[:, head_dim:].astype(LOW)


def project_kernel(att, w0, w1, whole, *parts):
    rows, wide = att.shape[1], att.shape[2]
    for row, slot in slots(rows):
        for pair in range(PAIRS):
            whole[row : row + rows, pair * wide : (pair + 1) * wide] = att[slot + pair]
    for start in range(0, w0.shape[0], 512):
        cols = slice(start, start + 512)
        block = dot(whole[:, :wide], w0[cols, :], 1, 1) + dot(whole[:, wide:], w1[cols, :], 1, 1)
        write_parts(block.astype(LOW), parts, cols)


def residual_kernel(own, last_up, last_down, up, down, x, bias, gain, shift, residual, top, low):
    total = summed_parts(own, last_up, last_down, up, down)
    total = x[...].astype(F32) + total + bias[...]
    residual[...] = total
    normed, _ = center(total)
    out = (normed * gain[...] + shift[...]).astype(LOW)
    half = top.shape[0]
    top[...] = out[:half]
    low[...] = out[half:]


def hidden_kernel(*refs):
    pieces, cot_pieces = refs[:8], refs[8:16]
    up, down, bias, whole, cot, act, d_pre, sums, sems, cot_sems = refs[16:]

    @pl.when(pl.program_id(0) == 0)
    def _():
        join_pieces(cot_pieces, cot, cot_sems)
        join_pieces(pieces, whole, sems)

    u = dot(whole[...], up[...], 1, 0) + bias[...]
    slope = 2.0 ** 0.5 * jnp.pi ** -0.5
    square = u * u
    bent = jnp.tanh(slope * (u + 0.044715 * (square * u)))
    half = 0.5 * (1.0 + bent)
    act[...] = (u * half).astype(LOW)
    gate = half + 0.5 * u * (1.0 - bent * bent) * (slope * (1.0 + 3.0 * 0.044715 * square))
    grad = (dot(cot[...], down[...], 1, 0) * gate).astype(LOW)
    d_pre[...] = grad
    sums[...] = jnp.sum(grad.astype(F32), axis=0, keepdims=True)


def wide_kernel(x, w, *parts):
    wide = w.shape[2]
    block = dot(x[:, :wide], w[0], 1, 1) + dot(x[:, wide:], w[1], 1, 1)
    write_parts(block.astype(LOW), parts, slice(None))


def wide_grad_kernel(hid, cot, d_pre, act, out):
    cores, pairs, rows, cols = out.shape
    wide = cols // 2
    for half, left, right in ((0, hid, d_pre), (1, cot, act)):
        for pair in range(pairs):
            block = dot(left[...], right[:, pair * wide : (pair + 1) * wide], 0, 0).astype(LOW)
            for core in range(cores):
                out[core, pair, :, half * wide : (half + 1) * wide] = block[
                    core * rows : (core + 1) * rows, :
                ]


def wide_out_kernel(total, up, down):
    wide = up.shape[1]
    up[...] = total[:, :wide].astype(F32)
    down[...] = total[:, wide:].astype(F32).T


def residual_back_kernel(
    own, last_up, last_down, up, down, cot, residual, gain, d_res, top, low, sums
):
    d_hidden = summed_parts(own, last_up, last_down, up, down)
    normed, inv_std = center(residual[...])
    cot_float = cot[...].astype(F32)
    total = cot_float + norm_back(d_hidden, normed, inv_std, gain[...])
    d_res[...] = total
    half = top.shape[0]
    top[...] = total[:half].astype(LOW)
    low[...] = total[half:].astype(LOW)
    rows = (total, d_hidden * normed, d_hidden, cot_float)
    for i, values in enumerate(rows):
        sums[i : i + 1, :] = jnp.sum(values, axis=0, keepdims=True)


def d_att_kernel(*refs):
    pieces, (w0, w1, whole, out, sems) = refs[:8], refs[8:]
    join_pieces(pieces, whole, sems)
    rows = out.shape[1]
    for pair, weight in enumerate((w0, w1)):
        grads = dot(whole[...], weight[...], 1, 0).astype(LOW)
        for row, slot in slots(rows):
            out[slot + pair] = grads[row : row + rows, :]


def d_in_kernel(grads, w0_far, w1_far, normed, whole, sums, totals, *more):
    *parts, w0, w1, sems = more
    copies = [
        pltpu.make_async_copy(far, near, sems.at[i])
        for i, (far, near) in enumerate(((w0_far, w0), (w1_far, w1)))
    ]
    for copy in copies:
        copy.start()
    rows, wide = grads.shape[1], w0.shape[1]
    q_cols = grads.shape[2] // 2
    key_cols = wide - q_cols
    for row, slot in slots(rows):
        cut = slice(row, row + rows)
        for pair in range(PAIRS):
            start = pair * wide
            from_col = q_cols + pair * key_cols
            shared = grads[slot, :, from_col : from_col + key_cols].astype(F32) + grads[
                slot + 1, :, from_col : from_col + key_cols
            ].astype(F32)
            whole[cut, start : start + q_cols] = grads[slot + pair, :, :q_cols]
            whole[cut, start + q_cols : start + wide] = shared.astype(LOW)
    totals[...] = jnp.sum(whole[...].astype(F32), axis=0, keepdims=True)
    for copy in copies:
        copy.wait()
    for start in range(0, w0.shape[0], 512):
        cols = slice(start, start + 512)
        block = dot(whole[:, :wide], w0[cols, :], 1, 1) + dot(whole[:, wide:], w1[cols, :], 1, 1)
        write_parts(block.astype(LOW), parts, cols)
        sums[0:1, cols] = jnp.sum(block * normed[:, cols].astype(F32), axis=0, keepdims=True)
        sums[1:2, cols] = jnp.sum(block, axis=0, keepdims=True)


def grad_rows_kernel(core_ref, left0, left1, right, *refs):
    *extra, out = refs
    wide, rows = right.shape[1] // PAIRS, left0.shape[1]
    left = jnp.concatenate([left0[...], left1[...]], axis=1)
    for pair in range(PAIRS):
        both = dot(left, right[:, pair * wide : (pair + 1) * wide], 0, 0)
        for i in range(2):
            block = both[i * rows : (i + 1) * rows, :]
            if extra:
                block = block + extra[0][0, i, pair].astype(F32)
            out[0, i, pair, :, :wide] = block.astype(LOW)
            if len(extra) > 1:
                out[0, i, pair, :, wide:] = extra[1][0, i, pair]


def output_kernel(own, last_up, last_down, up, down, residual, bias, out):
    mlp = summed_parts(own, last_up, last_down, up, down)
    out[...] = (residual[...] + mlp + bias[...]).astype(LOW)


def input_kernel(own, last_up, last_down, up, down, x, d_res, gain, out):
    d_in = summed_parts(own, last_up, last_down, up, down)
    normed, inv_std = center(x[...].astype(F32))
    out[...] = d_res[...] + norm_back(d_in, normed, inv_std, gain[...])


VECTOR_ROWS = dict(
    ln1_gain=(0, 16),
    ln1_bias=(16, 16),
    b_query=(32, 16),
    b_out=(48, 16),
    ln2_gain=(64, 16),
    ln2_bias=(80, 16),
    b_fc2=(96, 16),
    b_fc=(112, 64),
    b_value=(176, 1),
)
VECTOR_TOTAL = 184


def vectors_kernel(rank_ref, ln1_sums, totals, ln2_sums, fc_sums, gain, shift, out):
    out[...] = jnp.zeros_like(out)

    def put(name, offset, values):
        row = VECTOR_ROWS[name][0] + offset
        for i in range(values.shape[1] // 128):
            out[row + i : row + i + 1, :] = values[:, i * 128 : (i + 1) * 128]

    def put_mine(name, values):
        size = values.shape[1] // PAIRS
        for pair in range(PAIRS):
            for member in range(TEAM):
                block = values[:, pair * size : (pair + 1) * size]
                block = jnp.where(rank_ref[0] == member, block, 0.0)
                put(name, (pair * TEAM + member) * size // 128, block)

    put("ln1_gain", 0, (ln1_sums[0:1, :] - shift[...] * ln1_sums[1:2, :]) / gain[...])
    put("ln1_bias", 0, ln1_sums[1:2, :])
    wide = totals.shape[1] // PAIRS
    q_cols = wide * 2 // 3
    put_mine("b_query", jnp.concatenate([totals[:, :q_cols], totals[:, wide : wide + q_cols]], axis=1))
    put("b_value", 0, totals[:, wide + q_cols :])
    for i, name in enumerate(("b_out", "ln2_gain", "ln2_bias", "b_fc2")):
        put(name, 0, ln2_sums[i : i + 1, :])
    put_mine("b_fc", fc_sums[...])


def plane_sum_kernel(blocks, d_query, kv_rows, d_out):
    total = jnp.sum(blocks[...].astype(F32), axis=0)
    cut = d_query.shape[1]
    edge = cut + kv_rows.shape[0]
    d_query[...] = total[:, :cut]
    kv_rows[...] = total[:, cut:edge].T.astype(LOW)
    d_out[...] = total[:, edge:].T


def shaped(shape, kind=LOW):
    return jax.ShapeDtypeStruct(shape, kind)


ALONE = ("attend_back", "small_grads")


def run(kernel, name, outs, args, flops=0, vmem=None, scalars=0, **more):
    vmem = vmem or (58 if name in ALONE else 20)
    size = sum(a.size * a.dtype.itemsize for a in args)
    size += sum(o.size * o.dtype.itemsize for o in outs)
    if scalars and "grid" not in more and "grid_spec" not in more:
        more["in_specs"] = [pl.BlockSpec(memory_space=pltpu.SMEM)] * scalars + [
            pl.BlockSpec(memory_space=pltpu.VMEM)
        ] * (len(args) - scalars)
    result = pl.pallas_call(
        kernel,
        out_shape=tuple(outs),
        compiler_params=pltpu.CompilerParams(vmem_limit_bytes=vmem * 2**20),
        cost_estimate=pl.CostEstimate(flops=flops, bytes_accessed=size, transcendentals=0),
        name=name,
        **more,
    )(*args)
    return result


def part_shapes(own, width):
    return [shaped((own, width))] + [shaped((own // 2, width))] * 6


def whole_block(array):
    return pl.BlockSpec(array.shape, lambda *_: (0,) * array.ndim)


def add_low(left, right):
    return (left.astype(F32) + right.astype(F32)).astype(LOW)


def after(values, *earlier):
    return lax.optimization_barrier((values, earlier))[0]


def shift(values, axis, step):
    return lax.ppermute(values, axis, [(i, (i + step) % TEAM) for i in range(TEAM)])


def other_core(values):
    return lax.ppermute(values, "c", [(0, 1), (1, 0)])


def ring_pieces(halves, axis, *meanwhile):
    top, low = halves
    ahead_top = shift(top, axis, -1)
    behind_low = shift(low, axis, 1)
    ahead_low = shift(low, axis, -1)
    behind_top = shift(top, axis, 1)
    sent_top, sent_low = ahead_top, behind_low
    if meanwhile:
        sent_top, sent_low = after((ahead_top, behind_low), *meanwhile)
    far_top = shift(sent_top, axis, -1)
    far_low = shift(sent_low, axis, 1)
    return top, low, ahead_top, ahead_low, far_top, far_low, behind_top, behind_low


def ring_sum(parts, axis):
    own, ahead_top, ahead_low, far_top, far_low, behind_top, behind_low = parts
    up = shift(far_top, axis, 1)
    down = shift(far_low, axis, -1)
    up_near = shift(ahead_low, axis, 1)
    down_near = shift(behind_top, axis, -1)
    last_up = shift(add_low(ahead_top, up), axis, 1)
    last_down = shift(add_low(behind_low, down), axis, -1)
    return own, last_up, last_down, up_near, down_near


def plane_scatter(blocks):
    return lax.all_to_all(blocks.reshape(16, *blocks.shape[3:]), PLANE, 0, 0, tiled=True)


def sum_over(values, axis):
    size = lax.axis_size(axis)
    found = [values] + [
        lax.ppermute(values, axis, [(i, i ^ bits) for i in range(size)]) for bits in range(1, size)
    ]
    if size == 2:
        return found[0] + found[1]
    return (found[0] + found[1]) + (found[2] + found[3])


def grad_rows(name, core, left, right, *extra):
    rows = left.shape[1] // 16
    wide = right.shape[1] // PAIRS
    cols = wide + sum(more.shape[-1] for more in extra[1:])

    def place(cols):
        return pl.BlockSpec(
            (1, 2, PAIRS, rows, cols), lambda i, core: (i // 2, i % 2, 0, 0, 0)
        )

    (result,) = run(
        grad_rows_kernel,
        name,
        [shaped((2, 4, PAIRS, rows, cols))],
        [core, left, left, right, *extra],
        flops=left.size * right.shape[1],
        grid_spec=pltpu.PrefetchScalarGridSpec(
            num_scalar_prefetch=1,
            grid=(4,),
            in_specs=[
                pl.BlockSpec((left.shape[0], rows), lambda i, core: (0, 4 * i + core[0])),
                pl.BlockSpec((left.shape[0], rows), lambda i, core: (0, 4 * i + 2 + core[0])),
                pl.BlockSpec(right.shape, lambda i, core: (0, 0)),
            ]
            + [place(more.shape[-1]) for more in extra],
            out_specs=[place(cols)],
        ),
    )
    return result


def body(
    tokens,
    segment_ids,
    ln1_gain,
    ln1_bias,
    w_query,
    b_query,
    w_kv,
    b_value,
    w_out,
    b_out,
    ln2_gain,
    ln2_bias,
    w_fc,
    b_fc,
    w_fc2,
    b_fc2,
    cotangent,
):
    micro, _, rows, width = tokens.shape
    head_dim = b_value.shape[0]
    q_cols = w_query.shape[1]
    heads = q_cols // head_dim
    hidden = w_fc.shape[1]
    wide = q_cols + head_dim
    own = micro * rows
    team_rows = TEAM * own
    rank = lax.axis_index("y")
    core_id = lax.axis_index("c")
    core = core_id.reshape(1)

    def row_of(vector):
        return vector.reshape(1, -1)

    def my_columns(vector):
        blocks = vector.reshape(PAIRS, TEAM, -1)
        return lax.dynamic_index_in_dim(blocks, rank, 1, keepdims=False)

    x_own = tokens.reshape(own, width)
    (norm_own,) = run(
        norm_kernel, "norm", [shaped((own, width))], [x_own, row_of(ln1_gain), row_of(ln1_bias)]
    )
    kv_spread = jnp.broadcast_to(w_kv.T[None], (TEAM,) + w_kv.T.shape)
    kv_block = lax.all_to_all(kv_spread, "y", 0, 0, tiled=True)
    gathered = lax.all_gather(norm_own, "y")

    small = shaped((w_query.shape[0], wide + q_cols))
    (spread,) = run(
        spread_kernel,
        "spread",
        [shaped((16,) + small.shape)],
        [w_query, kv_block, w_out],
        grid=(4,),
        in_specs=[whole_block(w_query), whole_block(kv_block), whole_block(w_out)],
        out_specs=[pl.BlockSpec((4,) + small.shape, lambda i: (i, 0, 0))],
    )
    small_mine = lax.all_to_all(spread, PLANE, 0, 0, tiled=True).reshape(8, PAIRS, *small.shape)
    cot_own = cotangent.reshape(own, width)
    half_rows = own // 2
    cot_halves = after((cot_own[:half_rows], cot_own[half_rows:]), gathered)
    cot_pieces = ring_pieces(cot_halves, "y")
    small_mine = after(small_mine, cot_pieces)
    block = pl.BlockSpec((1, PAIRS) + small.shape, lambda i, core: (i, 0, 0, 0))
    w_qkv0, w_qkv1, w_out0, w_out1 = run(
        weights_kernel,
        "weights",
        [shaped((width, wide))] * PAIRS + [shaped((width, q_cols))] * PAIRS,
        [core, small_mine, other_core(small_mine)],
        grid_spec=pltpu.PrefetchScalarGridSpec(
            num_scalar_prefetch=1,
            grid=(8,),
            in_specs=[block, block],
            out_specs=[
                pl.BlockSpec((2 * small.shape[0], cols), lambda i, core: (i, 0))
                for cols in (wide, wide, q_cols, q_cols)
            ],
        ),
    )
    packed = jnp.concatenate([w_fc, w_fc2.T], axis=1)
    w_wide = lax.all_gather(after(packed, small_mine, gathered), SHARERS, axis=0, tiled=True)

    bias_q = my_columns(b_query)
    bias0 = jnp.concatenate([bias_q[0], jnp.zeros((head_dim,), F32)])
    bias1 = jnp.concatenate([bias_q[1], b_value])
    normed_in, qkv_out = run(
        qkv_kernel,
        "qkv",
        [shaped((team_rows, width)), shaped((16, rows, 2 * q_cols))],
        [rank.reshape(1), gathered, w_qkv0, w_qkv1, row_of(bias0), row_of(bias1)],
        flops=4 * team_rows * width * wide,
        scalars=1,
    )
    qkv = lax.all_to_all(qkv_out, BLK, 0, 0, tiled=True)
    qkv = qkv.reshape(16 * rows, 2 * q_cols)

    seq_rank = lax.axis_index("zl") * TEAM + (rank + lax.axis_index("x")) % TEAM
    segments = lax.dynamic_slice(
        segment_ids,
        (lax.axis_index("zh"), seq_rank, 0),
        (1, 1, segment_ids.shape[2]),
    ).reshape(-1, 1)
    length = qkv.shape[0]
    (attended,) = run(
        functools.partial(attend_kernel, heads, head_dim),
        "attend",
        [shaped((length, q_cols))],
        [segments, qkv],
        flops=3 * length * length * q_cols,
    )
    attended = lax.all_to_all(attended.reshape(16, rows, q_cols), BLK, 0, 0, tiled=True)

    attention, *parts = run(
        project_kernel,
        "project",
        [shaped((team_rows, 2 * q_cols))] + part_shapes(own, width),
        [attended, w_out0, w_out1],
        flops=4 * team_rows * width * q_cols,
    )
    residual, *hidden_own = run(
        residual_kernel,
        "residual",
        [shaped((own, width), F32)] + [shaped((half_rows, width))] * 2,
        [*ring_sum(parts, "y"), x_own, row_of(b_out), row_of(ln2_gain), row_of(ln2_bias)],
    )
    hidden_pieces = ring_pieces(hidden_own, "y")

    step = 512
    steps = PAIRS * hidden // step
    bias_fc = my_columns(b_fc).reshape(1, -1)
    piece_specs = [pl.BlockSpec(memory_space=pl.ANY)] * 16
    col_block = pl.BlockSpec((team_rows, step), lambda i: (0, i))
    row_block = pl.BlockSpec((1, step), lambda i: (0, i))
    per = hidden // step
    hidden_in, cot, act, d_pre, fc_sums = run(
        hidden_kernel,
        "hidden",
        [shaped((team_rows, width))] * 2
        + [shaped((team_rows, PAIRS * hidden))] * 2
        + [shaped((1, PAIRS * hidden), F32)],
        [*hidden_pieces, *cot_pieces, w_wide, w_wide, bias_fc],
        flops=8 * team_rows * width * hidden,
        grid=(steps,),
        in_specs=piece_specs
        + [
            pl.BlockSpec((width, step), lambda i: (i // per, i % per)),
            pl.BlockSpec((width, step), lambda i: (i // per, per + i % per)),
            row_block,
        ],
        out_specs=[pl.BlockSpec((team_rows, width), lambda i: (0, 0))] * 2
        + [col_block, col_block, row_block],
        scratch_shapes=[pltpu.SemaphoreType.DMA((8,))] * 2,
        vmem=40,
    )
    column = step = 512
    col_block = pl.BlockSpec((team_rows, step), lambda i: (0, i))
    w_pair = w_wide.reshape(PAIRS, width, 2 * hidden)


    def wide_product(name, values, half):
        outs = part_shapes(own, width)
        return run(
            wide_kernel,
            name,
            outs,
            [values, w_pair],
            flops=4 * team_rows * width * hidden,
            vmem=45,
            grid=(width // column,),
            in_specs=[
                whole_block(values),
                pl.BlockSpec((PAIRS, column, hidden), lambda i: (0, i, half)),
            ],
            out_specs=[pl.BlockSpec((o.shape[0], column), lambda i: (0, i)) for o in outs],
        )

    (g_wide,) = run(
        wide_grad_kernel,
        "wide_grad",
        [shaped((8, 4, width // 16, 2 * hidden))],
        [hidden_in, cot, d_pre, act],
        flops=8 * team_rows * width * hidden,
        vmem=40,
        grid=(width // step,),
        in_specs=[col_block, col_block, whole_block(d_pre), whole_block(act)],
        out_specs=[
            pl.BlockSpec((4, PAIRS, width // 16, 2 * hidden), lambda i: (i % 2, i // 2, 0, 0))
        ],
    )
    g_sum = lax.psum_scatter(
        g_wide.reshape(-1, 2 * hidden), ("x", "c"), scatter_dimension=0, tiled=True
    )
    g_sum = lax.psum_scatter(g_sum, Z, scatter_dimension=0, tiled=True)
    d_up, d_down = run(
        wide_out_kernel,
        "wide_out",
        [shaped(w_fc.shape, F32), shaped(w_fc2.shape, F32)],
        [g_sum],
    )
    d_hidden_parts = wide_product("d_hidden", after(d_pre, g_wide), 0)

    d_res, *d_res_own, ln2_sums = run(
        residual_back_kernel,
        "residual_back",
        [shaped((own, width), F32)]
        + [shaped((half_rows, width))] * 2
        + [shaped((4, width), F32)],
        [*ring_sum(d_hidden_parts, "y"), cot_own, residual, row_of(ln2_gain)],
    )
    mlp_parts = wide_product("mlp", after(act, d_res_own[0]), 1)
    d_res_low, d_att = run(
        d_att_kernel,
        "d_att",
        [shaped((team_rows, width)), shaped((16, rows, q_cols))],
        [*ring_pieces(d_res_own, "y", mlp_parts[0]), w_out0, w_out1],
        flops=4 * team_rows * width * q_cols,
        in_specs=[pl.BlockSpec(memory_space=pl.ANY)] * 8
        + [pl.BlockSpec(memory_space=pltpu.VMEM)] * 2,
        scratch_shapes=[pltpu.SemaphoreType.DMA((8,))],
    )
    d_att_seq = lax.all_to_all(d_att, BLK, 0, 0, tiled=True).reshape(length, q_cols)
    g_out_sent = grad_rows("g_out_sent", 1 - core, d_res_low, attention)
    mlp_parts = after(mlp_parts, d_att)

    (d_qkv_seq,) = run(
        functools.partial(attend_back_kernel, heads, head_dim),
        "attend_back",
        [shaped((length, 2 * q_cols))],
        [segments, qkv, after(d_att_seq, g_out_sent)],
        flops=6 * length * length * q_cols,
        scratch_shapes=[pltpu.VMEM((length, 2 * head_dim), F32)],
    )
    g_out = grad_rows(
        "g_out_kept", core, after(d_res_low, d_qkv_seq), attention, other_core(g_out_sent)
    )
    mlp_sums = ring_sum(mlp_parts, "y")
    (output,) = run(
        output_kernel, "output", [shaped((own, width))], [*mlp_sums, residual, row_of(b_fc2)]
    )
    d_qkv_seq = lax.all_to_all(d_qkv_seq.reshape(16, rows, 2 * q_cols), BLK, 0, 0, tiled=True)
    d_qkv_seq = after(d_qkv_seq, g_out, mlp_sums)
    d_qkv, ln1_sums, totals, *d_in_parts = run(
        d_in_kernel,
        "d_in",
        [shaped((team_rows, PAIRS * wide)), shaped((2, width), F32), shaped((1, PAIRS * wide), F32)]
        + part_shapes(own, width),
        [d_qkv_seq, w_qkv0, w_qkv1, normed_in],
        flops=4 * team_rows * width * wide,
        in_specs=[
            pl.BlockSpec(memory_space=pltpu.VMEM),
            pl.BlockSpec(memory_space=pl.ANY),
            pl.BlockSpec(memory_space=pl.ANY),
            pl.BlockSpec(memory_space=pltpu.VMEM),
        ],
        scratch_shapes=[pltpu.VMEM((width, wide), LOW)] * 2 + [pltpu.SemaphoreType.DMA((2,))],
    )
    (flat,) = run(
        vectors_kernel,
        "vectors",
        [shaped((VECTOR_TOTAL, 128), F32)],
        [
            rank.reshape(1),
            ln1_sums,
            totals,
            ln2_sums,
            fc_sums,
            row_of(ln1_gain),
            row_of(ln1_bias),
        ],
        scalars=1,
    )
    g_qkv_sent = grad_rows("g_qkv_sent", 1 - core, normed_in, d_qkv)
    small = grad_rows("small_grads", core, normed_in, d_qkv, other_core(g_qkv_sent), g_out)
    small_here = plane_scatter(small)
    d_in_sums = ring_sum(after(d_in_parts, small), "y")
    flat = sum_over(sum_over(after(flat, d_in_sums[3]), "y"), "c")
    (input_grad,) = run(
        input_kernel,
        "input",
        [shaped((own, width), F32)],
        [*d_in_sums, x_own, d_res, row_of(ln1_gain)],
    )

    rows_here = width // 16
    d_wq, kv_rows, d_wout = run(
        plane_sum_kernel,
        "plane_sum",
        [
            shaped((rows_here, q_cols), F32),
            shaped((head_dim, rows_here)),
            shaped((q_cols, rows_here), F32),
        ],
        [after(small_here, input_grad, output)],
    )
    kv_rows = lax.all_to_all(kv_rows.reshape(TEAM, -1, rows_here), "y", 0, 0, tiled=True)
    d_wkv = jnp.sum(after(kv_rows, d_up, d_down).astype(F32), axis=0).T
    flat = sum_over(after(sum_over(flat, Z), d_wq), "x")
    vector = {
        name: flat[start : start + size].reshape(-1) for name, (start, size) in VECTOR_ROWS.items()
    }
    return (
        output.reshape(tokens.shape),
        input_grad.reshape(tokens.shape),
        vector["ln1_gain"],
        vector["ln1_bias"],
        d_wq,
        vector["b_query"],
        d_wkv,
        vector["b_value"],
        d_wout,
        vector["b_out"],
        vector["ln2_gain"],
        vector["ln2_bias"],
        d_up,
        vector["b_fc"],
        d_down,
        vector["b_fc2"],
    )


def solution(mesh):
    fine = Mesh(mesh.devices.reshape(2, 4, 2, 2, 4), ALL)
    activations = P(None, HEAD, BLK, None)
    rows_first, cols_first = P(BLK, HEAD), P(HEAD, BLK)
    return jax.shard_map(
        body,
        mesh=fine,
        in_specs=(
            activations,
            P(),
            P(),
            P(),
            rows_first,
            P(),
            rows_first,
            P(),
            cols_first,
            P(),
            P(),
            P(),
            rows_first,
            P(),
            cols_first,
            P(),
            activations,
        ),
        out_specs=(
            activations,
            activations,
            P(),
            P(),
            rows_first,
            P(),
            rows_first,
            P(),
            cols_first,
            P(),
            P(),
            P(),
            rows_first,
            P(),
            cols_first,
            P(),
        ),
        check_vma=False,
    )
```
